256 devices in a mesh: gz: 128 (over y, x, z), xy: 2 (over core).
Axes of the slice: x: 4, y: 4, z: 8, core: 2. Of those that a mesh axis runs over, the one named last changes fastest.
Arguments:
- right_side: float32 [256, 512, 640], P('gz', 'xy'), may hold values from -6 to 6
- labels: int32 [256, 512, 640], P('gz', 'xy'), may hold values from 0 to 2
- fraction: float32 [256, 512, 640], P('gz', 'xy'), may hold values from 0.5 to 2
Outputs:
- fine_iterate: float32 [256, 512, 640], P('gz', 'xy')
- plane_iterate: float32 [128, 512, 640], P('gz', 'xy')
- coarse_return: float32 [128, 512, 640], P('gz', 'xy')
The draws below stay inside these ranges and needn't reach their ends.
Inputs may be any that keep to these rules, and one draw needn't show every extreme that they name: `labels`: 0 marks pore, 1 grain, 2 clay.
All inputs are finite; a program needn't handle non-finite values.
Results may differ from the reference program's by a relative error of at most 0.00002.
Values sent between devices are 32-bit elements; how exact they have to be, the bound alone decides.
No kernel may reach another device: no remote copies, remote signals or barrier semaphores. Data moves between devices by JAX's collectives and lax.ppermute only.
A program may use at most 64 MiB of HBM per device.

```python
import math
import jax
import jax.numpy as jnp
from jax import lax

NX = 512
NY = 640
SWEEPS = 2
LEVELS = 5
NZ = 256


def place_ends(result, rng, low, largest):
    longest = result.shape.index(max(result.shape))
    spots = []
    for shift in (0, 1):
        where = [jax.random.randint(jax.random.fold_in(rng, axis), (), 0, length) for axis, length in enumerate(result.shape)]
        where[longest] = (where[longest] + shift) % result.shape[longest]
        spots.append(tuple(where))
    return result.at[spots[0]].set(low).at[spots[1]].set(largest)


def block_scale(key, shape, pieces, low, largest):
    gain = 1.0
    for axis_at, shards_of in pieces:
        draws = jax.random.uniform(jax.random.fold_in(jax.random.fold_in(key, 6), axis_at), (shards_of,), jnp.float32, low / len(pieces), largest / len(pieces))
        gain = gain * jnp.repeat(jnp.exp(draws), shape[axis_at] // shards_of).reshape((-1,) + (1,) * (len(shape) - 1 - axis_at))
    return gain


def noise(own_key, dims, scale, limit, pieces=(), kind=jnp.bfloat16):
    array = scale * jax.random.normal(own_key, dims, jnp.float32)
    if pieces:
        array = array * block_scale(own_key, dims, pieces, -0.22, 0.18)
    return jnp.clip(array, -limit, limit).astype(kind)


def setup_inputs(seed: int = 0) -> dict:
    seeds = jax.random.split(jax.random.key(seed), 4)
    return {
        "right_side": noise(seeds[0], (NZ, NX, NY), 1.0, 6.0, ((0, 128), (1, 2)), jnp.float32),
        "labels": place_ends(jax.random.randint(seeds[1], (NZ, NX, NY), 0, 3), jax.random.fold_in(seeds[1], 1), 0, 2).astype(jnp.int32),
        "fraction": jnp.clip(jnp.exp(math.log(2.0) - 1.3862944 * jax.random.uniform(seeds[2], (NZ, NX, NY), jnp.float32) ** block_scale(seeds[2], (NZ, NX, NY), ((0, 128), (1, 2)), -0.2, 0.2)), 0.5, 2.0),
    }


damping = 0.8
pore_value = 1.0
grain_value = 0.1
clay_value = 0.3


def harmonic(one_side, other_side):
    return (2.0 * one_side * other_side) / (one_side + other_side)


def later_along(values, along):
    extent = values.shape[along]
    trimmed = lax.slice_in_dim(values, 1, extent, axis=along)
    filler = jnp.zeros_like(lax.slice_in_dim(values, 0, 1, axis=along))
    return jnp.concatenate([trimmed, filler], axis=along)


def earlier_along(values, along):
    extent = values.shape[along]
    trimmed = lax.slice_in_dim(values, 0, extent - 1, axis=along)
    filler = jnp.zeros_like(lax.slice_in_dim(values, 0, 1, axis=along))
    return jnp.concatenate([filler, trimmed], axis=along)


def conductivity(labels, fraction):
    base_value = jnp.where(labels == 0, pore_value, jnp.where(labels == 1, grain_value, clay_value))
    return base_value.astype(fraction.dtype) * fraction


def diagonal_of(face_set):
    face_north = face_set[2]
    face_south = earlier_along(face_north, face_north.ndim - 1)
    return ((((face_set[0] + face_set[1]) + face_north) + face_south) + face_set[3]) + face_set[4]


def combine_terms(values, face_set, diagonal, east_rows, west_rows, down_plane, up_plane):
    last_axis = values.ndim - 1
    face_north = face_set[2]
    face_south = earlier_along(face_north, last_axis)
    north_cells = later_along(values, last_axis)
    south_cells = earlier_along(values, last_axis)
    return (diagonal * values - face_set[0] * east_rows - face_set[1] * west_rows
            - face_north * north_cells - face_south * south_cells
            - face_set[3] * down_plane - face_set[4] * up_plane)


def apply_operator(values, face_set, diagonal):
    return combine_terms(values, face_set, diagonal, later_along(values, 1), earlier_along(values, 1),
                         earlier_along(values, 0), later_along(values, 0))


def smooth(source, face_set, diagonal):
    iterate = jnp.zeros_like(source)
    for sweep_no in range(SWEEPS):
        iterate = iterate + (damping * (source - apply_operator(iterate, face_set, diagonal))) / diagonal
    return iterate


def coarsen(residual, face_set):
    source = residual[0::2] + residual[1::2]
    coarse_set = (face_set[0][0::2] + face_set[0][1::2],
                  face_set[1][0::2] + face_set[1][1::2],
                  face_set[2][0::2] + face_set[2][1::2],
                  face_set[3][0::2],
                  face_set[4][1::2])
    return source, coarse_set


def fine_faces(conduct):
    planes = lax.broadcasted_iota(jnp.int32, conduct.shape, 0)
    face_east = harmonic(conduct, later_along(conduct, 1))
    face_west = harmonic(conduct, earlier_along(conduct, 1))
    face_north = harmonic(conduct, later_along(conduct, 2))
    face_down = jnp.where(planes == 0, 2.0 * conduct, harmonic(conduct, earlier_along(conduct, 0)))
    face_up = jnp.where(planes == conduct.shape[0] - 1, 2.0 * conduct, harmonic(conduct, later_along(conduct, 0)))
    return (face_east, face_west, face_north, face_down, face_up)


def reference(right_side, labels, fraction):
    conduct = conductivity(labels, fraction)
    face_set = fine_faces(conduct)
    source = right_side
    iterates = []
    for level_no in range(LEVELS + 1):
        diagonal = diagonal_of(face_set)
        iterate = smooth(source, face_set, diagonal)
        iterates.append(iterate)
        if level_no < LEVELS:
            residual = source - apply_operator(iterate, face_set, diagonal)
            source, face_set = coarsen(residual, face_set)
    running = jnp.zeros_like(iterates[1])
    for level_no in range(2, LEVELS + 1):
        running = running + jnp.repeat(iterates[level_no], 2 ** (level_no - 1), axis=0)
    return iterates[0], iterates[1], running
```

```python
from functools import partial

import jax
import jax.numpy as jnp
from jax import lax
from jax.experimental import pallas as pl
from jax.experimental.pallas import tpu as pltpu
from jax.sharding import PartitionSpec as P

RING = 8
HALO = 8
THIN = 4
damping = 0.8
pore_value = 1.0
grain_value = 0.1
clay_value = 0.3
TINY = 1e-30


def ring_groups(count):
    return [[r * RING + k for k in range(RING)] for r in range(count // RING)]


def shifted(value, by):
    size = lax.axis_size("gz")
    pairs = [(i, i + by) for i in range(size) if 0 <= i + by < size]
    return lax.ppermute(value, "gz", pairs)


def row_shifted(value, by):
    pairs = []
    for ring in range(lax.axis_size("gz") // RING):
        for t in range(2 * RING):
            u = t + by
            if 0 <= u < 2 * RING:
                pairs.append(((ring * RING + t % RING) * 2 + t // RING, (ring * RING + u % RING) * 2 + u // RING))
    return lax.ppermute(value, ("gz", "xy"), pairs)


def partner(value):
    size = lax.axis_size("gz")
    return lax.ppermute(value, "gz", [(i, i + RING if (i // RING) % 2 == 0 else i - RING) for i in range(size)])


def transposed(value):
    return lax.all_to_all(value, "gz", 0, 0, axis_index_groups=ring_groups(lax.axis_size("gz")), tiled=True)


def conductivity(labels, fraction):
    return jnp.where(labels == 0, pore_value, jnp.where(labels == 1, grain_value, clay_value)) * fraction


def harmonic(one_side, other_side):
    return (2.0 * one_side * other_side) / jnp.maximum(one_side + other_side, TINY)


def next_row(v):
    return pltpu.roll(v, v.shape[0] - 1, 0)


def previous_row(v):
    return pltpu.roll(v, 1, 0)


def next_column(v):
    return pltpu.roll(v, v.shape[1] - 1, 1)


def previous_column(v):
    return pltpu.roll(v, 1, 1)


def neighbours(v, below, above, east, north, down, up):
    return (
        east * next_row(v)
        + previous_row(east * v)
        + north * next_column(v)
        + previous_column(north * v)
        + down * below
        + up * above
    )


def weight(c, east, north, down, up):
    diagonal = east + previous_row(east) + north + previous_column(north) + down + up
    return jnp.where(c > 0, damping / jnp.where(c > 0, diagonal, 1.0), 0.0)


def loop(count, body):
    def step(k, carry):
        body(k)
        return carry

    lax.fori_loop(0, count, step, 0)


def call(kernel, outs, scratch, *args):
    shapes = [jax.ShapeDtypeStruct(s, jnp.float32) for s in outs]
    vmem = pl.BlockSpec(memory_space=pltpu.VMEM)
    return pl.pallas_call(
        kernel,
        out_shape=shapes,
        in_specs=[vmem] * len(args),
        out_specs=[vmem] * len(shapes),
        scratch_shapes=[pltpu.VMEM(s, jnp.float32) for s in scratch],
        compiler_params=pltpu.CompilerParams(vmem_limit_bytes=48 * 1024 * 1024),
    )(*args)


def cut_conduct(labels, fraction, top, bottom, out, full):
    planes, rows, _ = labels.shape
    strip = rows // RING
    for p in range(planes):
        full[p, :HALO] = top[p]
        full[p, HALO + rows:] = bottom[p]

        def fill(k):
            at = pl.multiple_of(k * strip, strip)
            full[p, pl.ds(at + HALO, strip)] = conductivity(labels[p, pl.ds(at, strip)], fraction[p, pl.ds(at, strip)])

        loop(RING, fill)
        for k in range(RING):
            out[k, p] = full[p, k * strip:k * strip + strip + 2 * HALO]


def cut_source(source, top, bottom, out):
    planes, rows, _ = source.shape
    strip = rows // RING
    for p in range(planes):
        for k in range(RING):
            start = k * strip
            if k == 0:
                out[k, p, :THIN] = top[p, HALO - THIN:]
            else:
                out[k, p, :THIN] = source[p, start - THIN:start]
            out[k, p, THIN:THIN + strip] = source[p, start:start + strip]
            if k == RING - 1:
                out[k, p, THIN + strip:] = bottom[p, :THIN]
            else:
                out[k, p, THIN + strip:] = source[p, start + strip:start + strip + THIN]


def make_faces(c_own, c_low, c_high, east0, north0, z0, w0, east1, north1, w1, east2, north2, z2, w2,
               east3, north3, z3, w3, east4, north4, z4, w4, c):
    rows, columns = c_own.shape[1:]
    c[0:3] = c_low[...]
    c[3:19] = c_own[...]
    c[19:22] = c_high[...]
    last = lax.broadcasted_iota(jnp.int32, (rows, columns), 1) == columns - 1

    def z_face(i):
        z0[i] = harmonic(c[i], c[i + 1])

    loop(21, z_face)
    z0[2] = jnp.where(c[2] > 0, z0[2], 2.0 * c[3])
    z0[18] = jnp.where(c[19] > 0, z0[18], 2.0 * c[18])

    def plane(i):
        here = c[i + 1]
        east = harmonic(here, next_row(here))
        north = jnp.where(last, 0.0, harmonic(here, next_column(here)))
        east0[i] = east
        north0[i] = north
        w0[i] = weight(here, east, north, z0[i], z0[i + 1])

    loop(20, plane)

    def plane1(j):
        east = east0[2 * j] + east0[2 * j + 1]
        north = north0[2 * j] + north0[2 * j + 1]
        east1[j] = east
        north1[j] = north
        w1[j] = weight(c[2 * j + 1], east, north, z0[2 * j], z0[2 * j + 2])

    loop(10, plane1)
    for q in range(4):
        east2[q] = east1[2 * q + 1] + east1[2 * q + 2]
        north2[q] = north1[2 * q + 1] + north1[2 * q + 2]
        z2[q] = z0[4 * q + 2]
    z2[4] = z0[18]
    for q in range(4):
        w2[q] = weight(c[3], east2[q], north2[q], z2[q], z2[q + 1])
    for q in range(2):
        east3[q] = east2[2 * q] + east2[2 * q + 1]
        north3[q] = north2[2 * q] + north2[2 * q + 1]
        z3[q] = z2[2 * q]
    z3[2] = z2[4]
    for q in range(2):
        w3[q] = weight(c[3], east3[q], north3[q], z3[q], z3[q + 1])
    east4[0] = east3[0] + east3[1]
    north4[0] = north3[0] + north3[1]
    z4[0] = z3[0]
    z4[1] = z3[2]
    w4[0] = weight(c[3], east4[0], north4[0], z4[0], z4[1])


def make_last_faces(east4, north4, w4, other, down, up, east5, north5, w5):
    east5[0] = east4[0] + other[0]
    north5[0] = north4[0] + other[1]
    w5[0] = weight(w4[0], east5[0], north5[0], down[0], up[0])


def fine_level(s_own, s_low, s_high, east0, north0, z0, w0, w1, fine, source1, edge_down, edge_up, s, first, total, second):
    rows = east0.shape[1]
    strip = fine.shape[2]
    inner = slice(HALO - THIN, HALO + strip + THIN)
    blank = jnp.zeros((HALO - THIN, s.shape[2]), jnp.float32)

    def place(k, value):
        s[k, :HALO - THIN] = blank
        s[k, inner] = value
        s[k, HALO + strip + THIN:] = blank

    for k in range(2):
        place(k, s_low[k])
        place(18 + k, s_high[k])
    loop(16, lambda k: place(k + 2, s_own[k]))

    def start(i):
        first[i] = w0[i] * s[i]

    loop(20, start)

    def sweep(k):
        i = k + 1
        t = 1.2 * s[i] + neighbours(first[i], first[i - 1], first[i + 1], east0[i], north0[i], z0[i], z0[i + 1])
        total[i] = t
        second[i] = w0[i] * t

    loop(18, sweep)

    def rest(i):
        return s[i] - damping * total[i] + neighbours(
            second[i], second[i - 1], second[i + 1], east0[i], north0[i], z0[i], z0[i + 1])

    def pair(q):
        source1[q] = rest(2 * q + 2) + rest(2 * q + 3)
        fine[q, 0] = second[2 * q + 2, HALO:HALO + strip]
        fine[q, 1] = second[2 * q + 3, HALO:HALO + strip]

    loop(8, pair)
    edge_down[0] = source1[0, inner]
    edge_down[1] = w1[2, inner] * source1[1, inner]
    edge_up[0] = w1[7, inner] * source1[6, inner]
    edge_up[1] = source1[7, inner]


def first_coarse_level(source1, low, high, east1, north1, z0, w1, plane_out, source2, top, bottom, s, first, total, second):
    strip = plane_out.shape[1]
    inner = slice(HALO - THIN, HALO + strip + THIN)
    blank = jnp.zeros((HALO - THIN, s.shape[2]), jnp.float32)
    for ref, k, value in ((s, 0, low[1]), (s, 9, high[0]), (first, 0, low[0]), (first, 11, high[1])):
        ref[k, :HALO - THIN] = blank
        ref[k, inner] = value
        ref[k, HALO + strip + THIN:] = blank
    s[1:9] = source1[...]

    def start(j):
        first[j + 1] = w1[j] * s[j]

    loop(10, start)

    def sweep(j):
        t = 1.2 * s[j] + neighbours(first[j + 1], first[j], first[j + 2], east1[j], north1[j], z0[2 * j], z0[2 * j + 2])
        total[j] = t
        second[j] = w1[j] * t

    loop(10, sweep)

    def rest(j):
        return s[j] - damping * total[j] + neighbours(
            second[j], second[j - 1], second[j + 1], east1[j], north1[j], z0[2 * j], z0[2 * j + 2])

    def pair(q):
        value = rest(2 * q + 1) + rest(2 * q + 2)
        source2[q] = value[HALO:HALO + strip]
        top[q] = value[HALO:2 * HALO]
        bottom[q] = value[strip:HALO + strip]
        plane_out[2 * q] = second[2 * q + 1, HALO:HALO + strip]
        plane_out[2 * q + 1] = second[2 * q + 2, HALO:HALO + strip]

    loop(4, pair)


def widen(source2, above, below, w2, s, first, edge_low, edge_high):
    count, strip, _ = source2.shape
    for q in range(count):
        s[q, :HALO] = above[q]
        s[q, HALO:HALO + strip] = source2[q]
        s[q, HALO + strip:] = below[q]
        first[q] = w2[q] * s[q]
    edge_low[0] = first[0]
    edge_high[0] = first[count - 1]


def around(ref, low, high, q):
    count = ref.shape[0]
    return (ref[q], low[0] if q == 0 else ref[q - 1], high[0] if q == count - 1 else ref[q + 1])


def sweep_level(s, first, low, high, east, north, z, w, total, second, *edges):
    count = s.shape[0]
    for q in range(count):
        t = 1.2 * s[q] + neighbours(*around(first, low, high, q), east[q], north[q], z[q], z[q + 1])
        total[q] = t
        second[q] = w[q] * t
    if edges:
        edges[0][0] = second[0]
        edges[1][0] = second[count - 1]


def rest_level(s, total, second, low, high, east, north, z, w_next, s_next, first_next, *edges):
    count = s.shape[0]

    def rest(q):
        return s[q] - damping * total[q] + neighbours(*around(second, low, high, q), east[q], north[q], z[q], z[q + 1])

    for q in range(count // 2):
        value = rest(2 * q) + rest(2 * q + 1)
        s_next[q] = value
        first_next[q] = w_next[q] * value
    if edges:
        edges[0][0] = first_next[0]
        edges[1][0] = first_next[count // 2 - 1]


def rest_last(s, total, second, low, high, east, north, z, out):
    out[0] = s[0] - damping * total[0] + neighbours(second[0], low[0], high[0], east[0], north[0], z[0], z[1])


def finish(s, first, low, high, east, north, down, up, w, second2, second3, second4, out):
    strip = out.shape[1]
    second5 = w[0] * (1.2 * s[0] + neighbours(first[0], low[0], high[0], east[0], north[0], down[0], up[0]))
    own = slice(HALO, HALO + strip)
    for k in range(RING):
        out[k] = ((second2[k // 2, own] + second3[k // 4, own]) + second4[0, own]) + second5[own]


def exchange(edge_low, edge_high, distance=RING):
    return shifted(edge_high, distance), shifted(edge_low, -distance)


def on_device(right_side, labels, fraction):
    planes, rows, columns = right_side.shape
    strip = rows // RING
    frame = strip + 2 * HALO
    at_core = lax.axis_index("xy")
    even_ring = (lax.axis_index("gz") // RING) % 2 == 0

    def edges_of(first_rows, last_rows):
        got = lax.ppermute(jnp.where(at_core == 0, last_rows, first_rows), "xy", [(0, 1), (1, 0)])
        return jnp.where(at_core == 1, got, 0.0), jnp.where(at_core == 0, got, 0.0)

    c_top, c_bottom = edges_of(conductivity(labels[:, :HALO], fraction[:, :HALO]),
                               conductivity(labels[:, rows - HALO:], fraction[:, rows - HALO:]))
    s_top, s_bottom = edges_of(right_side[:, :HALO], right_side[:, rows - HALO:])
    (c_cut,) = call(cut_conduct, [(RING, planes, frame, columns)], [(planes, rows + 2 * HALO, columns)],
                    labels, fraction, c_top, c_bottom)
    c = transposed(c_cut).reshape(RING * planes, frame, columns)
    (s_cut,) = call(cut_source, [(RING, planes, strip + 2 * THIN, columns)], [], right_side, s_top, s_bottom)
    s = transposed(s_cut).reshape(RING * planes, strip + 2 * THIN, columns)

    c_low, c_high = exchange(c[:3], c[-3:])

    def shape(n):
        return (n, frame, columns)

    (east0, north0, z0, w0, east1, north1, w1, east2, north2, z2, w2, east3, north3, z3, w3,
     east4, north4, z4, w4) = call(
        make_faces,
        [shape(n) for n in (20, 20, 21, 20, 10, 10, 10, 4, 4, 5, 4, 2, 2, 3, 2, 1, 1, 2, 1)],
        [shape(22)], c, c_low, c_high)
    outer = jnp.where(even_ring, z4[:1], z4[1:])
    other = partner(jnp.concatenate([east4, north4, outer], axis=0))
    down5 = jnp.where(even_ring, z4[:1], other[2:])
    up5 = jnp.where(even_ring, other[2:], z4[1:])
    east5, north5, w5 = call(make_last_faces, [shape(1)] * 3, [], east4, north4, w4, other, down5, up5)

    s_low, s_high = exchange(s[:2], s[-2:])
    thin = (2, strip + 2 * THIN, columns)
    fine, source1, edge_down, edge_up = call(
        fine_level, [(RING, planes, strip, columns), shape(8), thin, thin],
        [shape(20)] * 4, s, s_low, s_high, east0, north0, z0, w0, w1)

    low, high = exchange(edge_down, edge_up)
    plane_out, source2, top, bottom = call(
        first_coarse_level,
        [(8, strip, columns), (4, strip, columns), (4, HALO, columns), (4, HALO, columns)],
        [shape(10), shape(12), shape(10), shape(10)], source1, low, high, east1, north1, z0, w1)

    above = row_shifted(bottom, 1)
    below = row_shifted(top, -1)
    s2, first2, a, b = call(widen, [shape(4), shape(4), shape(1), shape(1)], [], source2, above, below, w2)
    low, high = exchange(a, b)
    total2, second2, a, b = call(sweep_level, [shape(4), shape(4), shape(1), shape(1)], [],
                                 s2, first2, low, high, east2, north2, z2, w2)
    low, high = exchange(a, b)
    s3, first3, a, b = call(rest_level, [shape(2), shape(2), shape(1), shape(1)], [],
                            s2, total2, second2, low, high, east2, north2, z2, w3)
    low, high = exchange(a, b)
    total3, second3, a, b = call(sweep_level, [shape(2), shape(2), shape(1), shape(1)], [],
                                 s3, first3, low, high, east3, north3, z3, w3)
    low, high = exchange(a, b)
    s4, first4 = call(rest_level, [shape(1), shape(1)], [], s3, total3, second3, low, high, east3, north3, z3, w4)
    low, high = exchange(first4, first4)
    total4, second4 = call(sweep_level, [shape(1), shape(1)], [], s4, first4, low, high, east4, north4, z4, w4)
    low, high = exchange(second4, second4)
    (rest4,) = call(rest_last, [shape(1)], [], s4, total4, second4, low, high, east4, north4, z4)
    s5 = rest4 + partner(rest4)
    first5 = w5 * s5
    low, high = exchange(first5, first5, 2 * RING)
    (summed,) = call(finish, [(RING, strip, columns)], [],
                     s5, first5, low, high, east5, north5, down5, up5, w5, second2, second3, second4)

    fine_iterate = jnp.transpose(transposed(fine), (1, 0, 2, 3)).reshape(planes, rows, columns)
    plane_iterate = transposed(plane_out).reshape(1, rows, columns)
    coarse_return = transposed(summed).reshape(1, rows, columns)
    return fine_iterate, plane_iterate, coarse_return


def solution(mesh):
    spec = P("gz", "xy", None)
    return jax.shard_map(
        on_device,
        mesh=mesh,
        in_specs=(spec, spec, spec),
        out_specs=(spec, spec, spec),
        check_vma=False,
    )
```

```python
from functools import partial

import jax
import jax.numpy as jnp
from jax import lax
from jax.experimental import pallas as pl
from jax.experimental.pallas import tpu as pltpu
from jax.sharding import PartitionSpec as P

RING = 8
HALO = 8
THIN = 4
damping = 0.8
pore_value = 1.0
grain_value = 0.1
clay_value = 0.3
TINY = 1e-30


def ring_groups(count):
    return [[r * RING + k for k in range(RING)] for r in range(count // RING)]


def shifted(value, by):
    size = lax.axis_size("gz")
    pairs = [(i, i + by) for i in range(size) if 0 <= i + by < size]
    return lax.ppermute(value, "gz", pairs)


def row_shifted(value, by):
    pairs = []
    for ring in range(lax.axis_size("gz") // RING):
        for t in range(2 * RING):
            u = t + by
            if 0 <= u < 2 * RING:
                pairs.append(((ring * RING + t % RING) * 2 + t // RING, (ring * RING + u % RING) * 2 + u // RING))
    return lax.ppermute(value, ("gz", "xy"), pairs)


def partner(value):
    size = lax.axis_size("gz")
    return lax.ppermute(value, "gz", [(i, i + RING if (i // RING) % 2 == 0 else i - RING) for i in range(size)])


def transposed(value):
    return lax.all_to_all(value, "gz", 0, 0, axis_index_groups=ring_groups(lax.axis_size("gz")), tiled=True)


def conductivity(labels, fraction):
    return jnp.where(labels == 0, pore_value, jnp.where(labels == 1, grain_value, clay_value)) * fraction


def harmonic(one_side, other_side):
    return (2.0 * one_side * other_side) / jnp.maximum(one_side + other_side, TINY)


def next_row(v):
    return pltpu.roll(v, v.shape[0] - 1, 0)


def previous_row(v):
    return pltpu.roll(v, 1, 0)


def next_column(v):
    return pltpu.roll(v, v.shape[1] - 1, 1)


def previous_column(v):
    return pltpu.roll(v, 1, 1)


def neighbours(v, below, above, east, north, down, up):
    return (
        east * next_row(v)
        + previous_row(east * v)
        + north * next_column(v)
        + previous_column(north * v)
        + down * below
        + up * above
    )


def weight(c, east, north, down, up):
    diagonal = east + previous_row(east) + north + previous_column(north) + down + up
    return jnp.where(c > 0, damping / jnp.where(c > 0, diagonal, 1.0), 0.0)


def loop(count, body):
    def step(k, carry):
        body(k)
        return carry

    lax.fori_loop(0, count, step, 0)


def call(kernel, outs, scratch, *args, limit=8, work=0.0):
    shapes = [jax.ShapeDtypeStruct(s, jnp.float32) for s in outs]
    vmem = pl.BlockSpec(memory_space=pltpu.VMEM)
    cost = pl.CostEstimate(flops=int(work * 1.0e9), bytes_accessed=int(work * 3.0e6), transcendentals=0) if work else None
    return pl.pallas_call(
        kernel,
        out_shape=shapes,
        in_specs=[vmem] * len(args),
        out_specs=[vmem] * len(shapes),
        scratch_shapes=[pltpu.VMEM(s, jnp.float32) for s in scratch],
        compiler_params=pltpu.CompilerParams(vmem_limit_bytes=limit * 1024 * 1024),
        cost_estimate=cost,
    )(*args)


def cut_conduct(labels, fraction, out):
    planes, rows, _ = labels.shape
    strip = rows // RING
    for p in range(planes):
        for k in range(RING):
            at = slice(k * strip, (k + 1) * strip)
            out[k, p] = conductivity(labels[p, at], fraction[p, at])


def cut_source(source, top, bottom, out):
    planes, rows, _ = source.shape
    strip = rows // RING
    for p in range(planes):
        for k in range(RING):
            start = k * strip
            if k == 0:
                out[k, p, :THIN] = top[p, HALO - THIN:]
            else:
                out[k, p, :THIN] = source[p, start - THIN:start]
            out[k, p, THIN:THIN + strip] = source[p, start:start + strip]
            if k == RING - 1:
                out[k, p, THIN + strip:] = bottom[p, :THIN]
            else:
                out[k, p, THIN + strip:] = source[p, start + strip:start + strip + THIN]


def plane_faces(c):
    last = lax.broadcasted_iota(jnp.int32, c.shape, 1) == c.shape[1] - 1
    return harmonic(c, next_row(c)), jnp.where(last, 0.0, harmonic(c, next_column(c)))


def make_faces(c_own, above, below, c, east0, north0, east1, north1, east2, north2, east3, north3, east4, north4,
               bundle_down, bundle_up):
    strip = c_own.shape[1]

    def plane(p):
        c[p, :HALO] = above[p]
        c[p, HALO:HALO + strip] = c_own[p]
        c[p, HALO + strip:] = below[p]
        east0[p], north0[p] = plane_faces(c[p])

    loop(16, plane)

    def plane1(q):
        east1[q] = east0[2 * q] + east0[2 * q + 1]
        north1[q] = north0[2 * q] + north0[2 * q + 1]

    loop(8, plane1)
    for finer, coarser in ((east1, east2), (north1, north2), (east2, east3), (north2, north3), (east3, east4), (north3, north4)):
        for q in range(coarser.shape[0]):
            coarser[q] = finer[2 * q] + finer[2 * q + 1]
    middle = harmonic(c[7], c[8])
    for bundle, first, edge2, face2, edge3 in ((bundle_down, 0, 0, 4, 0), (bundle_up, 13, 3, 12, 1)):
        for k in range(3):
            bundle[k] = c[first + k]
        bundle[3] = east2[edge2]
        bundle[4] = north2[edge2]
        bundle[5] = harmonic(c[face2 - 1], c[face2])
        bundle[6] = east3[edge3]
        bundle[7] = north3[edge3]
        bundle[8] = middle


def make_weights(c, low, high, east0, north0, east1, north1, east2, north2, east3, north3, east4, north4,
                 z0, z1, z2, z3, z4, w0, w1, w2, w3, w4, halo0, halo1, halo2, halo3):
    def z_face(p):
        z0[p] = harmonic(c[p - 1], c[p])

    loop(15, lambda k: z_face(k + 1))
    z0[0] = jnp.where(low[2] > 0, harmonic(low[2], c[0]), 2.0 * c[0])
    z0[16] = jnp.where(high[0] > 0, harmonic(c[15], high[0]), 2.0 * c[15])

    def weigh(p):
        w0[p] = weight(c[p], east0[p], north0[p], z0[p], z0[p + 1])

    loop(16, weigh)
    loop(9, lambda q: z1.__setitem__(q, z0[2 * q]))

    def weigh1(q):
        w1[q] = weight(c[0], east1[q], north1[q], z1[q], z1[q + 1])

    loop(8, weigh1)
    for z_fine, z, east, north, w in ((z1, z2, east2, north2, w2), (z2, z3, east3, north3, w3), (z3, z4, east4, north4, w4)):
        for q in range(z.shape[0]):
            z[q] = z_fine[2 * q]
        for q in range(w.shape[0]):
            w[q] = weight(c[0], east[q], north[q], z[q], z[q + 1])

    for side, bundle, near, far, last, face in ((0, low, 2, 1, 0, 0), (1, high, 0, 1, 2, 16)):
        shared = z0[face]
        middle = harmonic(bundle[near], bundle[far])
        outer = harmonic(bundle[far], bundle[last])
        east_near, north_near = plane_faces(bundle[near])
        east_far, north_far = plane_faces(bundle[far])
        halo0[side] = east_near
        halo0[2 + side] = north_near
        halo0[4 + side] = middle
        halo0[6 + side] = weight(bundle[near], east_near, north_near, shared, middle)
        halo0[8 + side] = weight(bundle[far], east_far, north_far, middle, outer)
        halo1[side] = east_near + east_far
        halo1[2 + side] = north_near + north_far
        halo1[4 + side] = outer
        halo1[6 + side] = weight(bundle[near], east_near + east_far, north_near + north_far, shared, outer)
        for halo, at in ((halo2, 3), (halo3, 6)):
            halo[side] = bundle[at]
            halo[2 + side] = bundle[at + 1]
            halo[4 + side] = bundle[at + 2]
            halo[6 + side] = weight(bundle[near], bundle[at], bundle[at + 1], shared, bundle[at + 2])


def make_last_faces(east4, north4, w4, other, down, up, east5, north5, w5):
    east5[0] = east4[0] + other[0]
    north5[0] = north4[0] + other[1]
    w5[0] = weight(w4[0], east5[0], north5[0], down[0], up[0])


def sweep_and_rest(s, first, total, second, east, north, z, w, halo):
    count = w.shape[0]

    def sweep(q):
        t = 1.2 * s[q + 1] + neighbours(first[q + 2], first[q + 1], first[q + 3], east[q], north[q], z[q], z[q + 1])
        total[q] = t
        second[q + 1] = w[q] * t

    loop(count, sweep)
    for side, q, down, up in ((0, -1, halo[4], z[0]), (1, count, z[count], halo[5])):
        second[q + 1] = halo[6 + side] * (1.2 * s[q + 1] + neighbours(
            first[q + 2], first[q + 1], first[q + 3], halo[side], halo[2 + side], down, up))

    def rest(q):
        return s[q + 1] - damping * total[q] + neighbours(
            second[q + 1], second[q], second[q + 2], east[q], north[q], z[q], z[q + 1])

    return rest


def fine_level(s_own, s_low, s_high, east, north, z, w, halo, w_next, fine, s_next, edge_down, edge_up, s, first, total, second):
    strip = fine.shape[2]
    columns = s.shape[2]
    blank = jnp.zeros((HALO - THIN, columns), jnp.float32)

    def place(k, value):
        s[k, :HALO - THIN] = blank
        s[k, HALO - THIN:HALO + strip + THIN] = value
        s[k, HALO + strip + THIN:] = blank

    place(0, s_low[0])
    first[0] = halo[8] * s[0]
    place(0, s_high[1])
    first[19] = halo[9] * s[0]
    place(0, s_low[1])
    first[1] = halo[6] * s[0]
    place(17, s_high[0])
    first[18] = halo[7] * s[17]

    def start(q):
        place(q + 1, s_own[q])
        first[q + 2] = w[q] * s[q + 1]

    loop(16, start)
    rest = sweep_and_rest(s, first, total, second, east, north, z, w, halo)

    def pair(q):
        s_next[q] = rest(2 * q) + rest(2 * q + 1)
        fine[q, 0] = second[2 * q + 1, HALO:HALO + strip]
        fine[q, 1] = second[2 * q + 2, HALO:HALO + strip]

    loop(8, pair)
    edge_down[0] = s_next[0]
    edge_down[1] = w_next[1] * s_next[1]
    edge_up[0] = w_next[6] * s_next[6]
    edge_up[1] = s_next[7]


def open_level(s_own, w, low, high, halo, s, first):
    count = w.shape[0]
    s[0] = low[1]
    s[count + 1] = high[0]
    first[0] = low[0]
    first[1] = halo[6] * low[1]
    first[count + 2] = halo[7] * high[0]
    first[count + 3] = high[1]

    def start(q):
        s[q + 1] = s_own[q]
        first[q + 2] = w[q] * s_own[q]

    loop(count, start)


def first_coarse_level(s_own, low, high, east, north, z, w, halo, out, s_next, top, bottom, s, first, total, second):
    strip = out.shape[1]
    open_level(s_own, w, low, high, halo, s, first)
    rest = sweep_and_rest(s, first, total, second, east, north, z, w, halo)

    def pair(q):
        value = rest(2 * q) + rest(2 * q + 1)
        s_next[q] = value[HALO:HALO + strip]
        top[q] = value[HALO:2 * HALO]
        bottom[q] = value[strip:HALO + strip]
        out[2 * q] = second[2 * q + 1, HALO:HALO + strip]
        out[2 * q + 1] = second[2 * q + 2, HALO:HALO + strip]

    loop(4, pair)


def middle_level(s_own, low, high, east, north, z, w, halo, w_next, out, s_next, *rest_refs):
    edges, (s, first, total, second) = rest_refs[:-4], rest_refs[-4:]
    count = w.shape[0]
    strip = out.shape[1]
    open_level(s_own, w, low, high, halo, s, first)
    rest = sweep_and_rest(s, first, total, second, east, north, z, w, halo)
    for q in range(count // 2):
        s_next[q] = rest(2 * q) + rest(2 * q + 1)
    for q in range(count):
        out[q] = second[q + 1, HALO:HALO + strip]
    if len(edges) == 2:
        edge_down, edge_up = edges
        edge_down[0] = s_next[0]
        edge_down[1] = w_next[1] * s_next[1]
        edge_up[0] = w_next[count // 2 - 2] * s_next[count // 2 - 2]
        edge_up[1] = s_next[count // 2 - 1]
    else:
        edges[0][0] = w_next[0] * s_next[0]


def widen(source2, above, below, w2, fine, plane_out, s, edge_down, edge_up, back):
    count, strip, _ = source2.shape
    for q in range(count):
        s[q, :HALO] = above[q]
        s[q, HALO:HALO + strip] = source2[q]
        s[q, HALO + strip:] = below[q]
    edge_down[0] = s[0]
    edge_down[1] = w2[1] * s[1]
    edge_up[0] = w2[count - 2] * s[count - 2]
    edge_up[1] = s[count - 1]

    def gather(k):
        back[k, 0] = fine[k, 0]
        back[k, 1] = fine[k, 1]
        back[k, 2] = plane_out[k]

    loop(RING, gather)


def sweep_last(s, first, low, high, east, north, z, w, total, second):
    t = 1.2 * s[0] + neighbours(first[0], low[0], high[0], east[0], north[0], z[0], z[1])
    total[0] = t
    second[0] = w[0] * t


def rest_last(s, total, second, low, high, east, north, z, out):
    out[0] = s[0] - damping * total[0] + neighbours(second[0], low[0], high[0], east[0], north[0], z[0], z[1])


def finish(s, first, low, high, east, north, down, up, w, second2, second3, second4, settled, out):
    strip = out.shape[1]
    second5 = w[0] * (1.2 * s[0] + neighbours(first[0], low[0], high[0], east[0], north[0], down[0], up[0]))
    own = slice(HALO, HALO + strip)
    for k in range(RING):
        out[k] = ((second2[k // 2] + second3[k // 4]) + second4[0, own]) + second5[own]


def exchange(edge_low, edge_high, distance=RING):
    return shifted(edge_high, distance), shifted(edge_low, -distance)


def on_device(right_side, labels, fraction):
    planes, rows, columns = right_side.shape
    strip = rows // RING
    frame = strip + 2 * HALO
    at_core = lax.axis_index("xy")
    even_ring = (lax.axis_index("gz") // RING) % 2 == 0

    def edges_of(first_rows, last_rows):
        got = lax.ppermute(jnp.where(at_core == 0, last_rows, first_rows), "xy", [(0, 1), (1, 0)])
        return jnp.where(at_core == 1, got, 0.0), jnp.where(at_core == 0, got, 0.0)

    def shape(n):
        return (n, frame, columns)

    (c_cut,) = call(cut_conduct, [(RING, planes, strip, columns)], [], labels, fraction, limit=10)
    c_own = transposed(c_cut).reshape(RING * planes, strip, columns)
    s_top, s_bottom = edges_of(right_side[:, :HALO], right_side[:, rows - HALO:])
    (s_cut,) = call(cut_source, [(RING, planes, strip + 2 * THIN, columns)], [], right_side, s_top, s_bottom, limit=10)
    s_own = transposed(s_cut).reshape(RING * planes, strip + 2 * THIN, columns)

    above = row_shifted(c_own[:, strip - HALO:], 1)
    below = row_shifted(c_own[:, :HALO], -1)
    c, *plane_set, bundle_down, bundle_up = call(
        make_faces, [shape(n) for n in (16, 16, 16, 8, 8, 4, 4, 2, 2, 1, 1, 9, 9)], [], c_own, above, below, limit=18, work=8.0)
    c_low, c_high = exchange(bundle_down, bundle_up)
    z0, z1, z2, z3, z4, w0, w1, w2, w3, w4, halo0, halo1, halo2, halo3 = call(
        make_weights, [shape(n) for n in (17, 9, 5, 3, 2, 16, 8, 4, 2, 1, 10, 8, 8, 8)], [],
        c, c_low, c_high, *plane_set, limit=26, work=8.0)
    east0, north0, east1, north1, east2, north2, east3, north3, east4, north4 = plane_set
    outer = jnp.where(even_ring, z4[:1], z4[1:])
    other = partner(jnp.concatenate([east4, north4, outer], axis=0))
    down5 = jnp.where(even_ring, z4[:1], other[2:])
    up5 = jnp.where(even_ring, other[2:], z4[1:])
    east5, north5, w5 = call(make_last_faces, [shape(1)] * 3, [], east4, north4, w4, other, down5, up5)

    s_low, s_high = exchange(s_own[:2], s_own[-2:])
    fine, s1, edge_down, edge_up = call(
        fine_level, [(RING, planes, strip, columns), shape(8), shape(2), shape(2)],
        [shape(18), shape(20), shape(16), shape(18)],
        s_own, s_low, s_high, east0, north0, z0, w0, halo0, w1, limit=26, work=8.0)

    low, high = exchange(edge_down, edge_up)
    plane_out, s2, top, bottom = call(
        first_coarse_level,
        [(8, strip, columns), (4, strip, columns), (4, HALO, columns), (4, HALO, columns)],
        [shape(10), shape(12), shape(8), shape(10)], s1, low, high, east1, north1, z1, w1, halo1, limit=15, work=4.0)

    above = row_shifted(bottom, 1)
    below = row_shifted(top, -1)
    s2, edge_down, edge_up, back = call(
        widen, [shape(4), shape(2), shape(2), (RING, planes + 1, strip, columns)], [], s2, above, below, w2, fine, plane_out, limit=10)
    low, high = exchange(edge_down, edge_up)
    second2, s3, edge_down, edge_up = call(
        middle_level, [(4, strip, columns), shape(2), shape(2), shape(2)], [shape(6), shape(8), shape(4), shape(6)],
        s2, low, high, east2, north2, z2, w2, halo2, w3, limit=10)
    low, high = exchange(edge_down, edge_up)
    second3, s4, first4 = call(
        middle_level, [(2, strip, columns), shape(1), shape(1)], [shape(4), shape(6), shape(2), shape(4)],
        s3, low, high, east3, north3, z3, w3, halo3, w4)
    low, high = exchange(first4, first4)
    total4, second4 = call(sweep_last, [shape(1), shape(1)], [], s4, first4, low, high, east4, north4, z4, w4)
    low, high = exchange(second4, second4)
    (rest4,) = call(rest_last, [shape(1)], [], s4, total4, second4, low, high, east4, north4, z4)
    s5 = rest4 + partner(rest4)
    first5 = w5 * s5
    low, high = exchange(first5, first5, 2 * RING)
    back = transposed(back)
    (summed,) = call(finish, [(RING, strip, columns)], [],
                     s5, first5, low, high, east5, north5, down5, up5, w5, second2, second3, second4, back[0, 0, :HALO])

    fine_iterate = jnp.transpose(back[:, :planes], (1, 0, 2, 3)).reshape(planes, rows, columns)
    plane_iterate = back[:, planes].reshape(1, rows, columns)
    coarse_return = transposed(summed).reshape(1, rows, columns)
    return fine_iterate, plane_iterate, coarse_return


def solution(mesh):
    spec = P("gz", "xy", None)
    return jax.shard_map(
        on_device,
        mesh=mesh,
        in_specs=(spec, spec, spec),
        out_specs=(spec, spec, spec),
        check_vma=False,
    )
```

```python
from functools import partial

import jax
import jax.numpy as jnp
from jax import lax
from jax.experimental import pallas as pl
from jax.experimental.pallas import tpu as pltpu
from jax.sharding import PartitionSpec as P

RING = 8
HALO = 8
REACH = 9
THIN = 4
damping = 0.8
pore_value = 1.0
grain_value = 0.1
clay_value = 0.3
TINY = 1e-30


def ring_groups(count):
    return [[r * RING + k for k in range(RING)] for r in range(count // RING)]


def shifted(value, by):
    size = lax.axis_size("gz")
    pairs = [(i, i + by) for i in range(size) if 0 <= i + by < size]
    return lax.ppermute(value, "gz", pairs)


def row_shifted(value, by):
    pairs = []
    for ring in range(lax.axis_size("gz") // RING):
        for t in range(2 * RING):
            u = t + by
            if 0 <= u < 2 * RING:
                pairs.append(((ring * RING + t % RING) * 2 + t // RING, (ring * RING + u % RING) * 2 + u // RING))
    return lax.ppermute(value, ("gz", "xy"), pairs)


def partner(value):
    size = lax.axis_size("gz")
    return lax.ppermute(value, "gz", [(i, i + RING if (i // RING) % 2 == 0 else i - RING) for i in range(size)])


def transposed(value):
    return lax.all_to_all(value, "gz", 0, 0, axis_index_groups=ring_groups(lax.axis_size("gz")), tiled=True)


def conductivity(labels, fraction):
    return jnp.where(labels == 0, pore_value, jnp.where(labels == 1, grain_value, clay_value)) * fraction


def harmonic(one_side, other_side):
    return (2.0 * one_side * other_side) / jnp.maximum(one_side + other_side, TINY)


def next_row(v):
    return pltpu.roll(v, v.shape[0] - 1, 0)


def previous_row(v):
    return pltpu.roll(v, 1, 0)


def next_column(v):
    return pltpu.roll(v, v.shape[1] - 1, 1)


def previous_column(v):
    return pltpu.roll(v, 1, 1)


def neighbours(v, below, above, east, north, down, up):
    return (
        east * next_row(v)
        + previous_row(east * v)
        + north * next_column(v)
        + previous_column(north * v)
        + down * below
        + up * above
    )


def weight(c, east, north, down, up):
    diagonal = east + previous_row(east) + north + previous_column(north) + down + up
    return jnp.where(c > 0, damping / jnp.where(c > 0, diagonal, 1.0), 0.0)


def loop(count, body):
    def step(k, carry):
        body(k)
        return carry

    lax.fori_loop(0, count, step, 0)


def call(kernel, outs, scratch, *args, limit=8, work=0.0):
    shapes = [jax.ShapeDtypeStruct(s, jnp.float32) for s in outs]
    vmem = pl.BlockSpec(memory_space=pltpu.VMEM)
    cost = pl.CostEstimate(flops=int(work * 1.0e9), bytes_accessed=int(work * 3.0e6), transcendentals=0) if work else None
    return pl.pallas_call(
        kernel,
        out_shape=shapes,
        in_specs=[vmem] * len(args),
        out_specs=[vmem] * len(shapes),
        scratch_shapes=[pltpu.VMEM(s, jnp.float32) for s in scratch],
        compiler_params=pltpu.CompilerParams(vmem_limit_bytes=limit * 1024 * 1024),
        cost_estimate=cost,
    )(*args)


def after(value, *settled):
    def nothing(*refs):
        pass

    there = pl.BlockSpec(memory_space=pl.ANY)
    return pl.pallas_call(
        nothing,
        out_shape=jax.ShapeDtypeStruct(value.shape, value.dtype),
        in_specs=[there] * (1 + len(settled)),
        out_specs=there,
        input_output_aliases={0: 0},
    )(value, *settled)


def cut_conduct(labels, fraction, out):
    planes, rows, _ = labels.shape
    strip = rows // RING
    for p in range(planes):
        for k in range(RING):
            at = slice(k * strip, (k + 1) * strip)
            out[k, p] = conductivity(labels[p, at], fraction[p, at])


def cut_source(source, top, bottom, out):
    planes, rows, _ = source.shape
    strip = rows // RING
    for p in range(planes):
        for k in range(RING):
            start = k * strip
            if k == 0:
                out[k, p, :THIN] = top[p, HALO - THIN:]
            else:
                out[k, p, :THIN] = source[p, start - THIN:start]
            out[k, p, THIN:THIN + strip] = source[p, start:start + strip]
            if k == RING - 1:
                out[k, p, THIN + strip:] = bottom[p, :THIN]
            else:
                out[k, p, THIN + strip:] = source[p, start + strip:start + strip + THIN]


def plane_faces(c):
    last = lax.broadcasted_iota(jnp.int32, c.shape, 1) == c.shape[1] - 1
    return harmonic(c, next_row(c)), jnp.where(last, 0.0, harmonic(c, next_column(c)))


def parts(faces, count):
    east, north = faces.at[0:count], faces.at[count:2 * count]
    z, w = faces.at[2 * count:3 * count + 1], faces.at[3 * count + 1:4 * count + 1]
    return east, north, z, w, faces.at[4 * count + 1:] if count > 1 else None


def planes_of(count):
    return 4 * count + 1 + (0 if count == 1 else 10 if count == 16 else 8)


def frames(c_own, above, below, c, low, high):
    strip = c_own.shape[1]

    def place(ref, k, p):
        ref[k, :HALO] = above[p]
        ref[k, HALO:HALO + strip] = c_own[p]
        ref[k, HALO + strip:] = below[p]

    loop(16, lambda p: place(c, p, p))
    loop(REACH, lambda p: place(low, p, p))
    loop(REACH, lambda p: place(high, p, p + 16 - REACH))


def make_faces(c, low, high, faces0, faces1, faces2, faces3, faces4):
    east0, north0, z0, w0, halo0 = parts(faces0, 16)

    def z_face(p):
        z0[p] = harmonic(c[p - 1], c[p])

    loop(15, lambda k: z_face(k + 1))
    z0[0] = jnp.where(low[REACH - 1] > 0, harmonic(low[REACH - 1], c[0]), 2.0 * c[0])
    z0[16] = jnp.where(high[0] > 0, harmonic(c[15], high[0]), 2.0 * c[15])

    def weigh(p):
        east, north = plane_faces(c[p])
        east0[p] = east
        north0[p] = north
        w0[p] = weight(c[p], east, north, z0[p], z0[p + 1])

    loop(16, weigh)
    finer, count = faces0, 16
    for coarser in (faces1, faces2, faces3, faces4):
        east_f, north_f, z_f, _, _ = parts(finer, count)
        count //= 2
        east, north, z, w, _ = parts(coarser, count)

        def faces_and_weight(q):
            east_q = east_f[2 * q] + east_f[2 * q + 1]
            north_q = north_f[2 * q] + north_f[2 * q + 1]
            east[q] = east_q
            north[q] = north_q
            z[q] = z_f[2 * q]
            w[q] = weight(c[0], east_q, north_q, z_f[2 * q], z_f[2 * q + 2])

        loop(count, faces_and_weight)
        z[count] = z_f[2 * count]
        finer = coarser

    for side, ref, at, face in ((0, low, [REACH - 1 - k for k in range(REACH)], 0), (1, high, list(range(REACH)), 16)):
        shared = z0[face]
        near = ref[at[0]]
        middle = harmonic(near, ref[at[1]])
        east_sum, north_sum = plane_faces(near)
        halo0[side] = east_sum
        halo0[2 + side] = north_sum
        halo0[4 + side] = middle
        halo0[6 + side] = weight(near, east_sum, north_sum, shared, middle)
        thick = 1
        for faces, count in ((faces1, 8), (faces2, 4), (faces3, 2)):
            for k in range(thick, 2 * thick):
                east_k, north_k = plane_faces(ref[at[k]])
                if k == 1:
                    halo0[8 + side] = weight(ref[at[1]], east_k, north_k, middle, harmonic(ref[at[1]], ref[at[2]]))
                east_sum = east_sum + east_k
                north_sum = north_sum + north_k
            thick *= 2
            halo = parts(faces, count)[4]
            outer = harmonic(ref[at[thick - 1]], ref[at[thick]])
            halo[side] = east_sum
            halo[2 + side] = north_sum
            halo[4 + side] = outer
            halo[6 + side] = weight(near, east_sum, north_sum, shared, outer)


def make_last_faces(faces4, other, down, up, east5, north5, w5):
    east4, north4, _, w4, _ = parts(faces4, 1)
    east5[0] = east4[0] + other[0]
    north5[0] = north4[0] + other[1]
    w5[0] = weight(w4[0], east5[0], north5[0], down[0], up[0])


def sweep_and_rest(s, first, total, second, faces, count):
    east, north, z, w, halo = parts(faces, count)

    def sweep(q):
        t = 1.2 * s[q + 1] + neighbours(first[q + 2], first[q + 1], first[q + 3], east[q], north[q], z[q], z[q + 1])
        total[q] = t
        second[q + 1] = w[q] * t

    loop(count, sweep)
    for side, q, down, up in ((0, -1, halo[4], z[0]), (1, count, z[count], halo[5])):
        second[q + 1] = halo[6 + side] * (1.2 * s[q + 1] + neighbours(
            first[q + 2], first[q + 1], first[q + 3], halo[side], halo[2 + side], down, up))

    def rest(q):
        return s[q + 1] - damping * total[q] + neighbours(
            second[q + 1], second[q], second[q + 2], east[q], north[q], z[q], z[q + 1])

    return rest


def fine_level(s_own, s_low, s_high, faces, faces_next, fine, s_next, edge_down, edge_up, s, first, total, second):
    strip = fine.shape[2]
    columns = s.shape[2]
    _, _, _, w, halo = parts(faces, 16)
    w_next = parts(faces_next, 8)[3]
    blank = jnp.zeros((HALO - THIN, columns), jnp.float32)

    def place(k, value):
        s[k, :HALO - THIN] = blank
        s[k, HALO - THIN:HALO + strip + THIN] = value
        s[k, HALO + strip + THIN:] = blank

    place(0, s_low[0])
    first[0] = halo[8] * s[0]
    place(0, s_high[1])
    first[19] = halo[9] * s[0]
    place(0, s_low[1])
    first[1] = halo[6] * s[0]
    place(17, s_high[0])
    first[18] = halo[7] * s[17]

    def start(q):
        place(q + 1, s_own[q])
        first[q + 2] = w[q] * s[q + 1]

    loop(16, start)
    rest = sweep_and_rest(s, first, total, second, faces, 16)

    def pair(q):
        s_next[q] = rest(2 * q) + rest(2 * q + 1)
        fine[q, 0] = second[2 * q + 1, HALO:HALO + strip]
        fine[q, 1] = second[2 * q + 2, HALO:HALO + strip]

    loop(8, pair)
    edge_down[0] = s_next[0]
    edge_down[1] = w_next[1] * s_next[1]
    edge_up[0] = w_next[6] * s_next[6]
    edge_up[1] = s_next[7]


def open_level(s_own, faces, low, high, s, first):
    count = s_own.shape[0]
    _, _, _, w, halo = parts(faces, count)
    s[0] = low[1]
    s[count + 1] = high[0]
    first[0] = low[0]
    first[1] = halo[6] * low[1]
    first[count + 2] = halo[7] * high[0]
    first[count + 3] = high[1]

    def start(q):
        s[q + 1] = s_own[q]
        first[q + 2] = w[q] * s_own[q]

    loop(count, start)


def first_coarse_level(s_own, low, high, faces, out, s_next, top, bottom, s, first, total, second):
    strip = out.shape[1]
    open_level(s_own, faces, low, high, s, first)
    rest = sweep_and_rest(s, first, total, second, faces, s_own.shape[0])

    def pair(q):
        value = rest(2 * q) + rest(2 * q + 1)
        s_next[q] = value[HALO:HALO + strip]
        top[q] = value[HALO:2 * HALO]
        bottom[q] = value[strip:HALO + strip]
        out[2 * q] = second[2 * q + 1, HALO:HALO + strip]
        out[2 * q + 1] = second[2 * q + 2, HALO:HALO + strip]

    loop(4, pair)


def middle_level(s_own, low, high, faces, faces_next, out, s_next, *rest_refs):
    edges, (s, first, total, second) = rest_refs[:-4], rest_refs[-4:]
    count = s_own.shape[0]
    w_next = parts(faces_next, count // 2)[3]
    strip = out.shape[1]
    open_level(s_own, faces, low, high, s, first)
    rest = sweep_and_rest(s, first, total, second, faces, s_own.shape[0])
    for q in range(count // 2):
        s_next[q] = rest(2 * q) + rest(2 * q + 1)
    for q in range(count):
        out[q] = second[q + 1, HALO:HALO + strip]
    if len(edges) == 2:
        edge_down, edge_up = edges
        edge_down[0] = s_next[0]
        edge_down[1] = w_next[1] * s_next[1]
        edge_up[0] = w_next[count // 2 - 2] * s_next[count // 2 - 2]
        edge_up[1] = s_next[count // 2 - 1]
    else:
        edges[0][0] = w_next[0] * s_next[0]


def widen(source2, above, below, faces2, fine, plane_out, s, edge_down, edge_up, back):
    count, strip, _ = source2.shape
    w2 = parts(faces2, count)[3]
    for q in range(count):
        s[q, :HALO] = above[q]
        s[q, HALO:HALO + strip] = source2[q]
        s[q, HALO + strip:] = below[q]
    edge_down[0] = s[0]
    edge_down[1] = w2[1] * s[1]
    edge_up[0] = w2[count - 2] * s[count - 2]
    edge_up[1] = s[count - 1]

    def gather(k):
        back[k, 0] = fine[k, 0]
        back[k, 1] = fine[k, 1]
        back[k, 2] = plane_out[k]

    loop(RING, gather)


def sweep_last(s, first, low, high, faces, total, second):
    east, north, z, w, _ = parts(faces, 1)
    t = 1.2 * s[0] + neighbours(first[0], low[0], high[0], east[0], north[0], z[0], z[1])
    total[0] = t
    second[0] = w[0] * t


def rest_last(s, total, second, low, high, faces, out):
    east, north, z, _, _ = parts(faces, 1)
    out[0] = s[0] - damping * total[0] + neighbours(second[0], low[0], high[0], east[0], north[0], z[0], z[1])


def finish(s, first, low, high, east, north, down, up, w, second2, second3, second4, settled, out):
    strip = out.shape[1]
    second5 = w[0] * (1.2 * s[0] + neighbours(first[0], low[0], high[0], east[0], north[0], down[0], up[0]))
    own = slice(HALO, HALO + strip)
    for k in range(RING):
        out[k] = ((second2[k // 2] + second3[k // 4]) + second4[0, own]) + second5[own]


def exchange(edge_low, edge_high, distance=RING):
    return shifted(edge_high, distance), shifted(edge_low, -distance)


def on_device(right_side, labels, fraction):
    planes, rows, columns = right_side.shape
    strip = rows // RING
    frame = strip + 2 * HALO
    at_core = lax.axis_index("xy")
    even_ring = (lax.axis_index("gz") // RING) % 2 == 0

    def edges_of(first_rows, last_rows):
        got = lax.ppermute(jnp.where(at_core == 0, last_rows, first_rows), "xy", [(0, 1), (1, 0)])
        return jnp.where(at_core == 1, got, 0.0), jnp.where(at_core == 0, got, 0.0)

    def shape(n):
        return (n, frame, columns)

    (c_cut,) = call(cut_conduct, [(RING, planes, strip, columns)], [], labels, fraction, limit=10)
    c_own = transposed(c_cut).reshape(RING * planes, strip, columns)
    above = row_shifted(c_own[:, strip - HALO:], 1)
    below = row_shifted(c_own[:, :HALO], -1)
    s_top, s_bottom = edges_of(right_side[:, :HALO], right_side[:, rows - HALO:])
    (s_cut,) = call(cut_source, [(RING, planes, strip + 2 * THIN, columns)], [],
                    right_side, s_top, s_bottom, limit=10, work=4.0)
    s_own = transposed(after(s_cut, above[0], below[0])).reshape(RING * planes, strip + 2 * THIN, columns)

    c, bundle_down, bundle_up = call(frames, [shape(16), shape(REACH), shape(REACH)], [], c_own, above, below, limit=10, work=2.0)
    c_low, c_high = exchange(bundle_down, bundle_up)
    faces0, faces1, faces2, faces3, faces4 = call(
        make_faces, [shape(planes_of(n)) for n in (16, 8, 4, 2, 1)], [], c, c_low, c_high, limit=28, work=12.0)
    east4, north4, z_low, z_high = faces4[0:1], faces4[1:2], faces4[2:3], faces4[3:4]
    other = partner(jnp.concatenate([east4, north4, jnp.where(even_ring, z_low, z_high)], axis=0))
    down5 = jnp.where(even_ring, z_low, other[2:])
    up5 = jnp.where(even_ring, other[2:], z_high)
    east5, north5, w5 = call(make_last_faces, [shape(1)] * 3, [], faces4, other, down5, up5)

    s_low, s_high = exchange(s_own[:2], s_own[-2:])
    fine, s1, edge_down, edge_up = call(
        fine_level, [(RING, planes, strip, columns), shape(8), shape(2), shape(2)],
        [shape(18), shape(20), shape(16), shape(18)],
        s_own, s_low, s_high, faces0, faces1, limit=30, work=8.0)

    low, high = exchange(edge_down, edge_up)
    plane_out, s2, top, bottom = call(
        first_coarse_level,
        [(8, strip, columns), (4, strip, columns), (4, HALO, columns), (4, HALO, columns)],
        [shape(10), shape(12), shape(8), shape(10)], s1, low, high, faces1, limit=15, work=4.0)

    above = row_shifted(bottom, 1)
    below = row_shifted(top, -1)
    s2, edge_down, edge_up, back = call(
        widen, [shape(4), shape(2), shape(2), (RING, planes + 1, strip, columns)], [], s2, above, below, faces2, fine, plane_out, limit=10)
    low, high = exchange(edge_down, edge_up)
    second2, s3, edge_down, edge_up = call(
        middle_level, [(4, strip, columns), shape(2), shape(2), shape(2)], [shape(6), shape(8), shape(4), shape(6)],
        s2, low, high, faces2, faces3, limit=10)
    low, high = exchange(edge_down, edge_up)
    second3, s4, first4 = call(
        middle_level, [(2, strip, columns), shape(1), shape(1)], [shape(4), shape(6), shape(2), shape(4)],
        s3, low, high, faces3, faces4)
    low, high = exchange(first4, first4)
    total4, second4 = call(sweep_last, [shape(1), shape(1)], [], s4, first4, low, high, faces4)
    low, high = exchange(second4, second4)
    (rest4,) = call(rest_last, [shape(1)], [], s4, total4, second4, low, high, faces4)
    s5 = rest4 + partner(rest4)
    first5 = w5 * s5
    low, high = exchange(first5, first5, 2 * RING)
    back = transposed(back)
    (summed,) = call(finish, [(RING, strip, columns)], [],
                     s5, first5, low, high, east5, north5, down5, up5, w5, second2, second3, second4, back[0, 0, :HALO])

    fine_iterate = jnp.transpose(back[:, :planes], (1, 0, 2, 3)).reshape(planes, rows, columns)
    plane_iterate = back[:, planes].reshape(1, rows, columns)
    coarse_return = transposed(summed).reshape(1, rows, columns)
    return fine_iterate, plane_iterate, coarse_return


def solution(mesh):
    spec = P("gz", "xy", None)
    return jax.shard_map(
        on_device,
        mesh=mesh,
        in_specs=(spec, spec, spec),
        out_specs=(spec, spec, spec),
        check_vma=False,
    )
```

```python
from functools import partial

import jax
import jax.numpy as jnp
from jax import lax
from jax.experimental import pallas as pl
from jax.experimental.pallas import tpu as pltpu
from jax.sharding import PartitionSpec as P

RING = 8
HALO = 8
REACH = 9
THIN = 4
damping = 0.8
pore_value = 1.0
grain_value = 0.1
clay_value = 0.3
TINY = 1e-30


def ring_groups(count):
    return [[r * RING + k for k in range(RING)] for r in range(count // RING)]


def shifted(value, by):
    size = lax.axis_size("gz")
    pairs = [(i, i + by) for i in range(size) if 0 <= i + by < size]
    return lax.ppermute(value, "gz", pairs)


def row_shifted(value, by):
    pairs = []
    for ring in range(lax.axis_size("gz") // RING):
        for t in range(2 * RING):
            u = t + by
            if 0 <= u < 2 * RING:
                pairs.append(((ring * RING + t % RING) * 2 + t // RING, (ring * RING + u % RING) * 2 + u // RING))
    return lax.ppermute(value, ("gz", "xy"), pairs)


def partner(value):
    size = lax.axis_size("gz")
    return lax.ppermute(value, "gz", [(i, i + RING if (i // RING) % 2 == 0 else i - RING) for i in range(size)])


def transposed(value):
    return lax.all_to_all(value, "gz", 0, 0, axis_index_groups=ring_groups(lax.axis_size("gz")), tiled=True)


def conductivity(labels, fraction):
    return jnp.where(labels == 0, pore_value, jnp.where(labels == 1, grain_value, clay_value)) * fraction


def harmonic(one_side, other_side):
    return (2.0 * one_side * other_side) / jnp.maximum(one_side + other_side, TINY)


def next_row(v):
    return pltpu.roll(v, v.shape[0] - 1, 0)


def previous_row(v):
    return pltpu.roll(v, 1, 0)


def next_column(v):
    return pltpu.roll(v, v.shape[1] - 1, 1)


def previous_column(v):
    return pltpu.roll(v, 1, 1)


def neighbours(v, below, above, east, north, down, up):
    return (
        east * next_row(v)
        + previous_row(east * v)
        + north * next_column(v)
        + previous_column(north * v)
        + down * below
        + up * above
    )


def weight(c, east, north, down, up):
    diagonal = east + previous_row(east) + north + previous_column(north) + down + up
    return jnp.where(c > 0, damping / jnp.where(c > 0, diagonal, 1.0), 0.0)


def loop(count, body):
    def step(k, carry):
        body(k)
        return carry

    lax.fori_loop(0, count, step, 0)


def call(kernel, outs, scratch, *args, limit=8, work=0.0, settled=()):
    shapes = [jax.ShapeDtypeStruct(s, jnp.float32) for s in outs]
    vmem = pl.BlockSpec(memory_space=pltpu.VMEM)
    smem = pl.BlockSpec(memory_space=pltpu.SMEM)
    cost = pl.CostEstimate(flops=int(work * 1.0e9), bytes_accessed=int(work * 3.0e6), transcendentals=0) if work else None

    def body(*refs):
        kernel(*refs[len(settled):])

    return pl.pallas_call(
        body,
        out_shape=shapes,
        in_specs=[pl.BlockSpec(memory_space=pl.ANY)] * len(settled) + [smem if a.dtype == jnp.int32 and a.ndim == 1 else vmem for a in args],
        out_specs=[vmem] * len(shapes),
        scratch_shapes=[pltpu.VMEM(s, jnp.float32) for s in scratch],
        compiler_params=pltpu.CompilerParams(vmem_limit_bytes=limit * 1024 * 1024),
        cost_estimate=cost,
    )(*settled, *args)


def ring_permuted(value, by):
    size = lax.axis_size("gz")
    return lax.ppermute(value, "gz", [(i, i // RING * RING + (i + by) % RING) for i in range(size)])


def after(value, *settled):
    def nothing(*refs):
        pass

    there = pl.BlockSpec(memory_space=pl.ANY)
    return pl.pallas_call(
        nothing,
        out_shape=jax.ShapeDtypeStruct(value.shape, value.dtype),
        in_specs=[there] * (1 + len(settled)),
        out_specs=there,
        input_output_aliases={0: 0},
    )(value, *settled)


def cut_conduct(place, labels, fraction, top, bottom, *rest):
    outs, full = rest[:-1], rest[-1]
    planes, rows, _ = labels.shape
    strip = rows // RING
    for p in range(planes):
        full[p, :HALO] = top[p]
        full[p, HALO + rows:] = bottom[p]
        for k in range(RING):
            at = k * strip
            full[p, HALO + at:HALO + at + strip] = conductivity(labels[p, at:at + strip], fraction[p, at:at + strip])
        for k in range(RING):
            start = pl.multiple_of(((place[0] + k) % RING) * strip, strip)
            outs[k][p] = full[p, pl.ds(start, strip + 2 * HALO)]


def cut_source(place, source, top, bottom, *rest):
    outs, full = rest[:-1], rest[-1]
    planes, rows, _ = source.shape
    strip = rows // RING
    for p in range(planes):
        full[p, :HALO] = top[p]
        full[p, HALO + rows:] = bottom[p]
        full[p, HALO:HALO + rows] = source[p]
        for k in range(RING):
            start = pl.multiple_of(((place[0] + k) % RING) * strip, strip)
            outs[k][p] = full[p, pl.ds(start, strip + 2 * HALO)][HALO - THIN:HALO + strip + THIN]


def join(place, *refs):
    out, low, high = refs[RING:]
    for k in range(RING):
        start = ((place[0] + RING - k) % RING) * 2
        out[start] = refs[k][0]
        out[start + 1] = refs[k][1]
    reach = low.shape[0]
    loop(reach, lambda p: low.__setitem__(p, out[p]))
    loop(reach, lambda p: high.__setitem__(p, out[p + 16 - reach]))


def plane_faces(c):
    last = lax.broadcasted_iota(jnp.int32, c.shape, 1) == c.shape[1] - 1
    return harmonic(c, next_row(c)), jnp.where(last, 0.0, harmonic(c, next_column(c)))


def parts(faces, count):
    east, north = faces.at[0:count], faces.at[count:2 * count]
    z, w = faces.at[2 * count:3 * count + 1], faces.at[3 * count + 1:4 * count + 1]
    return east, north, z, w, faces.at[4 * count + 1:] if count > 1 else None


def planes_of(count):
    return 4 * count + 1 + (0 if count == 1 else 10 if count == 16 else 8)


def make_faces(c, low, high, faces0, faces1, faces2, faces3, faces4):
    east0, north0, z0, w0, halo0 = parts(faces0, 16)

    def z_face(p):
        z0[p] = harmonic(c[p - 1], c[p])

    loop(15, lambda k: z_face(k + 1))
    z0[0] = jnp.where(low[REACH - 1] > 0, harmonic(low[REACH - 1], c[0]), 2.0 * c[0])
    z0[16] = jnp.where(high[0] > 0, harmonic(c[15], high[0]), 2.0 * c[15])

    def weigh(p):
        east, north = plane_faces(c[p])
        east0[p] = east
        north0[p] = north
        w0[p] = weight(c[p], east, north, z0[p], z0[p + 1])

    loop(16, weigh)
    finer, count = faces0, 16
    for coarser in (faces1, faces2, faces3, faces4):
        east_f, north_f, z_f, _, _ = parts(finer, count)
        count //= 2
        east, north, z, w, _ = parts(coarser, count)

        def faces_and_weight(q):
            east_q = east_f[2 * q] + east_f[2 * q + 1]
            north_q = north_f[2 * q] + north_f[2 * q + 1]
            east[q] = east_q
            north[q] = north_q
            z[q] = z_f[2 * q]
            w[q] = weight(c[0], east_q, north_q, z_f[2 * q], z_f[2 * q + 2])

        loop(count, faces_and_weight)
        z[count] = z_f[2 * count]
        finer = coarser

    for side, ref, at, face in ((0, low, [REACH - 1 - k for k in range(REACH)], 0), (1, high, list(range(REACH)), 16)):
        shared = z0[face]
        near = ref[at[0]]
        middle = harmonic(near, ref[at[1]])
        east_sum, north_sum = plane_faces(near)
        halo0[side] = east_sum
        halo0[2 + side] = north_sum
        halo0[4 + side] = middle
        halo0[6 + side] = weight(near, east_sum, north_sum, shared, middle)
        thick = 1
        for faces, count in ((faces1, 8), (faces2, 4), (faces3, 2)):
            for k in range(thick, 2 * thick):
                east_k, north_k = plane_faces(ref[at[k]])
                if k == 1:
                    halo0[8 + side] = weight(ref[at[1]], east_k, north_k, middle, harmonic(ref[at[1]], ref[at[2]]))
                east_sum = east_sum + east_k
                north_sum = north_sum + north_k
            thick *= 2
            halo = parts(faces, count)[4]
            outer = harmonic(ref[at[thick - 1]], ref[at[thick]])
            halo[side] = east_sum
            halo[2 + side] = north_sum
            halo[4 + side] = outer
            halo[6 + side] = weight(near, east_sum, north_sum, shared, outer)


def make_last_faces(faces4, other, down, up, east5, north5, w5):
    east4, north4, _, w4, _ = parts(faces4, 1)
    east5[0] = east4[0] + other[0]
    north5[0] = north4[0] + other[1]
    w5[0] = weight(w4[0], east5[0], north5[0], down[0], up[0])


def sweep_and_rest(s, first, total, second, faces, count):
    east, north, z, w, halo = parts(faces, count)

    def sweep(q):
        t = 1.2 * s[q + 1] + neighbours(first[q + 2], first[q + 1], first[q + 3], east[q], north[q], z[q], z[q + 1])
        total[q] = t
        second[q + 1] = w[q] * t

    loop(count, sweep)
    for side, q, down, up in ((0, -1, halo[4], z[0]), (1, count, z[count], halo[5])):
        second[q + 1] = halo[6 + side] * (1.2 * s[q + 1] + neighbours(
            first[q + 2], first[q + 1], first[q + 3], halo[side], halo[2 + side], down, up))

    def rest(q):
        return s[q + 1] - damping * total[q] + neighbours(
            second[q + 1], second[q], second[q + 2], east[q], north[q], z[q], z[q + 1])

    return rest


def fine_level(s_own, s_low, s_high, faces, faces_next, fine, s_next, edge_down, edge_up, s, first, total, second):
    strip = fine.shape[2]
    columns = s.shape[2]
    _, _, _, w, halo = parts(faces, 16)
    w_next = parts(faces_next, 8)[3]
    blank = jnp.zeros((HALO - THIN, columns), jnp.float32)

    def place(k, value):
        s[k, :HALO - THIN] = blank
        s[k, HALO - THIN:HALO + strip + THIN] = value
        s[k, HALO + strip + THIN:] = blank

    place(0, s_low[0])
    first[0] = halo[8] * s[0]
    place(0, s_high[1])
    first[19] = halo[9] * s[0]
    place(0, s_low[1])
    first[1] = halo[6] * s[0]
    place(17, s_high[0])
    first[18] = halo[7] * s[17]

    def start(q):
        place(q + 1, s_own[q])
        first[q + 2] = w[q] * s[q + 1]

    loop(16, start)
    rest = sweep_and_rest(s, first, total, second, faces, 16)

    def pair(q):
        s_next[q] = rest(2 * q) + rest(2 * q + 1)
        fine[q, 0] = second[2 * q + 1, HALO:HALO + strip]
        fine[q, 1] = second[2 * q + 2, HALO:HALO + strip]

    loop(8, pair)
    edge_down[0] = s_next[0]
    edge_down[1] = w_next[1] * s_next[1]
    edge_up[0] = w_next[6] * s_next[6]
    edge_up[1] = s_next[7]


def open_level(s_own, faces, low, high, s, first):
    count = s_own.shape[0]
    _, _, _, w, halo = parts(faces, count)
    s[0] = low[1]
    s[count + 1] = high[0]
    first[0] = low[0]
    first[1] = halo[6] * low[1]
    first[count + 2] = halo[7] * high[0]
    first[count + 3] = high[1]

    def start(q):
        s[q + 1] = s_own[q]
        first[q + 2] = w[q] * s_own[q]

    loop(count, start)


def first_coarse_level(s_own, low, high, faces, out, s_next, top, bottom, s, first, total, second):
    strip = out.shape[1]
    open_level(s_own, faces, low, high, s, first)
    rest = sweep_and_rest(s, first, total, second, faces, s_own.shape[0])

    def pair(q):
        value = rest(2 * q) + rest(2 * q + 1)
        s_next[q] = value[HALO:HALO + strip]
        top[q] = value[HALO:2 * HALO]
        bottom[q] = value[strip:HALO + strip]
        out[2 * q] = second[2 * q + 1, HALO:HALO + strip]
        out[2 * q + 1] = second[2 * q + 2, HALO:HALO + strip]

    loop(4, pair)


def middle_level(s_own, low, high, faces, faces_next, out, s_next, *rest_refs):
    edges, (s, first, total, second) = rest_refs[:-4], rest_refs[-4:]
    count = s_own.shape[0]
    w_next = parts(faces_next, count // 2)[3]
    strip = out.shape[1]
    open_level(s_own, faces, low, high, s, first)
    rest = sweep_and_rest(s, first, total, second, faces, s_own.shape[0])
    for q in range(count // 2):
        s_next[q] = rest(2 * q) + rest(2 * q + 1)
    for q in range(count):
        out[q] = second[q + 1, HALO:HALO + strip]
    if len(edges) == 2:
        edge_down, edge_up = edges
        edge_down[0] = s_next[0]
        edge_down[1] = w_next[1] * s_next[1]
        edge_up[0] = w_next[count // 2 - 2] * s_next[count // 2 - 2]
        edge_up[1] = s_next[count // 2 - 1]
    else:
        edges[0][0] = w_next[0] * s_next[0]


def widen(source2, above, below, faces2, fine, plane_out, s, edge_down, edge_up, back):
    count, strip, _ = source2.shape
    w2 = parts(faces2, count)[3]
    for q in range(count):
        s[q, :HALO] = above[q]
        s[q, HALO:HALO + strip] = source2[q]
        s[q, HALO + strip:] = below[q]
    edge_down[0] = s[0]
    edge_down[1] = w2[1] * s[1]
    edge_up[0] = w2[count - 2] * s[count - 2]
    edge_up[1] = s[count - 1]

    def gather(k):
        back[k, 0] = fine[k, 0]
        back[k, 1] = fine[k, 1]
        back[k, 2] = plane_out[k]

    loop(RING, gather)


def sweep_last(s, first, low, high, faces, total, second):
    east, north, z, w, _ = parts(faces, 1)
    t = 1.2 * s[0] + neighbours(first[0], low[0], high[0], east[0], north[0], z[0], z[1])
    total[0] = t
    second[0] = w[0] * t


def rest_last(s, total, second, low, high, faces, out):
    east, north, z, _, _ = parts(faces, 1)
    out[0] = s[0] - damping * total[0] + neighbours(second[0], low[0], high[0], east[0], north[0], z[0], z[1])


def finish(s, first, low, high, east, north, down, up, w, second2, second3, second4, settled, out):
    strip = out.shape[1]
    second5 = w[0] * (1.2 * s[0] + neighbours(first[0], low[0], high[0], east[0], north[0], down[0], up[0]))
    own = slice(HALO, HALO + strip)
    for k in range(RING):
        out[k] = ((second2[k // 2] + second3[k // 4]) + second4[0, own]) + second5[own]


def exchange(edge_low, edge_high, distance=RING):
    return shifted(edge_high, distance), shifted(edge_low, -distance)


def on_device(right_side, labels, fraction):
    planes, rows, columns = right_side.shape
    strip = rows // RING
    frame = strip + 2 * HALO
    at_core = lax.axis_index("xy")
    even_ring = (lax.axis_index("gz") // RING) % 2 == 0

    def edges_of(first_rows, last_rows):
        got = lax.ppermute(jnp.where(at_core == 0, last_rows, first_rows), "xy", [(0, 1), (1, 0)])
        return jnp.where(at_core == 1, got, 0.0), jnp.where(at_core == 0, got, 0.0)

    def shape(n):
        return (n, frame, columns)

    place = jnp.reshape(lax.axis_index("gz") % RING, (1,)).astype(jnp.int32)
    c_top, c_bottom = edges_of(conductivity(labels[:, :HALO], fraction[:, :HALO]),
                               conductivity(labels[:, rows - HALO:], fraction[:, rows - HALO:]))
    cuts = call(cut_conduct, [(planes, frame, columns)] * RING, [(planes, rows + 2 * HALO, columns)],
                place, labels, fraction, c_top, c_bottom, limit=10)
    s_top, s_bottom = edges_of(right_side[:, :HALO], right_side[:, rows - HALO:])
    thin = strip + 2 * THIN
    s_cuts = call(cut_source, [(planes, thin, columns)] * RING, [(planes, rows + 2 * HALO, columns)],
                  place, right_side, s_top, s_bottom, limit=10)
    c_parts = [cuts[0]] + [ring_permuted(cuts[k], k) for k in range(1, RING)]
    s_cuts = list(s_cuts)
    for k in (1, RING - 1):
        s_cuts[k] = after(s_cuts[k], c_parts[1], c_parts[2])
    s_parts = [s_cuts[0]] + [ring_permuted(s_cuts[k], k) for k in range(1, RING)]

    c, bundle_down, bundle_up = call(join, [shape(16), shape(REACH), shape(REACH)], [], place, *c_parts, limit=10, settled=(s_parts[1], s_parts[7]))
    c_low, c_high = exchange(bundle_down, bundle_up)
    faces0, faces1, faces2, faces3, faces4 = call(
        make_faces, [shape(planes_of(n)) for n in (16, 8, 4, 2, 1)], [], c, c_low, c_high, limit=28, work=12.0)
    east4, north4, z_low, z_high = faces4[0:1], faces4[1:2], faces4[2:3], faces4[3:4]
    other = partner(jnp.concatenate([east4, north4, jnp.where(even_ring, z_low, z_high)], axis=0))
    down5 = jnp.where(even_ring, z_low, other[2:])
    up5 = jnp.where(even_ring, other[2:], z_high)
    east5, north5, w5 = call(make_last_faces, [shape(1)] * 3, [], faces4, other, down5, up5)

    s_own, edge_down, edge_up = call(
        join, [(16, thin, columns), (2, thin, columns), (2, thin, columns)], [], place, *s_parts, limit=10, settled=(faces4,))
    s_low, s_high = exchange(edge_down, edge_up)
    fine, s1, edge_down, edge_up = call(
        fine_level, [(RING, planes, strip, columns), shape(8), shape(2), shape(2)],
        [shape(18), shape(20), shape(16), shape(18)],
        s_own, s_low, s_high, faces0, faces1, limit=30, work=8.0)

    low, high = exchange(edge_down, edge_up)
    plane_out, s2, top, bottom = call(
        first_coarse_level,
        [(8, strip, columns), (4, strip, columns), (4, HALO, columns), (4, HALO, columns)],
        [shape(10), shape(12), shape(8), shape(10)], s1, low, high, faces1, limit=15, work=4.0)

    above = row_shifted(bottom, 1)
    below = row_shifted(top, -1)
    s2, edge_down, edge_up, back = call(
        widen, [shape(4), shape(2), shape(2), (RING, planes + 1, strip, columns)], [], s2, above, below, faces2, fine, plane_out, limit=10)
    low, high = exchange(edge_down, edge_up)
    second2, s3, edge_down, edge_up = call(
        middle_level, [(4, strip, columns), shape(2), shape(2), shape(2)], [shape(6), shape(8), shape(4), shape(6)],
        s2, low, high, faces2, faces3, limit=10)
    low, high = exchange(edge_down, edge_up)
    second3, s4, first4 = call(
        middle_level, [(2, strip, columns), shape(1), shape(1)], [shape(4), shape(6), shape(2), shape(4)],
        s3, low, high, faces3, faces4)
    low, high = exchange(first4, first4)
    total4, second4 = call(sweep_last, [shape(1), shape(1)], [], s4, first4, low, high, faces4)
    low, high = exchange(second4, second4)
    (rest4,) = call(rest_last, [shape(1)], [], s4, total4, second4, low, high, faces4)
    s5 = rest4 + partner(rest4)
    first5 = w5 * s5
    low, high = exchange(first5, first5, 2 * RING)
    back = transposed(back)
    (summed,) = call(finish, [(RING, strip, columns)], [],
                     s5, first5, low, high, east5, north5, down5, up5, w5, second2, second3, second4, back[0, 0, :HALO])

    fine_iterate = jnp.transpose(back[:, :planes], (1, 0, 2, 3)).reshape(planes, rows, columns)
    plane_iterate = back[:, planes].reshape(1, rows, columns)
    coarse_return = transposed(summed).reshape(1, rows, columns)
    return fine_iterate, plane_iterate, coarse_return


def solution(mesh):
    spec = P("gz", "xy", None)
    return jax.shard_map(
        on_device,
        mesh=mesh,
        in_specs=(spec, spec, spec),
        out_specs=(spec, spec, spec),
        check_vma=False,
    )
```

```python
from functools import partial

import jax
import jax.numpy as jnp
from jax import lax
from jax.experimental import pallas as pl
from jax.experimental.pallas import tpu as pltpu
from jax.sharding import PartitionSpec as P

RING = 8
HALO = 8
REACH = 9
THIN = 4
damping = 0.8
pore_value = 1.0
grain_value = 0.1
clay_value = 0.3
TINY = 1e-30


def ring_groups(count):
    return [[r * RING + k for k in range(RING)] for r in range(count // RING)]


def shifted(value, by):
    size = lax.axis_size("gz")
    pairs = [(i, i + by) for i in range(size) if 0 <= i + by < size]
    return lax.ppermute(value, "gz", pairs)


def row_shifted(value, by):
    pairs = []
    for ring in range(lax.axis_size("gz") // RING):
        for t in range(2 * RING):
            u = t + by
            if 0 <= u < 2 * RING:
                pairs.append(((ring * RING + t % RING) * 2 + t // RING, (ring * RING + u % RING) * 2 + u // RING))
    return lax.ppermute(value, ("gz", "xy"), pairs)


def partner(value):
    size = lax.axis_size("gz")
    return lax.ppermute(value, "gz", [(i, i + RING if (i // RING) % 2 == 0 else i - RING) for i in range(size)])


def transposed(value):
    return lax.all_to_all(value, "gz", 0, 0, axis_index_groups=ring_groups(lax.axis_size("gz")), tiled=True)


def conductivity(labels, fraction):
    return jnp.where(labels == 0, pore_value, jnp.where(labels == 1, grain_value, clay_value)) * fraction


def harmonic(one_side, other_side):
    return (2.0 * one_side * other_side) / jnp.maximum(one_side + other_side, TINY)


def next_row(v):
    return pltpu.roll(v, v.shape[0] - 1, 0)


def previous_row(v):
    return pltpu.roll(v, 1, 0)


def next_column(v):
    return pltpu.roll(v, v.shape[1] - 1, 1)


def previous_column(v):
    return pltpu.roll(v, 1, 1)


def neighbours(v, below, above, east, north, down, up):
    return (
        east * next_row(v)
        + previous_row(east * v)
        + north * next_column(v)
        + previous_column(north * v)
        + down * below
        + up * above
    )


def weight(c, east, north, down, up):
    diagonal = east + previous_row(east) + north + previous_column(north) + down + up
    return jnp.where(c > 0, damping / jnp.where(c > 0, diagonal, 1.0), 0.0)


def loop(count, body):
    def step(k, carry):
        body(k)
        return carry

    lax.fori_loop(0, count, step, 0)


def call(kernel, outs, scratch, *args, limit=8, work=0.0, settled=()):
    shapes = [jax.ShapeDtypeStruct(s, jnp.float32) for s in outs]
    vmem = pl.BlockSpec(memory_space=pltpu.VMEM)
    smem = pl.BlockSpec(memory_space=pltpu.SMEM)
    cost = pl.CostEstimate(flops=int(work * 1.0e9), bytes_accessed=int(work * 3.0e6), transcendentals=0) if work else None

    def body(*refs):
        kernel(*refs[len(settled):])

    return pl.pallas_call(
        body,
        out_shape=shapes,
        in_specs=[pl.BlockSpec(memory_space=pl.ANY)] * len(settled) + [smem if a.dtype == jnp.int32 and a.ndim == 1 else vmem for a in args],
        out_specs=[vmem] * len(shapes),
        scratch_shapes=[pltpu.VMEM(s, jnp.float32) for s in scratch],
        compiler_params=pltpu.CompilerParams(vmem_limit_bytes=limit * 1024 * 1024),
        cost_estimate=cost,
    )(*settled, *args)


def ring_permuted(value, by):
    size = lax.axis_size("gz")
    return lax.ppermute(value, "gz", [(i, i // RING * RING + (i + by) % RING) for i in range(size)])


def after(value, *settled):
    def nothing(*refs):
        pass

    there = pl.BlockSpec(memory_space=pl.ANY)
    return pl.pallas_call(
        nothing,
        out_shape=jax.ShapeDtypeStruct(value.shape, value.dtype),
        in_specs=[there] * (1 + len(settled)),
        out_specs=there,
        compiler_params=pltpu.CompilerParams(vmem_limit_bytes=1024 * 1024),
        input_output_aliases={0: 0},
    )(value, *settled)


def cut_conduct(place, labels, fraction, top, bottom, *rest):
    outs, full = rest[:-1], rest[-1]
    planes, rows, _ = labels.shape
    strip = rows // RING
    for p in range(planes):
        full[p, :HALO] = top[p]
        full[p, HALO + rows:] = bottom[p]
        for k in range(RING):
            at = k * strip
            full[p, HALO + at:HALO + at + strip] = conductivity(labels[p, at:at + strip], fraction[p, at:at + strip])
        for k in range(RING):
            start = pl.multiple_of(((place[0] + k) % RING) * strip, strip)
            outs[k][p] = full[p, pl.ds(start, strip + 2 * HALO)]


def cut_source(source, top, bottom, out):
    planes, rows, _ = source.shape
    strip = rows // RING
    for p in range(planes):
        for k in range(RING):
            start = k * strip
            out[k, p, :THIN] = top[p, HALO - THIN:] if k == 0 else source[p, start - THIN:start]
            out[k, p, THIN:THIN + strip] = source[p, start:start + strip]
            out[k, p, THIN + strip:] = bottom[p, :THIN] if k == RING - 1 else source[p, start + strip:start + strip + THIN]


def join(place, *refs):
    out, low, high, ready = refs[RING:]
    ready[...] = refs[0][0, :HALO]
    for k in range(RING):
        start = ((place[0] + RING - k) % RING) * 2
        out[start] = refs[k][0]
        out[start + 1] = refs[k][1]
    reach = low.shape[0]
    loop(reach, lambda p: low.__setitem__(p, out[p]))
    loop(reach, lambda p: high.__setitem__(p, out[p + 16 - reach]))


def plane_faces(c):
    last = lax.broadcasted_iota(jnp.int32, c.shape, 1) == c.shape[1] - 1
    return harmonic(c, next_row(c)), jnp.where(last, 0.0, harmonic(c, next_column(c)))


def parts(faces, count):
    east, north = faces.at[0:count], faces.at[count:2 * count]
    z, w = faces.at[2 * count:3 * count + 1], faces.at[3 * count + 1:4 * count + 1]
    return east, north, z, w, faces.at[4 * count + 1:] if count > 1 else None


def planes_of(count):
    return 4 * count + 1 + (0 if count == 1 else 10 if count == 16 else 8)


def make_faces(c, low, high, faces0, faces1, faces2, faces3, faces4):
    east0, north0, z0, w0, halo0 = parts(faces0, 16)

    def z_face(p):
        z0[p] = harmonic(c[p - 1], c[p])

    loop(15, lambda k: z_face(k + 1))
    z0[0] = jnp.where(low[REACH - 1] > 0, harmonic(low[REACH - 1], c[0]), 2.0 * c[0])
    z0[16] = jnp.where(high[0] > 0, harmonic(c[15], high[0]), 2.0 * c[15])

    def weigh(p):
        east, north = plane_faces(c[p])
        east0[p] = east
        north0[p] = north
        w0[p] = weight(c[p], east, north, z0[p], z0[p + 1])

    loop(16, weigh)
    finer, count = faces0, 16
    for coarser in (faces1, faces2, faces3, faces4):
        east_f, north_f, z_f, _, _ = parts(finer, count)
        count //= 2
        east, north, z, w, _ = parts(coarser, count)

        def faces_and_weight(q):
            east_q = east_f[2 * q] + east_f[2 * q + 1]
            north_q = north_f[2 * q] + north_f[2 * q + 1]
            east[q] = east_q
            north[q] = north_q
            z[q] = z_f[2 * q]
            w[q] = weight(c[0], east_q, north_q, z_f[2 * q], z_f[2 * q + 2])

        loop(count, faces_and_weight)
        z[count] = z_f[2 * count]
        finer = coarser

    for side, ref, at, face in ((0, low, [REACH - 1 - k for k in range(REACH)], 0), (1, high, list(range(REACH)), 16)):
        shared = z0[face]
        near = ref[at[0]]
        middle = harmonic(near, ref[at[1]])
        east_sum, north_sum = plane_faces(near)
        halo0[side] = east_sum
        halo0[2 + side] = north_sum
        halo0[4 + side] = middle
        halo0[6 + side] = weight(near, east_sum, north_sum, shared, middle)
        thick = 1
        for faces, count in ((faces1, 8), (faces2, 4), (faces3, 2)):
            for k in range(thick, 2 * thick):
                east_k, north_k = plane_faces(ref[at[k]])
                if k == 1:
                    halo0[8 + side] = weight(ref[at[1]], east_k, north_k, middle, harmonic(ref[at[1]], ref[at[2]]))
                east_sum = east_sum + east_k
                north_sum = north_sum + north_k
            thick *= 2
            halo = parts(faces, count)[4]
            outer = harmonic(ref[at[thick - 1]], ref[at[thick]])
            halo[side] = east_sum
            halo[2 + side] = north_sum
            halo[4 + side] = outer
            halo[6 + side] = weight(near, east_sum, north_sum, shared, outer)


def make_last_faces(faces4, other, down, up, east5, north5, w5):
    east4, north4, _, w4, _ = parts(faces4, 1)
    east5[0] = east4[0] + other[0]
    north5[0] = north4[0] + other[1]
    w5[0] = weight(w4[0], east5[0], north5[0], down[0], up[0])


def sweep_and_rest(s, first, total, second, faces, count):
    east, north, z, w, halo = parts(faces, count)

    def sweep(q):
        t = 1.2 * s[q + 1] + neighbours(first[q + 2], first[q + 1], first[q + 3], east[q], north[q], z[q], z[q + 1])
        total[q] = t
        second[q + 1] = w[q] * t

    loop(count, sweep)
    for side, q, down, up in ((0, -1, halo[4], z[0]), (1, count, z[count], halo[5])):
        second[q + 1] = halo[6 + side] * (1.2 * s[q + 1] + neighbours(
            first[q + 2], first[q + 1], first[q + 3], halo[side], halo[2 + side], down, up))

    def rest(q):
        return s[q + 1] - damping * total[q] + neighbours(
            second[q + 1], second[q], second[q + 2], east[q], north[q], z[q], z[q + 1])

    return rest


def fine_level(s_own, s_low, s_high, faces, faces_next, fine, s_next, edge_down, edge_up, s, first, total, second):
    strip = fine.shape[2]
    columns = s.shape[2]
    _, _, _, w, halo = parts(faces, 16)
    w_next = parts(faces_next, 8)[3]
    blank = jnp.zeros((HALO - THIN, columns), jnp.float32)

    def place(k, value):
        s[k, :HALO - THIN] = blank
        s[k, HALO - THIN:HALO + strip + THIN] = value
        s[k, HALO + strip + THIN:] = blank

    place(0, s_low[0])
    first[0] = halo[8] * s[0]
    place(0, s_high[1])
    first[19] = halo[9] * s[0]
    place(0, s_low[1])
    first[1] = halo[6] * s[0]
    place(17, s_high[0])
    first[18] = halo[7] * s[17]

    def start(q):
        place(q + 1, s_own[q])
        first[q + 2] = w[q] * s[q + 1]

    loop(16, start)
    rest = sweep_and_rest(s, first, total, second, faces, 16)

    def pair(q):
        s_next[q] = rest(2 * q) + rest(2 * q + 1)
        fine[q, 0] = second[2 * q + 1, HALO:HALO + strip]
        fine[q, 1] = second[2 * q + 2, HALO:HALO + strip]

    loop(8, pair)
    edge_down[0] = s_next[0]
    edge_down[1] = w_next[1] * s_next[1]
    edge_up[0] = w_next[6] * s_next[6]
    edge_up[1] = s_next[7]


def open_level(s_own, faces, low, high, s, first):
    count = s_own.shape[0]
    _, _, _, w, halo = parts(faces, count)
    s[0] = low[1]
    s[count + 1] = high[0]
    first[0] = low[0]
    first[1] = halo[6] * low[1]
    first[count + 2] = halo[7] * high[0]
    first[count + 3] = high[1]

    def start(q):
        s[q + 1] = s_own[q]
        first[q + 2] = w[q] * s_own[q]

    loop(count, start)


def first_coarse_level(s_own, low, high, faces, out, s_next, top, bottom, s, first, total, second):
    strip = out.shape[1]
    open_level(s_own, faces, low, high, s, first)
    rest = sweep_and_rest(s, first, total, second, faces, s_own.shape[0])

    def pair(q):
        value = rest(2 * q) + rest(2 * q + 1)
        s_next[q] = value[HALO:HALO + strip]
        top[q] = value[HALO:2 * HALO]
        bottom[q] = value[strip:HALO + strip]
        out[2 * q] = second[2 * q + 1, HALO:HALO + strip]
        out[2 * q + 1] = second[2 * q + 2, HALO:HALO + strip]

    loop(4, pair)


def middle_level(s_own, low, high, faces, faces_next, out, s_next, *rest_refs):
    edges, (s, first, total, second) = rest_refs[:-4], rest_refs[-4:]
    count = s_own.shape[0]
    w_next = parts(faces_next, count // 2)[3]
    strip = out.shape[1]
    open_level(s_own, faces, low, high, s, first)
    rest = sweep_and_rest(s, first, total, second, faces, s_own.shape[0])
    for q in range(count // 2):
        s_next[q] = rest(2 * q) + rest(2 * q + 1)
    for q in range(count):
        out[q] = second[q + 1, HALO:HALO + strip]
    if len(edges) == 2:
        edge_down, edge_up = edges
        edge_down[0] = s_next[0]
        edge_down[1] = w_next[1] * s_next[1]
        edge_up[0] = w_next[count // 2 - 2] * s_next[count // 2 - 2]
        edge_up[1] = s_next[count // 2 - 1]
    else:
        edges[0][0] = w_next[0] * s_next[0]


def widen(source2, above, below, faces2, fine, plane_out, s, edge_down, edge_up, back):
    count, strip, _ = source2.shape
    w2 = parts(faces2, count)[3]
    for q in range(count):
        s[q, :HALO] = above[q]
        s[q, HALO:HALO + strip] = source2[q]
        s[q, HALO + strip:] = below[q]
    edge_down[0] = s[0]
    edge_down[1] = w2[1] * s[1]
    edge_up[0] = w2[count - 2] * s[count - 2]
    edge_up[1] = s[count - 1]

    def gather(k):
        back[k, 0] = fine[k, 0]
        back[k, 1] = fine[k, 1]
        back[k, 2] = plane_out[k]

    loop(RING, gather)


def sweep_last(s, first, low, high, faces, total, second):
    east, north, z, w, _ = parts(faces, 1)
    t = 1.2 * s[0] + neighbours(first[0], low[0], high[0], east[0], north[0], z[0], z[1])
    total[0] = t
    second[0] = w[0] * t


def rest_last(s, total, second, low, high, faces, out):
    east, north, z, _, _ = parts(faces, 1)
    out[0] = s[0] - damping * total[0] + neighbours(second[0], low[0], high[0], east[0], north[0], z[0], z[1])


def finish(s, first, low, high, east, north, down, up, w, second2, second3, second4, settled, out):
    strip = out.shape[1]
    second5 = w[0] * (1.2 * s[0] + neighbours(first[0], low[0], high[0], east[0], north[0], down[0], up[0]))
    own = slice(HALO, HALO + strip)
    for k in range(RING):
        out[k] = ((second2[k // 2] + second3[k // 4]) + second4[0, own]) + second5[own]


def exchange(edge_low, edge_high, distance=RING):
    return shifted(edge_high, distance), shifted(edge_low, -distance)


def on_device(right_side, labels, fraction):
    planes, rows, columns = right_side.shape
    strip = rows // RING
    frame = strip + 2 * HALO
    at_core = lax.axis_index("xy")
    even_ring = (lax.axis_index("gz") // RING) % 2 == 0

    def edges_of(first_rows, last_rows):
        got = lax.ppermute(jnp.where(at_core == 0, last_rows, first_rows), "xy", [(0, 1), (1, 0)])
        return jnp.where(at_core == 1, got, 0.0), jnp.where(at_core == 0, got, 0.0)

    def shape(n):
        return (n, frame, columns)

    place = jnp.reshape(lax.axis_index("gz") % RING, (1,)).astype(jnp.int32)
    c_top, c_bottom = edges_of(conductivity(labels[:, :HALO], fraction[:, :HALO]),
                               conductivity(labels[:, rows - HALO:], fraction[:, rows - HALO:]))
    cuts = call(cut_conduct, [(planes, frame, columns)] * RING, [(planes, rows + 2 * HALO, columns)],
                place, labels, fraction, c_top, c_bottom, limit=10)
    s_top, s_bottom = edges_of(right_side[:, :HALO], right_side[:, rows - HALO:])
    thin = strip + 2 * THIN
    (s_cut,) = call(cut_source, [(RING, planes, thin, columns)], [], right_side, s_top, s_bottom, limit=10)
    c_parts = [cuts[0]] + [ring_permuted(cuts[k], k) for k in range(1, RING)]
    c, bundle_down, bundle_up, ready = call(join, [shape(16), shape(REACH), shape(REACH), (HALO, columns)], [], place, *c_parts, limit=10, settled=(s_cut,))
    s_own = transposed(after(s_cut, ready))
    c_low, c_high = exchange(bundle_down, bundle_up)
    faces0, faces1, faces2, faces3, faces4 = call(
        make_faces, [shape(planes_of(n)) for n in (16, 8, 4, 2, 1)], [], c, c_low, c_high, limit=28, work=12.0)
    east4, north4, z_low, z_high = faces4[0:1], faces4[1:2], faces4[2:3], faces4[3:4]
    other = partner(jnp.concatenate([east4, north4, jnp.where(even_ring, z_low, z_high)], axis=0))
    down5 = jnp.where(even_ring, z_low, other[2:])
    up5 = jnp.where(even_ring, other[2:], z_high)
    east5, north5, w5 = call(make_last_faces, [shape(1)] * 3, [], faces4, other, down5, up5)

    s_own = after(s_own, faces4).reshape(RING * planes, thin, columns)
    s_low, s_high = exchange(s_own[:2], s_own[-2:])
    fine, s1, edge_down, edge_up = call(
        fine_level, [(RING, planes, strip, columns), shape(8), shape(2), shape(2)],
        [shape(18), shape(20), shape(16), shape(18)],
        s_own, s_low, s_high, faces0, faces1, limit=30, work=8.0)

    low, high = exchange(edge_down, edge_up)
    plane_out, s2, top, bottom = call(
        first_coarse_level,
        [(8, strip, columns), (4, strip, columns), (4, HALO, columns), (4, HALO, columns)],
        [shape(10), shape(12), shape(8), shape(10)], s1, low, high, faces1, limit=15, work=4.0)

    above = row_shifted(bottom, 1)
    below = row_shifted(top, -1)
    s2, edge_down, edge_up, back = call(
        widen, [shape(4), shape(2), shape(2), (RING, planes + 1, strip, columns)], [], s2, above, below, faces2, fine, plane_out, limit=10)
    low, high = exchange(edge_down, edge_up)
    second2, s3, edge_down, edge_up = call(
        middle_level, [(4, strip, columns), shape(2), shape(2), shape(2)], [shape(6), shape(8), shape(4), shape(6)],
        s2, low, high, faces2, faces3, limit=10)
    low, high = exchange(edge_down, edge_up)
    second3, s4, first4 = call(
        middle_level, [(2, strip, columns), shape(1), shape(1)], [shape(4), shape(6), shape(2), shape(4)],
        s3, low, high, faces3, faces4)
    low, high = exchange(first4, first4)
    total4, second4 = call(sweep_last, [shape(1), shape(1)], [], s4, first4, low, high, faces4)
    low, high = exchange(second4, second4)
    (rest4,) = call(rest_last, [shape(1)], [], s4, total4, second4, low, high, faces4)
    s5 = rest4 + partner(rest4)
    first5 = w5 * s5
    low, high = exchange(first5, first5, 2 * RING)
    back = transposed(back)
    (summed,) = call(finish, [(RING, strip, columns)], [],
                     s5, first5, low, high, east5, north5, down5, up5, w5, second2, second3, second4, back[0, 0, :HALO])

    fine_iterate = jnp.transpose(back[:, :planes], (1, 0, 2, 3)).reshape(planes, rows, columns)
    plane_iterate = back[:, planes].reshape(1, rows, columns)
    coarse_return = transposed(summed).reshape(1, rows, columns)
    return fine_iterate, plane_iterate, coarse_return


def solution(mesh):
    spec = P("gz", "xy", None)
    return jax.shard_map(
        on_device,
        mesh=mesh,
        in_specs=(spec, spec, spec),
        out_specs=(spec, spec, spec),
        check_vma=False,
    )
```

```python
from functools import partial

import jax
import jax.numpy as jnp
from jax import lax
from jax.experimental import pallas as pl
from jax.experimental.pallas import tpu as pltpu
from jax.sharding import PartitionSpec as P

RING = 8
HALO = 8
REACH = 9
THIN = 4
damping = 0.8
pore_value = 1.0
grain_value = 0.1
clay_value = 0.3
TINY = 1e-30


def ring_groups(count):
    return [[r * RING + k for k in range(RING)] for r in range(count // RING)]


def shifted(value, by):
    size = lax.axis_size("gz")
    pairs = [(i, i + by) for i in range(size) if 0 <= i + by < size]
    return lax.ppermute(value, "gz", pairs)


def row_shifted(value, by):
    pairs = []
    for ring in range(lax.axis_size("gz") // RING):
        for t in range(2 * RING):
            u = t + by
            if 0 <= u < 2 * RING:
                pairs.append(((ring * RING + t % RING) * 2 + t // RING, (ring * RING + u % RING) * 2 + u // RING))
    return lax.ppermute(value, ("gz", "xy"), pairs)


def partner(value):
    size = lax.axis_size("gz")
    return lax.ppermute(value, "gz", [(i, i + RING if (i // RING) % 2 == 0 else i - RING) for i in range(size)])


def transposed(value):
    return lax.all_to_all(value, "gz", 0, 0, axis_index_groups=ring_groups(lax.axis_size("gz")), tiled=True)


def conductivity(labels, fraction):
    return jnp.where(labels == 0, pore_value, jnp.where(labels == 1, grain_value, clay_value)) * fraction


def harmonic(one_side, other_side):
    return (2.0 * one_side * other_side) / jnp.maximum(one_side + other_side, TINY)


def next_row(v):
    return pltpu.roll(v, v.shape[0] - 1, 0)


def previous_row(v):
    return pltpu.roll(v, 1, 0)


def next_column(v):
    return pltpu.roll(v, v.shape[1] - 1, 1)


def previous_column(v):
    return pltpu.roll(v, 1, 1)


def neighbours(v, below, above, east, north, down, up):
    return (
        east * next_row(v)
        + previous_row(east * v)
        + north * next_column(v)
        + previous_column(north * v)
        + down * below
        + up * above
    )


def weight(c, east, north, down, up):
    diagonal = east + previous_row(east) + north + previous_column(north) + down + up
    return jnp.where(c > 0, damping / jnp.where(c > 0, diagonal, 1.0), 0.0)


def loop(count, body):
    def step(k, carry):
        body(k)
        return carry

    lax.fori_loop(0, count, step, 0)


def call(kernel, outs, scratch, *args, limit=8, work=0.0, settled=()):
    shapes = [jax.ShapeDtypeStruct(s, jnp.float32) for s in outs]
    vmem = pl.BlockSpec(memory_space=pltpu.VMEM)
    smem = pl.BlockSpec(memory_space=pltpu.SMEM)
    cost = pl.CostEstimate(flops=int(work * 1.0e9), bytes_accessed=int(work * 3.0e6), transcendentals=0) if work else None

    def body(*refs):
        kernel(*refs[len(settled):])

    return pl.pallas_call(
        body,
        out_shape=shapes,
        in_specs=[pl.BlockSpec(memory_space=pl.ANY)] * len(settled) + [smem if a.dtype == jnp.int32 and a.ndim == 1 else vmem for a in args],
        out_specs=[vmem] * len(shapes),
        scratch_shapes=[pltpu.VMEM(s, jnp.float32) for s in scratch],
        compiler_params=pltpu.CompilerParams(vmem_limit_bytes=limit * 1024 * 1024),
        cost_estimate=cost,
    )(*settled, *args)


ORDER = (3, 5, 4, 2, 6, 1, 7)


def ring_permuted(value, by):
    size = lax.axis_size("gz")
    return lax.ppermute(value, "gz", [(i, i // RING * RING + (i + by) % RING) for i in range(size)])


def after(value, *settled):
    def nothing(*refs):
        pass

    there = pl.BlockSpec(memory_space=pl.ANY)
    return pl.pallas_call(
        nothing,
        out_shape=jax.ShapeDtypeStruct(value.shape, value.dtype),
        in_specs=[there] * (1 + len(settled)),
        out_specs=there,
        compiler_params=pltpu.CompilerParams(vmem_limit_bytes=1024 * 1024),
        input_output_aliases={0: 0},
    )(value, *settled)


def cut_conduct(place, labels, fraction, top, bottom, *rest):
    outs, full = rest[:-1], rest[-1]
    planes, rows, _ = labels.shape
    strip = rows // RING
    for p in range(planes):
        full[p, :HALO] = top[p]
        full[p, HALO + rows:] = bottom[p]
        for k in range(RING):
            at = k * strip
            full[p, HALO + at:HALO + at + strip] = conductivity(labels[p, at:at + strip], fraction[p, at:at + strip])
        for k in range(RING):
            start = pl.multiple_of(((place[0] + k) % RING) * strip, strip)
            outs[k][p] = full[p, pl.ds(start, strip + 2 * HALO)]


def cut_source(source, top, bottom, out):
    planes, rows, _ = source.shape
    strip = rows // RING
    for p in range(planes):
        for k in range(RING):
            start = k * strip
            out[k, p, :THIN] = top[p, HALO - THIN:] if k == 0 else source[p, start - THIN:start]
            out[k, p, THIN:THIN + strip] = source[p, start:start + strip]
            out[k, p, THIN + strip:] = bottom[p, :THIN] if k == RING - 1 else source[p, start + strip:start + strip + THIN]


def join(place, *refs):
    out, low, high, ready = refs[RING:]
    ready[...] = refs[0][0, :HALO]
    for k in range(RING):
        start = ((place[0] + RING - k) % RING) * 2
        out[start] = refs[k][0]
        out[start + 1] = refs[k][1]
    reach = low.shape[0]
    loop(reach, lambda p: low.__setitem__(p, out[p]))
    loop(reach, lambda p: high.__setitem__(p, out[p + 16 - reach]))


def plane_faces(c):
    last = lax.broadcasted_iota(jnp.int32, c.shape, 1) == c.shape[1] - 1
    return harmonic(c, next_row(c)), jnp.where(last, 0.0, harmonic(c, next_column(c)))


def parts(faces, count):
    east, north = faces.at[0:count], faces.at[count:2 * count]
    z, w = faces.at[2 * count:3 * count + 1], faces.at[3 * count + 1:4 * count + 1]
    return east, north, z, w, faces.at[4 * count + 1:] if count > 1 else None


def planes_of(count):
    return 4 * count + 1 + (0 if count == 1 else 10 if count == 16 else 8)


def make_faces(place, c, low, high, faces0, faces1, faces2, faces3, faces4, pack):
    east0, north0, z0, w0, halo0 = parts(faces0, 16)

    def z_face(p):
        z0[p] = harmonic(c[p - 1], c[p])

    loop(15, lambda k: z_face(k + 1))
    z0[0] = jnp.where(low[REACH - 1] > 0, harmonic(low[REACH - 1], c[0]), 2.0 * c[0])
    z0[16] = jnp.where(high[0] > 0, harmonic(c[15], high[0]), 2.0 * c[15])

    def weigh(p):
        east, north = plane_faces(c[p])
        east0[p] = east
        north0[p] = north
        w0[p] = weight(c[p], east, north, z0[p], z0[p + 1])

    loop(16, weigh)
    finer, count = faces0, 16
    for coarser in (faces1, faces2, faces3, faces4):
        east_f, north_f, z_f, _, _ = parts(finer, count)
        count //= 2
        east, north, z, w, _ = parts(coarser, count)

        def faces_and_weight(q):
            east_q = east_f[2 * q] + east_f[2 * q + 1]
            north_q = north_f[2 * q] + north_f[2 * q + 1]
            east[q] = east_q
            north[q] = north_q
            z[q] = z_f[2 * q]
            w[q] = weight(c[0], east_q, north_q, z_f[2 * q], z_f[2 * q + 2])

        loop(count, faces_and_weight)
        z[count] = z_f[2 * count]
        finer = coarser

    for side, ref, at, face in ((0, low, [REACH - 1 - k for k in range(REACH)], 0), (1, high, list(range(REACH)), 16)):
        shared = z0[face]
        near = ref[at[0]]
        middle = harmonic(near, ref[at[1]])
        east_sum, north_sum = plane_faces(near)
        halo0[side] = east_sum
        halo0[2 + side] = north_sum
        halo0[4 + side] = middle
        halo0[6 + side] = weight(near, east_sum, north_sum, shared, middle)
        thick = 1
        for faces, count in ((faces1, 8), (faces2, 4), (faces3, 2)):
            for k in range(thick, 2 * thick):
                east_k, north_k = plane_faces(ref[at[k]])
                if k == 1:
                    halo0[8 + side] = weight(ref[at[1]], east_k, north_k, middle, harmonic(ref[at[1]], ref[at[2]]))
                east_sum = east_sum + east_k
                north_sum = north_sum + north_k
            thick *= 2
            halo = parts(faces, count)[4]
            outer = harmonic(ref[at[thick - 1]], ref[at[thick]])
            halo[side] = east_sum
            halo[2 + side] = north_sum
            halo[4 + side] = outer
            halo[6 + side] = weight(near, east_sum, north_sum, shared, outer)
    pack[0] = faces4[0]
    pack[1] = faces4[1]
    pack[2] = jnp.where(place[1] == 0, faces4[2], faces4[3])


def make_last_faces(place, faces4, other, faces5):
    east4, north4, z4, w4, _ = parts(faces4, 1)
    lower = place[1] == 0
    east = east4[0] + other[0]
    north = north4[0] + other[1]
    down = jnp.where(lower, z4[0], other[2])
    up = jnp.where(lower, other[2], z4[1])
    for k, value in enumerate((east, north, down, up, weight(w4[0], east, north, down, up))):
        faces5[k] = value


def begin_last(rest4, other, faces5, s, first):
    s[0] = rest4[0] + other[0]
    first[0] = faces5[4] * s[0]
def sweep_and_rest(s, first, total, second, faces, count):
    east, north, z, w, halo = parts(faces, count)

    def sweep(q):
        t = 1.2 * s[q + 1] + neighbours(first[q + 2], first[q + 1], first[q + 3], east[q], north[q], z[q], z[q + 1])
        total[q] = t
        second[q + 1] = w[q] * t

    loop(count, sweep)
    for side, q, down, up in ((0, -1, halo[4], z[0]), (1, count, z[count], halo[5])):
        second[q + 1] = halo[6 + side] * (1.2 * s[q + 1] + neighbours(
            first[q + 2], first[q + 1], first[q + 3], halo[side], halo[2 + side], down, up))

    def rest(q):
        return s[q + 1] - damping * total[q] + neighbours(
            second[q + 1], second[q], second[q + 2], east[q], north[q], z[q], z[q + 1])

    return rest


def fine_level(s_own, s_low, s_high, faces, faces_next, fine, s_next, edge_down, edge_up, s, first, total, second):
    strip = fine.shape[2]
    columns = s.shape[2]
    _, _, _, w, halo = parts(faces, 16)
    w_next = parts(faces_next, 8)[3]
    blank = jnp.zeros((HALO - THIN, columns), jnp.float32)

    def place(k, value):
        s[k, :HALO - THIN] = blank
        s[k, HALO - THIN:HALO + strip + THIN] = value
        s[k, HALO + strip + THIN:] = blank

    place(0, s_low[0])
    first[0] = halo[8] * s[0]
    place(0, s_high[1])
    first[19] = halo[9] * s[0]
    place(0, s_low[1])
    first[1] = halo[6] * s[0]
    place(17, s_high[0])
    first[18] = halo[7] * s[17]

    def start(q):
        place(q + 1, s_own[q])
        first[q + 2] = w[q] * s[q + 1]

    loop(16, start)
    rest = sweep_and_rest(s, first, total, second, faces, 16)

    def pair(q):
        s_next[q] = rest(2 * q) + rest(2 * q + 1)
        fine[q, 0] = second[2 * q + 1, HALO:HALO + strip]
        fine[q, 1] = second[2 * q + 2, HALO:HALO + strip]

    loop(8, pair)
    edge_down[0] = s_next[0]
    edge_down[1] = w_next[1] * s_next[1]
    edge_up[0] = w_next[6] * s_next[6]
    edge_up[1] = s_next[7]


def open_level(s_own, faces, low, high, s, first):
    count = s_own.shape[0]
    _, _, _, w, halo = parts(faces, count)
    s[0] = low[1]
    s[count + 1] = high[0]
    first[0] = low[0]
    first[1] = halo[6] * low[1]
    first[count + 2] = halo[7] * high[0]
    first[count + 3] = high[1]

    def start(q):
        s[q + 1] = s_own[q]
        first[q + 2] = w[q] * s_own[q]

    loop(count, start)


def first_coarse_level(s_own, low, high, faces, out, s_next, top, bottom, s, first, total, second):
    strip = out.shape[1]
    open_level(s_own, faces, low, high, s, first)
    rest = sweep_and_rest(s, first, total, second, faces, s_own.shape[0])

    def pair(q):
        value = rest(2 * q) + rest(2 * q + 1)
        s_next[q] = value[HALO:HALO + strip]
        top[q] = value[HALO:2 * HALO]
        bottom[q] = value[strip:HALO + strip]
        out[2 * q] = second[2 * q + 1, HALO:HALO + strip]
        out[2 * q + 1] = second[2 * q + 2, HALO:HALO + strip]

    loop(4, pair)


def middle_level(s_own, low, high, faces, faces_next, out, s_next, *rest_refs):
    edges, (s, first, total, second) = rest_refs[:-4], rest_refs[-4:]
    count = s_own.shape[0]
    w_next = parts(faces_next, count // 2)[3]
    strip = out.shape[1]
    open_level(s_own, faces, low, high, s, first)
    rest = sweep_and_rest(s, first, total, second, faces, s_own.shape[0])
    for q in range(count // 2):
        s_next[q] = rest(2 * q) + rest(2 * q + 1)
    for q in range(count):
        out[q] = second[q + 1, HALO:HALO + strip]
    if len(edges) == 2:
        edge_down, edge_up = edges
        edge_down[0] = s_next[0]
        edge_down[1] = w_next[1] * s_next[1]
        edge_up[0] = w_next[count // 2 - 2] * s_next[count // 2 - 2]
        edge_up[1] = s_next[count // 2 - 1]
    else:
        edges[0][0] = w_next[0] * s_next[0]


def widen(source2, above, below, faces2, fine, plane_out, s, edge_down, edge_up, back):
    count, strip, _ = source2.shape
    w2 = parts(faces2, count)[3]
    for q in range(count):
        s[q, :HALO] = above[q]
        s[q, HALO:HALO + strip] = source2[q]
        s[q, HALO + strip:] = below[q]
    edge_down[0] = s[0]
    edge_down[1] = w2[1] * s[1]
    edge_up[0] = w2[count - 2] * s[count - 2]
    edge_up[1] = s[count - 1]

    def gather(k):
        back[k, 0] = fine[k, 0]
        back[k, 1] = fine[k, 1]
        back[k, 2] = plane_out[k]

    loop(RING, gather)


def sweep_last(s, first, low, high, faces, total, second):
    east, north, z, w, _ = parts(faces, 1)
    t = 1.2 * s[0] + neighbours(first[0], low[0], high[0], east[0], north[0], z[0], z[1])
    total[0] = t
    second[0] = w[0] * t


def rest_last(s, total, second, low, high, faces, out):
    east, north, z, _, _ = parts(faces, 1)
    out[0] = s[0] - damping * total[0] + neighbours(second[0], low[0], high[0], east[0], north[0], z[0], z[1])


def finish(s, first, low, high, faces5, second2, second3, second4, out):
    strip = out.shape[1]
    east, north, down, up, w = (faces5[k] for k in range(5))
    second5 = w * (1.2 * s[0] + neighbours(first[0], low[0], high[0], east, north, down, up))
    own = slice(HALO, HALO + strip)
    for k in range(RING):
        out[k] = ((second2[k // 2] + second3[k // 4]) + second4[0, own]) + second5[own]


def exchange(edge_low, edge_high, distance=RING):
    return shifted(edge_high, distance), shifted(edge_low, -distance)


def on_device(right_side, labels, fraction):
    planes, rows, columns = right_side.shape
    strip = rows // RING
    frame = strip + 2 * HALO
    at_core = lax.axis_index("xy")

    def edges_of(first_rows, last_rows):
        got = lax.ppermute(jnp.where(at_core == 0, last_rows, first_rows), "xy", [(0, 1), (1, 0)])
        return jnp.where(at_core == 1, got, 0.0), jnp.where(at_core == 0, got, 0.0)

    def shape(n):
        return (n, frame, columns)

    at_ring = lax.axis_index("gz")
    place = jnp.stack([at_ring % RING, at_ring // RING % 2]).astype(jnp.int32)
    c_top, c_bottom = edges_of(conductivity(labels[:, :HALO], fraction[:, :HALO]),
                               conductivity(labels[:, rows - HALO:], fraction[:, rows - HALO:]))
    cuts = call(cut_conduct, [(planes, frame, columns)] * RING, [(planes, rows + 2 * HALO, columns)],
                place, labels, fraction, c_top, c_bottom, limit=10)
    s_top, s_bottom = edges_of(right_side[:, :HALO], right_side[:, rows - HALO:])
    thin = strip + 2 * THIN
    (s_cut,) = call(cut_source, [(RING, planes, thin, columns)], [], right_side, s_top, s_bottom, limit=10)
    came = {k: ring_permuted(cuts[k], k) for k in ORDER}
    c_parts = [cuts[0]] + [came[k] for k in range(1, RING)]
    c, bundle_down, bundle_up, ready = call(join, [shape(16), shape(REACH), shape(REACH), (HALO, columns)], [], place, *c_parts, limit=10, settled=(s_cut,))
    s_own = transposed(after(s_cut, ready))
    c_low, c_high = exchange(bundle_down, bundle_up)
    faces0, faces1, faces2, faces3, faces4, pack = call(
        make_faces, [shape(planes_of(n)) for n in (16, 8, 4, 2, 1)] + [shape(3)], [], place, c, c_low, c_high, limit=28, work=12.0)
    (faces5,) = call(make_last_faces, [shape(5)], [], place, faces4, partner(pack))

    s_own = s_own.reshape(RING * planes, thin, columns)
    s_low, s_high = exchange(s_own[:2], s_own[-2:])
    fine, s1, edge_down, edge_up = call(
        fine_level, [(RING, planes, strip, columns), shape(8), shape(2), shape(2)],
        [shape(18), shape(20), shape(16), shape(18)],
        s_own, s_low, s_high, faces0, faces1, limit=30, work=8.0)

    low, high = exchange(edge_down, edge_up)
    plane_out, s2, top, bottom = call(
        first_coarse_level,
        [(8, strip, columns), (4, strip, columns), (4, HALO, columns), (4, HALO, columns)],
        [shape(10), shape(12), shape(8), shape(10)], s1, low, high, faces1, limit=15, work=4.0)

    above = row_shifted(bottom, 1)
    below = row_shifted(top, -1)
    s2, edge_down, edge_up, back = call(
        widen, [shape(4), shape(2), shape(2), (RING, planes + 1, strip, columns)], [], s2, above, below, faces2, fine, plane_out, limit=10)
    low, high = exchange(edge_down, edge_up)
    second2, s3, edge_down, edge_up = call(
        middle_level, [(4, strip, columns), shape(2), shape(2), shape(2)], [shape(6), shape(8), shape(4), shape(6)],
        s2, low, high, faces2, faces3, limit=10)
    low, high = exchange(edge_down, edge_up)
    second3, s4, first4 = call(
        middle_level, [(2, strip, columns), shape(1), shape(1)], [shape(4), shape(6), shape(2), shape(4)],
        s3, low, high, faces3, faces4)
    low, high = exchange(first4, first4)
    total4, second4 = call(sweep_last, [shape(1), shape(1)], [], s4, first4, low, high, faces4)
    low, high = exchange(second4, second4)
    (rest4,) = call(rest_last, [shape(1)], [], s4, total4, second4, low, high, faces4)
    s5, first5 = call(begin_last, [shape(1), shape(1)], [], rest4, partner(rest4), faces5)
    low, high = exchange(first5, first5, 2 * RING)
    back = transposed(back)
    (summed,) = call(finish, [(RING, strip, columns)], [],
                     s5, first5, low, high, faces5, second2, second3, second4, settled=(back,))

    fine_iterate = jnp.transpose(back[:, :planes], (1, 0, 2, 3)).reshape(planes, rows, columns)
    plane_iterate = back[:, planes].reshape(1, rows, columns)
    coarse_return = transposed(summed).reshape(1, rows, columns)
    return fine_iterate, plane_iterate, coarse_return


def solution(mesh):
    spec = P("gz", "xy", None)
    return jax.shard_map(
        on_device,
        mesh=mesh,
        in_specs=(spec, spec, spec),
        out_specs=(spec, spec, spec),
        check_vma=False,
    )
```

```python
from functools import partial

import jax
import jax.numpy as jnp
from jax import lax
from jax.experimental import pallas as pl
from jax.experimental.pallas import tpu as pltpu
from jax.sharding import PartitionSpec as P

RING = 8
HALO = 8
REACH = 9
THIN = 4
damping = 0.8
pore_value = 1.0
grain_value = 0.1
clay_value = 0.3
TINY = 1e-6


def ring_groups(count):
    return [[r * RING + k for k in range(RING)] for r in range(count // RING)]


def shifted(value, by):
    size = lax.axis_size("gz")
    pairs = [(i, i + by) for i in range(size) if 0 <= i + by < size]
    return lax.ppermute(value, "gz", pairs)


def row_shifted(value, by):
    pairs = []
    for ring in range(lax.axis_size("gz") // RING):
        for t in range(2 * RING):
            u = t + by
            if 0 <= u < 2 * RING:
                pairs.append(((ring * RING + t % RING) * 2 + t // RING, (ring * RING + u % RING) * 2 + u // RING))
    return lax.ppermute(value, ("gz", "xy"), pairs)


def partner(value):
    size = lax.axis_size("gz")
    return lax.ppermute(value, "gz", [(i, i + RING if (i // RING) % 2 == 0 else i - RING) for i in range(size)])


def transposed(value):
    return lax.all_to_all(value, "gz", 0, 0, axis_index_groups=ring_groups(lax.axis_size("gz")), tiled=True)


def conductivity(labels, fraction):
    return jnp.where(labels == 0, pore_value, jnp.where(labels == 1, grain_value, clay_value)) * fraction


def inverse(x):
    guess = pl.reciprocal(x, approx=True)
    return guess * (2.0 - x * guess)


def harmonic(one_side, other_side):
    return (2.0 * one_side * other_side) * inverse(jnp.maximum(one_side + other_side, TINY))


def next_row(v):
    return pltpu.roll(v, v.shape[0] - 1, 0)


def previous_row(v):
    return pltpu.roll(v, 1, 0)


def next_column(v):
    return pltpu.roll(v, v.shape[1] - 1, 1)


def previous_column(v):
    return pltpu.roll(v, 1, 1)


def neighbours(v, below, above, east, north, down, up):
    return (
        east * next_row(v)
        + previous_row(east * v)
        + north * next_column(v)
        + previous_column(north * v)
        + down * below
        + up * above
    )


def weight(c, east, north, down, up):
    diagonal = east + previous_row(east) + north + previous_column(north) + down + up
    return jnp.where(c > 0, damping * inverse(jnp.where(c > 0, diagonal, 1.0)), 0.0)


def loop(count, body):
    def step(k, carry):
        body(k)
        return carry

    lax.fori_loop(0, count, step, 0)


def call(kernel, outs, scratch, *args, limit=8, work=0.0, settled=()):
    shapes = [jax.ShapeDtypeStruct(s, jnp.float32) for s in outs]
    vmem = pl.BlockSpec(memory_space=pltpu.VMEM)
    smem = pl.BlockSpec(memory_space=pltpu.SMEM)
    cost = pl.CostEstimate(flops=int(work * 1.0e9), bytes_accessed=int(work * 3.0e6), transcendentals=0) if work else None

    def body(*refs):
        kernel(*refs[len(settled):])

    return pl.pallas_call(
        body,
        out_shape=shapes,
        in_specs=[pl.BlockSpec(memory_space=pl.ANY)] * len(settled) + [smem if a.dtype == jnp.int32 and a.ndim == 1 else vmem for a in args],
        out_specs=[vmem] * len(shapes),
        scratch_shapes=[pltpu.VMEM(s, jnp.float32) for s in scratch],
        compiler_params=pltpu.CompilerParams(vmem_limit_bytes=limit * 1024 * 1024),
        cost_estimate=cost,
    )(*settled, *args)


ORDER = (3, 5, 4, 2, 6, 1, 7)


def ring_permuted(value, by):
    size = lax.axis_size("gz")
    return lax.ppermute(value, "gz", [(i, i // RING * RING + (i + by) % RING) for i in range(size)])


def after(value, *settled):
    def nothing(*refs):
        pass

    there = pl.BlockSpec(memory_space=pl.ANY)
    return pl.pallas_call(
        nothing,
        out_shape=jax.ShapeDtypeStruct(value.shape, value.dtype),
        in_specs=[there] * (1 + len(settled)),
        out_specs=there,
        compiler_params=pltpu.CompilerParams(vmem_limit_bytes=1024 * 1024),
        input_output_aliases={0: 0},
    )(value, *settled)


def cut_conduct(place, labels, fraction, top, bottom, *rest):
    outs, full = rest[:-1], rest[-1]
    planes, rows, _ = labels.shape
    strip = rows // RING
    for p in range(planes):
        full[p, :HALO] = top[p]
        full[p, HALO + rows:] = bottom[p]
        for k in range(RING):
            at = k * strip
            full[p, HALO + at:HALO + at + strip] = conductivity(labels[p, at:at + strip], fraction[p, at:at + strip])
        for k in range(RING):
            start = pl.multiple_of(((place[0] + k) % RING) * strip, strip)
            outs[k][p] = full[p, pl.ds(start, strip + 2 * HALO)]


def cut_source(source, top, bottom, out):
    planes, rows, _ = source.shape
    strip = rows // RING
    for p in range(planes):
        for k in range(RING):
            start = k * strip
            out[k, p, :THIN] = top[p, HALO - THIN:] if k == 0 else source[p, start - THIN:start]
            out[k, p, THIN:THIN + strip] = source[p, start:start + strip]
            out[k, p, THIN + strip:] = bottom[p, :THIN] if k == RING - 1 else source[p, start + strip:start + strip + THIN]


def join(place, *refs):
    out, low, high, ready = refs[RING:]
    ready[...] = refs[0][0, :HALO]
    for k, ref in zip((0,) + ORDER, refs):
        start = ((place[0] + RING - k) % RING) * 2
        out[start] = ref[0]
        out[start + 1] = ref[1]
    reach = low.shape[0]
    loop(reach, lambda p: low.__setitem__(p, out[p]))
    loop(reach, lambda p: high.__setitem__(p, out[p + 16 - reach]))


def plane_faces(c):
    last = lax.broadcasted_iota(jnp.int32, c.shape, 1) == c.shape[1] - 1
    return harmonic(c, next_row(c)), jnp.where(last, 0.0, harmonic(c, next_column(c)))


def parts(faces, count):
    east, north = faces.at[0:count], faces.at[count:2 * count]
    z, w = faces.at[2 * count:3 * count + 1], faces.at[3 * count + 1:4 * count + 1]
    return east, north, z, w, faces.at[4 * count + 1:] if count > 1 else None


def planes_of(count):
    return 4 * count + 1 + (0 if count == 1 else 10 if count == 16 else 8)


def make_faces(place, c, low, high, faces0, faces1, faces2, faces3, faces4, pack):
    east0, north0, z0, w0, halo0 = parts(faces0, 16)

    def z_face(p):
        z0[p] = harmonic(c[p - 1], c[p])

    loop(15, lambda k: z_face(k + 1))
    z0[0] = jnp.where(low[REACH - 1] > 0, harmonic(low[REACH - 1], c[0]), 2.0 * c[0])
    z0[16] = jnp.where(high[0] > 0, harmonic(c[15], high[0]), 2.0 * c[15])

    def weigh(p):
        east, north = plane_faces(c[p])
        east0[p] = east
        north0[p] = north
        w0[p] = weight(c[p], east, north, z0[p], z0[p + 1])

    loop(16, weigh)
    finer, count = faces0, 16
    for coarser in (faces1, faces2, faces3, faces4):
        east_f, north_f, z_f, _, _ = parts(finer, count)
        count //= 2
        east, north, z, w, _ = parts(coarser, count)

        def faces_and_weight(q):
            east_q = east_f[2 * q] + east_f[2 * q + 1]
            north_q = north_f[2 * q] + north_f[2 * q + 1]
            east[q] = east_q
            north[q] = north_q
            z[q] = z_f[2 * q]
            w[q] = weight(c[0], east_q, north_q, z_f[2 * q], z_f[2 * q + 2])

        loop(count, faces_and_weight)
        z[count] = z_f[2 * count]
        finer = coarser

    for side, ref, at, face in ((0, low, [REACH - 1 - k for k in range(REACH)], 0), (1, high, list(range(REACH)), 16)):
        shared = z0[face]
        near = ref[at[0]]
        middle = harmonic(near, ref[at[1]])
        east_sum, north_sum = plane_faces(near)
        halo0[side] = east_sum
        halo0[2 + side] = north_sum
        halo0[4 + side] = middle
        halo0[6 + side] = weight(near, east_sum, north_sum, shared, middle)
        thick = 1
        for faces, count in ((faces1, 8), (faces2, 4), (faces3, 2)):
            for k in range(thick, 2 * thick):
                east_k, north_k = plane_faces(ref[at[k]])
                if k == 1:
                    halo0[8 + side] = weight(ref[at[1]], east_k, north_k, middle, harmonic(ref[at[1]], ref[at[2]]))
                east_sum = east_sum + east_k
                north_sum = north_sum + north_k
            thick *= 2
            halo = parts(faces, count)[4]
            outer = harmonic(ref[at[thick - 1]], ref[at[thick]])
            halo[side] = east_sum
            halo[2 + side] = north_sum
            halo[4 + side] = outer
            halo[6 + side] = weight(near, east_sum, north_sum, shared, outer)
    pack[0] = faces4[0]
    pack[1] = faces4[1]
    pack[2] = jnp.where(place[1] == 0, faces4[2], faces4[3])


def make_last_faces(place, faces4, other, faces5):
    east4, north4, z4, w4, _ = parts(faces4, 1)
    lower = place[1] == 0
    east = east4[0] + other[0]
    north = north4[0] + other[1]
    down = jnp.where(lower, z4[0], other[2])
    up = jnp.where(lower, other[2], z4[1])
    for k, value in enumerate((east, north, down, up, weight(w4[0], east, north, down, up))):
        faces5[k] = value


def begin_last(rest4, other, faces5, s, first):
    s[0] = rest4[0] + other[0]
    first[0] = faces5[4] * s[0]
def sweep_and_rest(s, first, total, second, faces, count):
    east, north, z, w, halo = parts(faces, count)

    def sweep(q):
        t = 1.2 * s[q + 1] + neighbours(first[q + 2], first[q + 1], first[q + 3], east[q], north[q], z[q], z[q + 1])
        total[q] = t
        second[q + 1] = w[q] * t

    loop(count, sweep)
    for side, q, down, up in ((0, -1, halo[4], z[0]), (1, count, z[count], halo[5])):
        second[q + 1] = halo[6 + side] * (1.2 * s[q + 1] + neighbours(
            first[q + 2], first[q + 1], first[q + 3], halo[side], halo[2 + side], down, up))

    def rest(q):
        return s[q + 1] - damping * total[q] + neighbours(
            second[q + 1], second[q], second[q + 2], east[q], north[q], z[q], z[q + 1])

    return rest


def fine_level(s_own, s_low, s_high, faces, faces_next, fine, s_next, edge_down, edge_up, s, first, total, second):
    strip = fine.shape[2]
    columns = s.shape[2]
    _, _, _, w, halo = parts(faces, 16)
    w_next = parts(faces_next, 8)[3]
    blank = jnp.zeros((HALO - THIN, columns), jnp.float32)

    def place(k, value):
        s[k, :HALO - THIN] = blank
        s[k, HALO - THIN:HALO + strip + THIN] = value
        s[k, HALO + strip + THIN:] = blank

    place(0, s_low[0])
    first[0] = halo[8] * s[0]
    place(0, s_high[1])
    first[19] = halo[9] * s[0]
    place(0, s_low[1])
    first[1] = halo[6] * s[0]
    place(17, s_high[0])
    first[18] = halo[7] * s[17]

    def start(q):
        place(q + 1, s_own[q])
        first[q + 2] = w[q] * s[q + 1]

    loop(16, start)
    rest = sweep_and_rest(s, first, total, second, faces, 16)

    def pair(q):
        s_next[q] = rest(2 * q) + rest(2 * q + 1)
        fine[q, 0] = second[2 * q + 1, HALO:HALO + strip]
        fine[q, 1] = second[2 * q + 2, HALO:HALO + strip]

    loop(8, pair)
    edge_down[0] = s_next[0]
    edge_down[1] = w_next[1] * s_next[1]
    edge_up[0] = w_next[6] * s_next[6]
    edge_up[1] = s_next[7]


def open_level(s_own, faces, low, high, s, first):
    count = s_own.shape[0]
    _, _, _, w, halo = parts(faces, count)
    s[0] = low[1]
    s[count + 1] = high[0]
    first[0] = low[0]
    first[1] = halo[6] * low[1]
    first[count + 2] = halo[7] * high[0]
    first[count + 3] = high[1]

    def start(q):
        s[q + 1] = s_own[q]
        first[q + 2] = w[q] * s_own[q]

    loop(count, start)


def first_coarse_level(s_own, low, high, faces, out, s_next, top, bottom, s, first, total, second):
    strip = out.shape[1]
    open_level(s_own, faces, low, high, s, first)
    rest = sweep_and_rest(s, first, total, second, faces, s_own.shape[0])

    def pair(q):
        value = rest(2 * q) + rest(2 * q + 1)
        s_next[q] = value[HALO:HALO + strip]
        top[q] = value[HALO:2 * HALO]
        bottom[q] = value[strip:HALO + strip]
        out[2 * q] = second[2 * q + 1, HALO:HALO + strip]
        out[2 * q + 1] = second[2 * q + 2, HALO:HALO + strip]

    loop(4, pair)


def middle_level(s_own, low, high, faces, faces_next, out, s_next, *rest_refs):
    edges, (s, first, total, second) = rest_refs[:-4], rest_refs[-4:]
    count = s_own.shape[0]
    w_next = parts(faces_next, count // 2)[3]
    strip = out.shape[1]
    open_level(s_own, faces, low, high, s, first)
    rest = sweep_and_rest(s, first, total, second, faces, s_own.shape[0])
    for q in range(count // 2):
        s_next[q] = rest(2 * q) + rest(2 * q + 1)
    for q in range(count):
        out[q] = second[q + 1, HALO:HALO + strip]
    if len(edges) == 2:
        edge_down, edge_up = edges
        edge_down[0] = s_next[0]
        edge_down[1] = w_next[1] * s_next[1]
        edge_up[0] = w_next[count // 2 - 2] * s_next[count // 2 - 2]
        edge_up[1] = s_next[count // 2 - 1]
    else:
        edges[0][0] = w_next[0] * s_next[0]


def widen(source2, above, below, faces2, fine, plane_out, s, edge_down, edge_up, back):
    count, strip, _ = source2.shape
    w2 = parts(faces2, count)[3]
    for q in range(count):
        s[q, :HALO] = above[q]
        s[q, HALO:HALO + strip] = source2[q]
        s[q, HALO + strip:] = below[q]
    edge_down[0] = s[0]
    edge_down[1] = w2[1] * s[1]
    edge_up[0] = w2[count - 2] * s[count - 2]
    edge_up[1] = s[count - 1]

    def gather(k):
        back[k, 0] = fine[k, 0]
        back[k, 1] = fine[k, 1]
        back[k, 2] = plane_out[k]

    loop(RING, gather)


def sweep_last(s, first, low, high, faces, total, second):
    east, north, z, w, _ = parts(faces, 1)
    t = 1.2 * s[0] + neighbours(first[0], low[0], high[0], east[0], north[0], z[0], z[1])
    total[0] = t
    second[0] = w[0] * t


def rest_last(s, total, second, low, high, faces, out):
    east, north, z, _, _ = parts(faces, 1)
    out[0] = s[0] - damping * total[0] + neighbours(second[0], low[0], high[0], east[0], north[0], z[0], z[1])


def finish(s, first, low, high, faces5, second2, second3, second4, out):
    strip = out.shape[1]
    east, north, down, up, w = (faces5[k] for k in range(5))
    second5 = w * (1.2 * s[0] + neighbours(first[0], low[0], high[0], east, north, down, up))
    own = slice(HALO, HALO + strip)
    for k in range(RING):
        out[k] = ((second2[k // 2] + second3[k // 4]) + second4[0, own]) + second5[own]


def exchange(edge_low, edge_high, distance=RING):
    return shifted(edge_high, distance), shifted(edge_low, -distance)


def on_device(right_side, labels, fraction):
    planes, rows, columns = right_side.shape
    strip = rows // RING
    frame = strip + 2 * HALO
    at_core = lax.axis_index("xy")

    def edges_of(first_rows, last_rows):
        got = lax.ppermute(jnp.where(at_core == 0, last_rows, first_rows), "xy", [(0, 1), (1, 0)])
        return jnp.where(at_core == 1, got, 0.0), jnp.where(at_core == 0, got, 0.0)

    def shape(n):
        return (n, frame, columns)

    at_ring = lax.axis_index("gz")
    place = jnp.stack([at_ring % RING, at_ring // RING % 2]).astype(jnp.int32)
    c_top, c_bottom = edges_of(conductivity(labels[:, :HALO], fraction[:, :HALO]),
                               conductivity(labels[:, rows - HALO:], fraction[:, rows - HALO:]))
    cuts = call(cut_conduct, [(planes, frame, columns)] * RING, [(planes, rows + 2 * HALO, columns)],
                place, labels, fraction, c_top, c_bottom, limit=10)
    s_top, s_bottom = edges_of(right_side[:, :HALO], right_side[:, rows - HALO:])
    thin = strip + 2 * THIN
    (s_cut,) = call(cut_source, [(RING, planes, thin, columns)], [], right_side, s_top, s_bottom, limit=10)
    c_parts = [cuts[0]] + [ring_permuted(cuts[k], k) for k in ORDER]
    c, bundle_down, bundle_up, ready = call(join, [shape(16), shape(REACH), shape(REACH), (HALO, columns)], [], place, *c_parts, limit=10, settled=(s_cut,))
    s_own = transposed(after(s_cut, ready))
    c_low, c_high = exchange(bundle_down, bundle_up)
    faces0, faces1, faces2, faces3, faces4, pack = call(
        make_faces, [shape(planes_of(n)) for n in (16, 8, 4, 2, 1)] + [shape(3)], [], place, c, c_low, c_high, limit=28, work=12.0)
    (faces5,) = call(make_last_faces, [shape(5)], [], place, faces4, partner(pack))

    s_own = s_own.reshape(RING * planes, thin, columns)
    s_low, s_high = exchange(s_own[:2], s_own[-2:])
    fine, s1, edge_down, edge_up = call(
        fine_level, [(RING, planes, strip, columns), shape(8), shape(2), shape(2)],
        [shape(18), shape(20), shape(16), shape(18)],
        s_own, s_low, s_high, faces0, faces1, limit=30, work=8.0)

    low, high = exchange(edge_down, edge_up)
    plane_out, s2, top, bottom = call(
        first_coarse_level,
        [(8, strip, columns), (4, strip, columns), (4, HALO, columns), (4, HALO, columns)],
        [shape(10), shape(12), shape(8), shape(10)], s1, low, high, faces1, limit=15, work=4.0)

    above = row_shifted(bottom, 1)
    below = row_shifted(top, -1)
    s2, edge_down, edge_up, back = call(
        widen, [shape(4), shape(2), shape(2), (RING, planes + 1, strip, columns)], [], s2, above, below, faces2, fine, plane_out, limit=10)
    low, high = exchange(edge_down, edge_up)
    second2, s3, edge_down, edge_up = call(
        middle_level, [(4, strip, columns), shape(2), shape(2), shape(2)], [shape(6), shape(8), shape(4), shape(6)],
        s2, low, high, faces2, faces3, limit=10)
    low, high = exchange(edge_down, edge_up)
    second3, s4, first4 = call(
        middle_level, [(2, strip, columns), shape(1), shape(1)], [shape(4), shape(6), shape(2), shape(4)],
        s3, low, high, faces3, faces4)
    low, high = exchange(first4, first4)
    total4, second4 = call(sweep_last, [shape(1), shape(1)], [], s4, first4, low, high, faces4)
    low, high = exchange(second4, second4)
    (rest4,) = call(rest_last, [shape(1)], [], s4, total4, second4, low, high, faces4)
    s5, first5 = call(begin_last, [shape(1), shape(1)], [], rest4, partner(rest4), faces5)
    low, high = exchange(first5, first5, 2 * RING)
    back = transposed(back)
    (summed,) = call(finish, [(RING, strip, columns)], [],
                     s5, first5, low, high, faces5, second2, second3, second4, settled=(back,))

    fine_iterate = jnp.transpose(back[:, :planes], (1, 0, 2, 3)).reshape(planes, rows, columns)
    plane_iterate = back[:, planes].reshape(1, rows, columns)
    coarse_return = transposed(summed).reshape(1, rows, columns)
    return fine_iterate, plane_iterate, coarse_return


def solution(mesh):
    spec = P("gz", "xy", None)
    return jax.shard_map(
        on_device,
        mesh=mesh,
        in_specs=(spec, spec, spec),
        out_specs=(spec, spec, spec),
        check_vma=False,
    )
```

```python
from functools import partial

import jax
import jax.numpy as jnp
from jax import lax
from jax.experimental import pallas as pl
from jax.experimental.pallas import tpu as pltpu
from jax.sharding import PartitionSpec as P

RING = 8
HALO = 8
REACH = 9
THIN = 4
damping = 0.8
pore_value = 1.0
grain_value = 0.1
clay_value = 0.3
TINY = 1e-6


def ring_groups(count):
    return [[r * RING + k for k in range(RING)] for r in range(count // RING)]


def shifted(value, by):
    size = lax.axis_size("gz")
    pairs = [(i, i + by) for i in range(size) if 0 <= i + by < size]
    return lax.ppermute(value, "gz", pairs)


def row_shifted(value, by):
    pairs = []
    for ring in range(lax.axis_size("gz") // RING):
        for t in range(2 * RING):
            u = t + by
            if 0 <= u < 2 * RING:
                pairs.append(((ring * RING + t % RING) * 2 + t // RING, (ring * RING + u % RING) * 2 + u // RING))
    return lax.ppermute(value, ("gz", "xy"), pairs)


def partner(value):
    size = lax.axis_size("gz")
    return lax.ppermute(value, "gz", [(i, i + RING if (i // RING) % 2 == 0 else i - RING) for i in range(size)])


def transposed(value):
    return lax.all_to_all(value, "gz", 0, 0, axis_index_groups=ring_groups(lax.axis_size("gz")), tiled=True)


def conductivity(labels, fraction):
    return jnp.where(labels == 0, pore_value, jnp.where(labels == 1, grain_value, clay_value)) * fraction


def harmonic(one_side, other_side):
    return (2.0 * one_side * other_side) / jnp.maximum(one_side + other_side, TINY)


def next_row(v):
    return pltpu.roll(v, v.shape[0] - 1, 0)


def previous_row(v):
    return pltpu.roll(v, 1, 0)


def next_column(v):
    return pltpu.roll(v, v.shape[1] - 1, 1)


def previous_column(v):
    return pltpu.roll(v, 1, 1)


def neighbours(v, below, above, east, north, down, up):
    return (
        east * next_row(v)
        + previous_row(east * v)
        + north * next_column(v)
        + previous_column(north * v)
        + down * below
        + up * above
    )


def weight(c, east, north, down, up):
    diagonal = east + previous_row(east) + north + previous_column(north) + down + up
    return jnp.where(c > 0, damping / jnp.where(c > 0, diagonal, 1.0), 0.0)


def loop(count, body):
    def step(k, carry):
        body(k)
        return carry

    lax.fori_loop(0, count, step, 0)


def call(kernel, outs, scratch, *args, limit=8, work=0.0, settled=(), hbm_in=(), hbm_out=(), copies=0):
    shapes = [(pltpu.HBM if i in hbm_out else jax.ShapeDtypeStruct)(s, jnp.float32) for i, s in enumerate(outs)]
    vmem = pl.BlockSpec(memory_space=pltpu.VMEM)
    smem = pl.BlockSpec(memory_space=pltpu.SMEM)
    hbm = pl.BlockSpec(memory_space=pltpu.HBM)
    kinds = [hbm if i in hbm_in else smem if a.dtype == jnp.int32 and a.ndim == 1 else vmem for i, a in enumerate(args)]
    cost = pl.CostEstimate(flops=int(work * 1.0e9), bytes_accessed=int(work * 3.0e6), transcendentals=0) if work else None

    def body(*refs):
        kernel(*refs[len(settled):])

    args = [pltpu.with_memory_space_constraint(a, pltpu.HBM) if i in hbm_in else a for i, a in enumerate(args)]

    return pl.pallas_call(
        body,
        out_shape=shapes,
        in_specs=[pl.BlockSpec(memory_space=pl.ANY)] * len(settled) + kinds,
        out_specs=[hbm if i in hbm_out else vmem for i in range(len(shapes))],
        scratch_shapes=[pltpu.VMEM(s, jnp.float32) for s in scratch] + ([pltpu.SemaphoreType.DMA((copies,))] if copies else []),
        compiler_params=pltpu.CompilerParams(vmem_limit_bytes=limit * 1024 * 1024),
        cost_estimate=cost,
    )(*settled, *args)


ORDER = (3, 5, 4, 2, 6, 1, 7)


def ring_permuted(value, by):
    size = lax.axis_size("gz")
    return lax.ppermute(value, "gz", [(i, i // RING * RING + (i + by) % RING) for i in range(size)])


def after(value, *settled):
    def nothing(*refs):
        pass

    there = pl.BlockSpec(memory_space=pl.ANY)
    return pl.pallas_call(
        nothing,
        out_shape=jax.ShapeDtypeStruct(value.shape, value.dtype),
        in_specs=[there] * (1 + len(settled)),
        out_specs=there,
        compiler_params=pltpu.CompilerParams(vmem_limit_bytes=1024 * 1024),
        input_output_aliases={0: 0},
    )(value, *settled)


class Copies:
    def __init__(self, semaphores):
        self.semaphores, self.started = semaphores, []

    def start(self, source, target):
        copy = pltpu.make_async_copy(source, target, self.semaphores.at[len(self.started)])
        copy.start()
        self.started.append(copy)
        return copy


def cut_conduct(place, labels, fraction, top, bottom, *rest):
    outs, full = rest[:-1], rest[-1]
    planes, rows, _ = labels.shape
    strip = rows // RING
    for p in range(planes):
        full[p, :HALO] = top[p]
        full[p, HALO + rows:] = bottom[p]
        for k in range(RING):
            at = k * strip
            full[p, HALO + at:HALO + at + strip] = conductivity(labels[p, at:at + strip], fraction[p, at:at + strip])
        for k in range(RING):
            start = pl.multiple_of(((place[0] + k) % RING) * strip, strip)
            outs[k][p] = full[p, pl.ds(start, strip + 2 * HALO)]


def cut_source(source, top, bottom, out):
    planes, rows, _ = source.shape
    strip = rows // RING
    for p in range(planes):
        for k in range(RING):
            start = k * strip
            out[k, p, :THIN] = top[p, HALO - THIN:] if k == 0 else source[p, start - THIN:start]
            out[k, p, THIN:THIN + strip] = source[p, start:start + strip]
            out[k, p, THIN + strip:] = bottom[p, :THIN] if k == RING - 1 else source[p, start + strip:start + strip + THIN]


def join(place, *refs):
    out, low, high, ready = refs[RING:]
    ready[...] = refs[0][0, :HALO]
    for k, ref in zip((0,) + ORDER, refs):
        start = ((place[0] + RING - k) % RING) * 2
        out[start] = ref[0]
        out[start + 1] = ref[1]
    reach = low.shape[0]
    loop(reach, lambda p: low.__setitem__(p, out[p]))
    loop(reach, lambda p: high.__setitem__(p, out[p + 16 - reach]))


def plane_faces(c):
    last = lax.broadcasted_iota(jnp.int32, c.shape, 1) == c.shape[1] - 1
    return harmonic(c, next_row(c)), jnp.where(last, 0.0, harmonic(c, next_column(c)))


def parts(faces, count):
    east, north = faces.at[0:count], faces.at[count:2 * count]
    z, w = faces.at[2 * count:3 * count + 1], faces.at[3 * count + 1:4 * count + 1]
    return east, north, z, w, faces.at[4 * count + 1:] if count > 1 else None


def planes_of(count):
    return 4 * count + 1 + (0 if count == 1 else 10 if count == 16 else 8)


def make_faces(place, c, low, high, out0, out1, out2, out3, out4, pack, ready, faces0, faces1, faces2, faces3, faces4, semaphores):
    east0, north0, z0, w0, halo0 = parts(faces0, 16)

    def z_face(p):
        z0[p] = harmonic(c[p - 1], c[p])

    loop(15, lambda k: z_face(k + 1))
    z0[0] = jnp.where(low[REACH - 1] > 0, harmonic(low[REACH - 1], c[0]), 2.0 * c[0])
    z0[16] = jnp.where(high[0] > 0, harmonic(c[15], high[0]), 2.0 * c[15])

    def weigh(p):
        east, north = plane_faces(c[p])
        east0[p] = east
        north0[p] = north
        w0[p] = weight(c[p], east, north, z0[p], z0[p + 1])

    copies = Copies(semaphores)
    loop(16, weigh)
    copies.start(faces0.at[0:65], out0.at[0:65])
    finer, count = faces0, 16
    for coarser in (faces1, faces2, faces3, faces4):
        east_f, north_f, z_f, _, _ = parts(finer, count)
        count //= 2
        east, north, z, w, _ = parts(coarser, count)

        def faces_and_weight(q):
            east_q = east_f[2 * q] + east_f[2 * q + 1]
            north_q = north_f[2 * q] + north_f[2 * q + 1]
            east[q] = east_q
            north[q] = north_q
            z[q] = z_f[2 * q]
            w[q] = weight(c[0], east_q, north_q, z_f[2 * q], z_f[2 * q + 2])

        loop(count, faces_and_weight)
        z[count] = z_f[2 * count]
        finer = coarser
    copies.start(faces1.at[0:33], out1.at[0:33])
    copies.start(faces2.at[0:17], out2.at[0:17])
    copies.start(faces3.at[0:9], out3.at[0:9])
    copies.start(faces4, out4)

    for side, ref, at, face in ((0, low, [REACH - 1 - k for k in range(REACH)], 0), (1, high, list(range(REACH)), 16)):
        shared = z0[face]
        near = ref[at[0]]
        middle = harmonic(near, ref[at[1]])
        east_sum, north_sum = plane_faces(near)
        halo0[side] = east_sum
        halo0[2 + side] = north_sum
        halo0[4 + side] = middle
        halo0[6 + side] = weight(near, east_sum, north_sum, shared, middle)
        thick = 1
        for faces, count in ((faces1, 8), (faces2, 4), (faces3, 2)):
            for k in range(thick, 2 * thick):
                east_k, north_k = plane_faces(ref[at[k]])
                if k == 1:
                    halo0[8 + side] = weight(ref[at[1]], east_k, north_k, middle, harmonic(ref[at[1]], ref[at[2]]))
                east_sum = east_sum + east_k
                north_sum = north_sum + north_k
            thick *= 2
            halo = parts(faces, count)[4]
            outer = harmonic(ref[at[thick - 1]], ref[at[thick]])
            halo[side] = east_sum
            halo[2 + side] = north_sum
            halo[4 + side] = outer
            halo[6 + side] = weight(near, east_sum, north_sum, shared, outer)
    copies.start(faces0.at[65:75], out0.at[65:75])
    copies.start(faces1.at[33:41], out1.at[33:41])
    copies.start(faces2.at[17:25], out2.at[17:25])
    copies.start(faces3.at[9:17], out3.at[9:17])
    ready[...] = faces4[0, :HALO]
    pack[0] = faces4[0]
    pack[1] = faces4[1]
    pack[2] = jnp.where(place[1] == 0, faces4[2], faces4[3])
    for copy in copies.started:
        copy.wait()


def make_last_faces(place, faces4, other, faces5):
    east4, north4, z4, w4, _ = parts(faces4, 1)
    lower = place[1] == 0
    east = east4[0] + other[0]
    north = north4[0] + other[1]
    down = jnp.where(lower, z4[0], other[2])
    up = jnp.where(lower, other[2], z4[1])
    for k, value in enumerate((east, north, down, up, weight(w4[0], east, north, down, up))):
        faces5[k] = value


def begin_last(rest4, other, faces5, s, first):
    s[0] = rest4[0] + other[0]
    first[0] = faces5[4] * s[0]
def sweep_and_rest(s, first, total, second, faces, count, groups=()):
    east, north, z, w, halo = parts(faces, count)

    def sweep(q):
        t = 1.2 * s[q + 1] + neighbours(first[q + 2], first[q + 1], first[q + 3], east[q], north[q], z[q], z[q + 1])
        total[q] = t
        second[q + 1] = w[q] * t

    if groups:
        each = count // len(groups)
        for k, group in enumerate(groups):
            for copy in group:
                copy.wait()
            loop(each, lambda q: sweep(q + k * each))
    else:
        loop(count, sweep)
    for side, q, down, up in ((0, -1, halo[4], z[0]), (1, count, z[count], halo[5])):
        second[q + 1] = halo[6 + side] * (1.2 * s[q + 1] + neighbours(
            first[q + 2], first[q + 1], first[q + 3], halo[side], halo[2 + side], down, up))

    def rest(q):
        return s[q + 1] - damping * total[q] + neighbours(
            second[q + 1], second[q], second[q + 2], east[q], north[q], z[q], z[q + 1])

    return rest


def fine_level(s_own, s_low, s_high, there, there_next, fine, s_next, edge_down, edge_up, s, first, total, second, faces, w_next, semaphores):
    strip = fine.shape[2]
    columns = s.shape[2]
    _, _, _, w, halo = parts(faces, 16)
    copies = Copies(semaphores)
    weights = copies.start(there.at[49:75], faces.at[49:75])
    groups = []
    for k in range(4):
        spans = ((4 * k, 4), (16 + 4 * k, 4), (32, 5) if k == 0 else (33 + 4 * k, 4))
        groups.append([copies.start(there.at[a:a + n], faces.at[a:a + n]) for a, n in spans])
    later = copies.start(there_next.at[25:33], w_next)
    blank = jnp.zeros((HALO - THIN, columns), jnp.float32)

    def place(k, value):
        s[k, :HALO - THIN] = blank
        s[k, HALO - THIN:HALO + strip + THIN] = value
        s[k, HALO + strip + THIN:] = blank

    loop(16, lambda q: place(q + 1, s_own[q]))
    weights.wait()
    place(0, s_low[0])
    first[0] = halo[8] * s[0]
    place(0, s_high[1])
    first[19] = halo[9] * s[0]
    place(0, s_low[1])
    first[1] = halo[6] * s[0]
    place(17, s_high[0])
    first[18] = halo[7] * s[17]

    def start(q):
        first[q + 2] = w[q] * s[q + 1]

    loop(16, start)
    rest = sweep_and_rest(s, first, total, second, faces, 16, groups)

    def pair(q):
        s_next[q] = rest(2 * q) + rest(2 * q + 1)
        fine[q, 0] = second[2 * q + 1, HALO:HALO + strip]
        fine[q, 1] = second[2 * q + 2, HALO:HALO + strip]

    loop(8, pair)
    later.wait()
    edge_down[0] = s_next[0]
    edge_down[1] = w_next[1] * s_next[1]
    edge_up[0] = w_next[6] * s_next[6]
    edge_up[1] = s_next[7]


def open_level(s_own, faces, low, high, s, first):
    count = s_own.shape[0]
    _, _, _, w, halo = parts(faces, count)
    s[0] = low[1]
    s[count + 1] = high[0]
    first[0] = low[0]
    first[1] = halo[6] * low[1]
    first[count + 2] = halo[7] * high[0]
    first[count + 3] = high[1]

    def start(q):
        s[q + 1] = s_own[q]
        first[q + 2] = w[q] * s_own[q]

    loop(count, start)


def first_coarse_level(s_own, low, high, faces, out, s_next, top, bottom, s, first, total, second):
    strip = out.shape[1]
    open_level(s_own, faces, low, high, s, first)
    rest = sweep_and_rest(s, first, total, second, faces, s_own.shape[0])

    def pair(q):
        value = rest(2 * q) + rest(2 * q + 1)
        s_next[q] = value[HALO:HALO + strip]
        top[q] = value[HALO:2 * HALO]
        bottom[q] = value[strip:HALO + strip]
        out[2 * q] = second[2 * q + 1, HALO:HALO + strip]
        out[2 * q + 1] = second[2 * q + 2, HALO:HALO + strip]

    loop(4, pair)


def middle_level(s_own, low, high, there, there_next, out, s_next, *rest_refs):
    edges, (s, first, total, second, faces, w_next, semaphores) = rest_refs[:-7], rest_refs[-7:]
    count = s_own.shape[0]
    strip = out.shape[1]
    copies = Copies(semaphores)
    at, size = 3 * count + 1, planes_of(count)
    weights = copies.start(there.at[at:size], faces.at[at:size])
    others = copies.start(there.at[0:at], faces.at[0:at])
    at, size = 3 * (count // 2) + 1, 4 * (count // 2) + 1
    later = copies.start(there_next.at[at:size], w_next)
    weights.wait()
    open_level(s_own, faces, low, high, s, first)
    others.wait()
    rest = sweep_and_rest(s, first, total, second, faces, s_own.shape[0])
    for q in range(count // 2):
        s_next[q] = rest(2 * q) + rest(2 * q + 1)
    later.wait()
    for q in range(count):
        out[q] = second[q + 1, HALO:HALO + strip]
    if len(edges) == 2:
        edge_down, edge_up = edges
        edge_down[0] = s_next[0]
        edge_down[1] = w_next[1] * s_next[1]
        edge_up[0] = w_next[count // 2 - 2] * s_next[count // 2 - 2]
        edge_up[1] = s_next[count // 2 - 1]
    else:
        edges[0][0] = w_next[0] * s_next[0]


def widen(source2, above, below, faces2, fine, plane_out, s, edge_down, edge_up, back, semaphores):
    copies = Copies(semaphores)
    copies.start(fine, back.at[:, 0:2])
    copies.start(plane_out, back.at[:, 2])
    count, strip, _ = source2.shape
    w2 = parts(faces2, count)[3]
    for q in range(count):
        s[q, :HALO] = above[q]
        s[q, HALO:HALO + strip] = source2[q]
        s[q, HALO + strip:] = below[q]
    edge_down[0] = s[0]
    edge_down[1] = w2[1] * s[1]
    edge_up[0] = w2[count - 2] * s[count - 2]
    edge_up[1] = s[count - 1]

    for copy in copies.started:
        copy.wait()


def sweep_last(s, first, low, high, faces, total, second):
    east, north, z, w, _ = parts(faces, 1)
    t = 1.2 * s[0] + neighbours(first[0], low[0], high[0], east[0], north[0], z[0], z[1])
    total[0] = t
    second[0] = w[0] * t


def rest_last(s, total, second, low, high, faces, out):
    east, north, z, _, _ = parts(faces, 1)
    out[0] = s[0] - damping * total[0] + neighbours(second[0], low[0], high[0], east[0], north[0], z[0], z[1])


def finish(place, s, first, low, high, faces5, second2, second3, second4, *outs):
    own = slice(HALO, HALO + outs[0].shape[0])
    east, north, down, up, w = (faces5[k] for k in range(5))
    second5 = (w * (1.2 * s[0] + neighbours(first[0], low[0], high[0], east, north, down, up)))[own]
    for k in range(RING):
        at = (place[0] + k) % RING
        outs[k][...] = ((second2[at // 2] + second3[at // 4]) + second4[0, own]) + second5


def collect(place, *refs):
    out = refs[RING]
    for k, ref in zip((0,) + ORDER, refs):
        out[(place[0] + RING - k) % RING] = ref[...]


def exchange(edge_low, edge_high, distance=RING):
    return shifted(edge_high, distance), shifted(edge_low, -distance)


def on_device(right_side, labels, fraction):
    planes, rows, columns = right_side.shape
    strip = rows // RING
    frame = strip + 2 * HALO
    at_core = lax.axis_index("xy")

    def edges_of(first_rows, last_rows):
        got = lax.ppermute(jnp.where(at_core == 0, last_rows, first_rows), "xy", [(0, 1), (1, 0)])
        return jnp.where(at_core == 1, got, 0.0), jnp.where(at_core == 0, got, 0.0)

    def shape(n):
        return (n, frame, columns)

    at_ring = lax.axis_index("gz")
    place = jnp.stack([at_ring % RING, at_ring // RING % 2]).astype(jnp.int32)
    c_top, c_bottom = edges_of(conductivity(labels[:, :HALO], fraction[:, :HALO]),
                               conductivity(labels[:, rows - HALO:], fraction[:, rows - HALO:]))
    cuts = call(cut_conduct, [(planes, frame, columns)] * RING, [(planes, rows + 2 * HALO, columns)],
                place, labels, fraction, c_top, c_bottom, limit=10)
    s_top, s_bottom = edges_of(right_side[:, :HALO], right_side[:, rows - HALO:])
    thin = strip + 2 * THIN
    (s_cut,) = call(cut_source, [(RING, planes, thin, columns)], [], right_side, s_top, s_bottom, limit=10)
    c_parts = [cuts[0]] + [ring_permuted(cuts[k], k) for k in ORDER]
    c, bundle_down, bundle_up, ready = call(join, [shape(16), shape(REACH), shape(REACH), (HALO, columns)], [], place, *c_parts, limit=10, settled=(s_cut,))
    s_own = transposed(after(s_cut, ready))
    c_low, c_high = exchange(bundle_down, bundle_up)
    sizes = [shape(planes_of(n)) for n in (16, 8, 4, 2, 1)]
    faces0, faces1, faces2, faces3, faces4, pack, ready = call(
        make_faces, sizes + [shape(3), (HALO, columns)], sizes, place, c, c_low, c_high,
        limit=30, work=12.0, hbm_out=range(5), copies=9)
    (faces5,) = call(make_last_faces, [shape(5)], [], place, faces4, partner(pack))

    s_own = after(s_own, ready).reshape(RING * planes, thin, columns)
    s_low, s_high = exchange(s_own[:2], s_own[-2:])
    fine, s1, edge_down, edge_up = call(
        fine_level, [(RING, planes, strip, columns), shape(8), shape(2), shape(2)],
        [shape(18), shape(20), shape(16), shape(18), shape(75), shape(8)],
        s_own, s_low, s_high, faces0, faces1, limit=28, work=8.0, hbm_in=(3, 4), copies=14)

    low, high = exchange(edge_down, edge_up)
    plane_out, s2, top, bottom = call(
        first_coarse_level,
        [(8, strip, columns), (4, strip, columns), (4, HALO, columns), (4, HALO, columns)],
        [shape(10), shape(12), shape(8), shape(10)], s1, low, high, faces1, limit=15, work=4.0)

    above = row_shifted(bottom, 1)
    below = row_shifted(top, -1)
    s2, edge_down, edge_up, back = call(
        widen, [shape(4), shape(2), shape(2), (RING, planes + 1, strip, columns)], [], s2, above, below, faces2, fine, plane_out, limit=10,
        hbm_out=(3,), copies=2)
    low, high = exchange(edge_down, edge_up)
    second2, s3, edge_down, edge_up = call(
        middle_level, [(4, strip, columns), shape(2), shape(2), shape(2)],
        [shape(6), shape(8), shape(4), shape(6), shape(planes_of(4)), shape(2)],
        s2, low, high, faces2, faces3, limit=14, hbm_in=(3, 4), copies=3)
    low, high = exchange(edge_down, edge_up)
    second3, s4, first4 = call(
        middle_level, [(2, strip, columns), shape(1), shape(1)],
        [shape(4), shape(6), shape(2), shape(4), shape(planes_of(2)), shape(1)],
        s3, low, high, faces3, faces4, limit=12, hbm_in=(3, 4), copies=3)
    low, high = exchange(first4, first4)
    total4, second4 = call(sweep_last, [shape(1), shape(1)], [], s4, first4, low, high, faces4)
    low, high = exchange(second4, second4)
    (rest4,) = call(rest_last, [shape(1)], [], s4, total4, second4, low, high, faces4)
    s5, first5 = call(begin_last, [shape(1), shape(1)], [], rest4, partner(rest4), faces5)
    low, high = exchange(first5, first5, 2 * RING)
    back = transposed(back)
    sums = call(finish, [(strip, columns)] * RING, [],
                place, s5, first5, low, high, faces5, second2, second3, second4, settled=(back,))
    (coarse_return,) = call(collect, [(RING, strip, columns)], [], place, sums[0], *[ring_permuted(sums[k], k) for k in ORDER])

    fine_iterate = jnp.transpose(back[:, :planes], (1, 0, 2, 3)).reshape(planes, rows, columns)
    plane_iterate = back[:, planes].reshape(1, rows, columns)
    return fine_iterate, plane_iterate, coarse_return.reshape(1, rows, columns)


def solution(mesh):
    spec = P("gz", "xy", None)
    return jax.shard_map(
        on_device,
        mesh=mesh,
        in_specs=(spec, spec, spec),
        out_specs=(spec, spec, spec),
        check_vma=False,
    )
```

```python
from functools import partial

import jax
import jax.numpy as jnp
from jax import lax
from jax.experimental import pallas as pl
from jax.experimental.pallas import tpu as pltpu
from jax.sharding import PartitionSpec as P

RING = 8
HALO = 8
NEAR, FAR = 3, 6
THIN = 4
damping = 0.8
pore_value = 1.0
grain_value = 0.1
clay_value = 0.3
TINY = 1e-6


def ring_groups(count):
    return [[r * RING + k for k in range(RING)] for r in range(count // RING)]


def shifted(value, by):
    size = lax.axis_size("gz")
    pairs = [(i, i + by) for i in range(size) if 0 <= i + by < size]
    return lax.ppermute(value, "gz", pairs)


def row_shifted(value, by):
    pairs = []
    for ring in range(lax.axis_size("gz") // RING):
        for t in range(2 * RING):
            u = t + by
            if 0 <= u < 2 * RING:
                pairs.append(((ring * RING + t % RING) * 2 + t // RING, (ring * RING + u % RING) * 2 + u // RING))
    return lax.ppermute(value, ("gz", "xy"), pairs)


def partner(value):
    size = lax.axis_size("gz")
    return lax.ppermute(value, "gz", [(i, i + RING if (i // RING) % 2 == 0 else i - RING) for i in range(size)])


def transposed(value):
    return lax.all_to_all(value, "gz", 0, 0, axis_index_groups=ring_groups(lax.axis_size("gz")), tiled=True)


def conductivity(labels, fraction):
    return jnp.where(labels == 0, pore_value, jnp.where(labels == 1, grain_value, clay_value)) * fraction


def harmonic(one_side, other_side):
    return (2.0 * one_side * other_side) / jnp.maximum(one_side + other_side, TINY)


def next_row(v):
    return pltpu.roll(v, v.shape[0] - 1, 0)


def previous_row(v):
    return pltpu.roll(v, 1, 0)


def next_column(v):
    return pltpu.roll(v, v.shape[1] - 1, 1)


def previous_column(v):
    return pltpu.roll(v, 1, 1)


def neighbours(v, below, above, east, north, down, up):
    return (
        east * next_row(v)
        + previous_row(east * v)
        + north * next_column(v)
        + previous_column(north * v)
        + down * below
        + up * above
    )


def weight(c, east, north, down, up):
    diagonal = east + previous_row(east) + north + previous_column(north) + down + up
    return jnp.where(c > 0, damping / jnp.where(c > 0, diagonal, 1.0), 0.0)


def loop(count, body):
    def step(k, carry):
        body(k)
        return carry

    lax.fori_loop(0, count, step, 0)


def call(kernel, outs, scratch, *args, limit=8, work=0.0, settled=(), hbm_in=(), hbm_out=(), copies=0):
    shapes = [(pltpu.HBM if i in hbm_out else jax.ShapeDtypeStruct)(s, jnp.float32) for i, s in enumerate(outs)]
    vmem = pl.BlockSpec(memory_space=pltpu.VMEM)
    smem = pl.BlockSpec(memory_space=pltpu.SMEM)
    hbm = pl.BlockSpec(memory_space=pltpu.HBM)
    kinds = [hbm if i in hbm_in else smem if a.dtype == jnp.int32 and a.ndim == 1 else vmem for i, a in enumerate(args)]
    cost = pl.CostEstimate(flops=int(work * 1.0e9), bytes_accessed=int(work * 3.0e6), transcendentals=0) if work else None

    def body(*refs):
        kernel(*refs[len(settled):])

    args = [pltpu.with_memory_space_constraint(a, pltpu.HBM) if i in hbm_in else a for i, a in enumerate(args)]

    return pl.pallas_call(
        body,
        out_shape=shapes,
        in_specs=[pl.BlockSpec(memory_space=pl.ANY)] * len(settled) + kinds,
        out_specs=[hbm if i in hbm_out else vmem for i in range(len(shapes))],
        scratch_shapes=[pltpu.VMEM(s, jnp.float32) for s in scratch] + ([pltpu.SemaphoreType.DMA((copies,))] if copies else []),
        compiler_params=pltpu.CompilerParams(vmem_limit_bytes=limit * 1024 * 1024),
        cost_estimate=cost,
    )(*settled, *args)


ORDER = (3, 5, 4, 2, 6, 1, 7)


def ring_permuted(value, by):
    size = lax.axis_size("gz")
    return lax.ppermute(value, "gz", [(i, i // RING * RING + (i + by) % RING) for i in range(size)])


def after(value, *settled):
    def nothing(*refs):
        pass

    there = pl.BlockSpec(memory_space=pl.ANY)
    return pl.pallas_call(
        nothing,
        out_shape=jax.ShapeDtypeStruct(value.shape, value.dtype),
        in_specs=[there] * (1 + len(settled)),
        out_specs=there,
        compiler_params=pltpu.CompilerParams(vmem_limit_bytes=1024 * 1024),
        input_output_aliases={0: 0},
    )(value, *settled)


class Copies:
    def __init__(self, semaphores):
        self.semaphores, self.started = semaphores, []

    def start(self, source, target):
        copy = pltpu.make_async_copy(source, target, self.semaphores.at[len(self.started)])
        copy.start()
        self.started.append(copy)
        return copy


def cut_conduct(place, labels, fraction, top, bottom, *rest):
    outs, full = rest[:-1], rest[-1]
    planes, rows, _ = labels.shape
    strip = rows // RING
    for p in range(planes):
        full[p, :HALO] = top[p]
        full[p, HALO + rows:] = bottom[p]
        for k in range(RING):
            at = k * strip
            full[p, HALO + at:HALO + at + strip] = conductivity(labels[p, at:at + strip], fraction[p, at:at + strip])
        for k in range(RING):
            start = pl.multiple_of(((place[0] + k) % RING) * strip, strip)
            outs[k][p] = full[p, pl.ds(start, strip + 2 * HALO)]


def cut_source(source, top, bottom, out):
    planes, rows, _ = source.shape
    strip = rows // RING
    for p in range(planes):
        for k in range(RING):
            start = k * strip
            out[k, p, :THIN] = top[p, HALO - THIN:] if k == 0 else source[p, start - THIN:start]
            out[k, p, THIN:THIN + strip] = source[p, start:start + strip]
            out[k, p, THIN + strip:] = bottom[p, :THIN] if k == RING - 1 else source[p, start + strip:start + strip + THIN]


def join(place, *refs):
    c, near_low, near_high, far_low, far_high, ready, out, semaphores = refs[RING:]
    ready[...] = refs[0][0, :HALO]
    for k, ref in zip((0,) + ORDER, refs):
        start = ((place[0] + RING - k) % RING) * 2
        out[start] = ref[0]
        out[start + 1] = ref[1]
    copies = Copies(semaphores)
    for ref, first in ((near_low, 0), (near_high, 16 - NEAR), (far_low, NEAR), (far_high, 16 - NEAR - FAR), (c, 0)):
        copies.start(out.at[first:first + ref.shape[0]], ref)
    for copy in copies.started:
        copy.wait()


def plane_faces(c):
    last = lax.broadcasted_iota(jnp.int32, c.shape, 1) == c.shape[1] - 1
    return harmonic(c, next_row(c)), jnp.where(last, 0.0, harmonic(c, next_column(c)))


def parts(faces, count):
    east, north = faces.at[0:count], faces.at[count:2 * count]
    z, w = faces.at[2 * count:3 * count + 1], faces.at[3 * count + 1:4 * count + 1]
    return east, north, z, w, faces.at[4 * count + 1:] if faces.shape[0] > 4 * count + 1 else None


def planes_of(count):
    return 4 * count + 1 + (0 if count == 1 else 10 if count == 16 else 8)


def own_planes_of(count):
    return planes_of(count) if count > 4 else 4 * count + 1


def make_faces(place, c, low, high, out0, out1, out2, out3, out4, pack, edge, faces0, faces1, faces2, faces3, faces4, semaphores):
    east0, north0, z0, w0, halo0 = parts(faces0, 16)

    def z_face(p):
        z0[p] = harmonic(c[p - 1], c[p])

    loop(15, lambda k: z_face(k + 1))
    z0[0] = jnp.where(low[NEAR - 1] > 0, harmonic(low[NEAR - 1], c[0]), 2.0 * c[0])
    z0[16] = jnp.where(high[0] > 0, harmonic(c[15], high[0]), 2.0 * c[15])

    def weigh(p):
        east, north = plane_faces(c[p])
        east0[p] = east
        north0[p] = north
        w0[p] = weight(c[p], east, north, z0[p], z0[p + 1])

    copies = Copies(semaphores)
    loop(16, weigh)
    copies.start(faces0.at[0:65], out0.at[0:65])
    finer, count = faces0, 16
    for coarser in (faces1, faces2, faces3, faces4):
        east_f, north_f, z_f, _, _ = parts(finer, count)
        count //= 2
        east, north, z, w, _ = parts(coarser, count)

        def faces_and_weight(q):
            east_q = east_f[2 * q] + east_f[2 * q + 1]
            north_q = north_f[2 * q] + north_f[2 * q + 1]
            east[q] = east_q
            north[q] = north_q
            z[q] = z_f[2 * q]
            w[q] = weight(c[0], east_q, north_q, z_f[2 * q], z_f[2 * q + 2])

        loop(count, faces_and_weight)
        z[count] = z_f[2 * count]
        finer = coarser
    copies.start(faces1.at[0:33], out1.at[0:33])
    copies.start(faces2.at[0:17], out2.at[0:17])
    copies.start(faces3.at[0:9], out3.at[0:9])
    copies.start(faces4, out4)

    for side, ref, at, face in ((0, low, (2, 1, 0), 0), (1, high, (0, 1, 2), 16)):
        shared = z0[face]
        near, after_near, third = (ref[k] for k in at)
        middle = harmonic(near, after_near)
        outer = harmonic(after_near, third)
        east_near, north_near = plane_faces(near)
        east_next, north_next = plane_faces(after_near)
        east_sum, north_sum = east_near + east_next, north_near + north_next
        halo0[side] = east_near
        halo0[2 + side] = north_near
        halo0[4 + side] = middle
        halo0[6 + side] = weight(near, east_near, north_near, shared, middle)
        halo0[8 + side] = weight(after_near, east_next, north_next, middle, outer)
        halo1 = parts(faces1, 8)[4]
        halo1[side] = east_sum
        halo1[2 + side] = north_sum
        halo1[4 + side] = outer
        halo1[6 + side] = weight(near, east_sum, north_sum, shared, outer)
        edge[side] = east_sum
        edge[2 + side] = north_sum
        edge[4 + side] = shared
    copies.start(faces0.at[65:75], out0.at[65:75])
    copies.start(faces1.at[33:41], out1.at[33:41])
    pack[0] = faces4[0]
    pack[1] = faces4[1]
    pack[2] = jnp.where(place[1] == 0, faces4[2], faces4[3])
    for copy in copies.started:
        copy.wait()


def make_far_halos(edge, low, high, far_low, far_high, out2, out3, ready, halo2, halo3, semaphores):
    for side in range(2):
        def at(k):
            if side == 0:
                return low[NEAR - 1 - k] if k < NEAR else far_low[NEAR + FAR - 1 - k]
            return high[k] if k < NEAR else far_high[k - NEAR]

        near, east_sum, north_sum, shared = at(0), edge[side], edge[2 + side], edge[4 + side]
        for halo, thick in ((halo2, 4), (halo3, 8)):
            for k in range(thick // 2, thick):
                east, north = plane_faces(at(k))
                east_sum = east_sum + east
                north_sum = north_sum + north
            outer = harmonic(at(thick - 1), at(thick))
            halo[side] = east_sum
            halo[2 + side] = north_sum
            halo[4 + side] = outer
            halo[6 + side] = weight(near, east_sum, north_sum, shared, outer)
    copies = Copies(semaphores)
    copies.start(halo2, out2)
    copies.start(halo3, out3)
    ready[...] = edge[0, :HALO]
    for copy in copies.started:
        copy.wait()


def make_last_faces(place, faces4, other, faces5):
    east4, north4, z4, w4, _ = parts(faces4, 1)
    lower = place[1] == 0
    east = east4[0] + other[0]
    north = north4[0] + other[1]
    down = jnp.where(lower, z4[0], other[2])
    up = jnp.where(lower, other[2], z4[1])
    for k, value in enumerate((east, north, down, up, weight(w4[0], east, north, down, up))):
        faces5[k] = value


def begin_last(rest4, other, faces5, s, first):
    s[0] = rest4[0] + other[0]
    first[0] = faces5[4] * s[0]
def sweep_and_rest(s, first, total, second, faces, count, groups=()):
    east, north, z, w, halo = parts(faces, count)

    def sweep(q):
        t = 1.2 * s[q + 1] + neighbours(first[q + 2], first[q + 1], first[q + 3], east[q], north[q], z[q], z[q + 1])
        total[q] = t
        second[q + 1] = w[q] * t

    if groups:
        each = count // len(groups)
        for k, group in enumerate(groups):
            for copy in group:
                copy.wait()
            loop(each, lambda q: sweep(q + k * each))
    else:
        loop(count, sweep)
    for side, q, down, up in ((0, -1, halo[4], z[0]), (1, count, z[count], halo[5])):
        second[q + 1] = halo[6 + side] * (1.2 * s[q + 1] + neighbours(
            first[q + 2], first[q + 1], first[q + 3], halo[side], halo[2 + side], down, up))

    def rest(q):
        return s[q + 1] - damping * total[q] + neighbours(
            second[q + 1], second[q], second[q + 2], east[q], north[q], z[q], z[q + 1])

    return rest


def fine_level(s_own, s_low, s_high, there, there_next, fine, s_next, edge_down, edge_up, s, first, total, second, faces, w_next, semaphores):
    strip = fine.shape[2]
    columns = s.shape[2]
    _, _, _, w, halo = parts(faces, 16)
    copies = Copies(semaphores)
    weights = copies.start(there.at[49:75], faces.at[49:75])
    groups = []
    for k in range(4):
        spans = ((4 * k, 4), (16 + 4 * k, 4), (32, 5) if k == 0 else (33 + 4 * k, 4))
        groups.append([copies.start(there.at[a:a + n], faces.at[a:a + n]) for a, n in spans])
    later = copies.start(there_next.at[25:33], w_next)
    blank = jnp.zeros((HALO - THIN, columns), jnp.float32)

    def place(k, value):
        s[k, :HALO - THIN] = blank
        s[k, HALO - THIN:HALO + strip + THIN] = value
        s[k, HALO + strip + THIN:] = blank

    loop(16, lambda q: place(q + 1, s_own[q]))
    weights.wait()
    place(0, s_low[0])
    first[0] = halo[8] * s[0]
    place(0, s_high[1])
    first[19] = halo[9] * s[0]
    place(0, s_low[1])
    first[1] = halo[6] * s[0]
    place(17, s_high[0])
    first[18] = halo[7] * s[17]

    def start(q):
        first[q + 2] = w[q] * s[q + 1]

    loop(16, start)
    rest = sweep_and_rest(s, first, total, second, faces, 16, groups)

    def pair(q):
        s_next[q] = rest(2 * q) + rest(2 * q + 1)
        fine[q, 0] = second[2 * q + 1, HALO:HALO + strip]
        fine[q, 1] = second[2 * q + 2, HALO:HALO + strip]

    loop(8, pair)
    later.wait()
    edge_down[0] = s_next[0]
    edge_down[1] = w_next[1] * s_next[1]
    edge_up[0] = w_next[6] * s_next[6]
    edge_up[1] = s_next[7]


def open_level(s_own, faces, low, high, s, first):
    count = s_own.shape[0]
    _, _, _, w, halo = parts(faces, count)
    s[0] = low[1]
    s[count + 1] = high[0]
    first[0] = low[0]
    first[1] = halo[6] * low[1]
    first[count + 2] = halo[7] * high[0]
    first[count + 3] = high[1]

    def start(q):
        s[q + 1] = s_own[q]
        first[q + 2] = w[q] * s_own[q]

    loop(count, start)


def first_coarse_level(s_own, low, high, faces, out, s_next, top, bottom, s, first, total, second):
    strip = out.shape[1]
    open_level(s_own, faces, low, high, s, first)
    rest = sweep_and_rest(s, first, total, second, faces, s_own.shape[0])

    def pair(q):
        value = rest(2 * q) + rest(2 * q + 1)
        s_next[q] = value[HALO:HALO + strip]
        top[q] = value[HALO:2 * HALO]
        bottom[q] = value[strip:HALO + strip]
        out[2 * q] = second[2 * q + 1, HALO:HALO + strip]
        out[2 * q + 1] = second[2 * q + 2, HALO:HALO + strip]

    loop(4, pair)


def middle_level(s_own, low, high, there, there_halo, there_next, out, s_next, faces_next, *rest_refs):
    edges, (s, first, total, second, faces, halo_next, semaphores) = rest_refs[:-7], rest_refs[-7:]
    count = s_own.shape[0]
    strip = out.shape[1]
    copies = Copies(semaphores)
    at = 3 * count + 1
    if count == 4:
        weights = [copies.start(there.at[at:at + count], faces.at[at:at + count]),
                   copies.start(there_halo, faces.at[at + count:at + count + 8])]
        others = copies.start(there.at[0:at], faces.at[0:at])
        later = [copies.start(there_next.at[0:9], faces_next.at[0:9]), copies.start(halo_next, faces_next.at[9:17])]
        for copy in weights:
            copy.wait()
    else:
        faces = there
        later = [copies.start(there_next, faces_next)]
    open_level(s_own, faces, low, high, s, first)
    if count == 4:
        others.wait()
    rest = sweep_and_rest(s, first, total, second, faces, count)
    for q in range(count // 2):
        s_next[q] = rest(2 * q) + rest(2 * q + 1)
    for copy in later:
        copy.wait()
    w_next = parts(faces_next, count // 2)[3]
    for q in range(count):
        out[q] = second[q + 1, HALO:HALO + strip]
    if len(edges) == 2:
        edge_down, edge_up = edges
        edge_down[0] = s_next[0]
        edge_down[1] = w_next[1] * s_next[1]
        edge_up[0] = w_next[count // 2 - 2] * s_next[count // 2 - 2]
        edge_up[1] = s_next[count // 2 - 1]
    else:
        edges[0][0] = w_next[0] * s_next[0]


def second_level(s_own, low, high, there, there_halo, there_next, halo_next, out, s_next, faces_next, edge_down, edge_up,
                 s, first, total, second, faces, semaphores):
    middle_level(s_own, low, high, there, there_halo, there_next, out, s_next, faces_next, edge_down, edge_up,
                 s, first, total, second, faces, halo_next, semaphores)


def third_level(s_own, low, high, faces, there_next, out, s_next, faces_next, first_next, s, first, total, second, semaphores):
    middle_level(s_own, low, high, faces, None, there_next, out, s_next, faces_next, first_next,
                 s, first, total, second, None, None, semaphores)


def widen(source2, above, below, faces2, fine, plane_out, s, edge_down, edge_up, back, semaphores):
    copies = Copies(semaphores)
    copies.start(fine, back.at[:, 0:2])
    copies.start(plane_out, back.at[:, 2])
    count, strip, _ = source2.shape
    w2 = faces2.at[3 * count + 1:4 * count + 1]
    for q in range(count):
        s[q, :HALO] = above[q]
        s[q, HALO:HALO + strip] = source2[q]
        s[q, HALO + strip:] = below[q]
    edge_down[0] = s[0]
    edge_down[1] = w2[1] * s[1]
    edge_up[0] = w2[count - 2] * s[count - 2]
    edge_up[1] = s[count - 1]

    for copy in copies.started:
        copy.wait()


def sweep_last(s, first, low, high, faces, total, second):
    east, north, z, w, _ = parts(faces, 1)
    t = 1.2 * s[0] + neighbours(first[0], low[0], high[0], east[0], north[0], z[0], z[1])
    total[0] = t
    second[0] = w[0] * t


def rest_last(s, total, second, low, high, faces, out):
    east, north, z, _, _ = parts(faces, 1)
    out[0] = s[0] - damping * total[0] + neighbours(second[0], low[0], high[0], east[0], north[0], z[0], z[1])


def finish(place, s, first, low, high, faces5, second2, second3, second4, *outs):
    own = slice(HALO, HALO + outs[0].shape[0])
    east, north, down, up, w = (faces5[k] for k in range(5))
    second5 = (w * (1.2 * s[0] + neighbours(first[0], low[0], high[0], east, north, down, up)))[own]
    for k in range(RING):
        at = (place[0] + k) % RING
        outs[k][...] = ((second2[at // 2] + second3[at // 4]) + second4[0, own]) + second5


def collect(place, *refs):
    out = refs[RING]
    for k, ref in zip((0,) + ORDER, refs):
        out[(place[0] + RING - k) % RING] = ref[...]


def exchange(edge_low, edge_high, distance=RING):
    return shifted(edge_high, distance), shifted(edge_low, -distance)


def on_device(right_side, labels, fraction):
    planes, rows, columns = right_side.shape
    strip = rows // RING
    frame = strip + 2 * HALO
    at_core = lax.axis_index("xy")

    def edges_of(first_rows, last_rows):
        got = lax.ppermute(jnp.where(at_core == 0, last_rows, first_rows), "xy", [(0, 1), (1, 0)])
        return jnp.where(at_core == 1, got, 0.0), jnp.where(at_core == 0, got, 0.0)

    def shape(n):
        return (n, frame, columns)

    at_ring = lax.axis_index("gz")
    place = jnp.stack([at_ring % RING, at_ring // RING % 2]).astype(jnp.int32)
    c_top, c_bottom = edges_of(conductivity(labels[:, :HALO], fraction[:, :HALO]),
                               conductivity(labels[:, rows - HALO:], fraction[:, rows - HALO:]))
    cuts = call(cut_conduct, [(planes, frame, columns)] * RING, [(planes, rows + 2 * HALO, columns)],
                place, labels, fraction, c_top, c_bottom, limit=10)
    s_top, s_bottom = edges_of(right_side[:, :HALO], right_side[:, rows - HALO:])
    thin = strip + 2 * THIN
    (s_cut,) = call(cut_source, [(RING, planes, thin, columns)], [], right_side, s_top, s_bottom, limit=10)
    c_parts = [cuts[0]] + [ring_permuted(cuts[k], k) for k in ORDER]
    c, near_down, near_up, far_down, far_up, ready = call(
        join, [shape(n) for n in (16, NEAR, NEAR, FAR, FAR)] + [(HALO, columns)], [shape(16)], place, *c_parts, limit=10,
        settled=(s_cut,), hbm_out=range(5), copies=5)
    s_own = transposed(after(s_cut, ready))
    c_low, c_high = exchange(near_down, near_up)
    far_low, far_high = exchange(far_down, far_up)
    sizes = [shape(own_planes_of(n)) for n in (16, 8, 4, 2, 1)]
    faces0, faces1, faces2, faces3, faces4, pack, edge = call(
        make_faces, sizes + [shape(3), shape(6)], sizes, place, c, c_low, c_high,
        limit=30, work=10.0, hbm_out=range(5), copies=7)
    halo2, halo3, ready = call(
        make_far_halos, [shape(8), shape(8), (HALO, columns)], [shape(8), shape(8)], edge, c_low, c_high, far_low, far_high,
        limit=10, work=3.0, hbm_out=range(2), copies=2)
    (faces5,) = call(make_last_faces, [shape(5)], [], place, faces4, partner(pack))

    s_own = after(s_own, ready).reshape(RING * planes, thin, columns)
    s_low, s_high = exchange(s_own[:2], s_own[-2:])
    fine, s1, edge_down, edge_up = call(
        fine_level, [(RING, planes, strip, columns), shape(8), shape(2), shape(2)],
        [shape(18), shape(20), shape(16), shape(18), shape(75), shape(8)],
        s_own, s_low, s_high, faces0, faces1, limit=28, work=8.0, hbm_in=(3, 4), copies=14)

    low, high = exchange(edge_down, edge_up)
    plane_out, s2, top, bottom = call(
        first_coarse_level,
        [(8, strip, columns), (4, strip, columns), (4, HALO, columns), (4, HALO, columns)],
        [shape(10), shape(12), shape(8), shape(10)], s1, low, high, faces1, limit=15, work=4.0)

    above = row_shifted(bottom, 1)
    below = row_shifted(top, -1)
    s2, edge_down, edge_up, back = call(
        widen, [shape(4), shape(2), shape(2), (RING, planes + 1, strip, columns)], [], s2, above, below, faces2, fine, plane_out, limit=10,
        hbm_out=(3,), copies=2)
    low, high = exchange(edge_down, edge_up)
    second2, s3, faces3, edge_down, edge_up = call(
        second_level, [(4, strip, columns), shape(2), shape(17), shape(2), shape(2)],
        [shape(6), shape(8), shape(4), shape(6), shape(25)],
        s2, low, high, faces2, halo2, faces3, halo3, limit=14, hbm_in=(3, 4, 5, 6), copies=5)
    low, high = exchange(edge_down, edge_up)
    second3, s4, faces4, first4 = call(
        third_level, [(2, strip, columns), shape(1), shape(5), shape(1)],
        [shape(4), shape(6), shape(2), shape(4)],
        s3, low, high, faces3, faces4, limit=12, hbm_in=(4,), copies=1)
    low, high = exchange(first4, first4)
    total4, second4 = call(sweep_last, [shape(1), shape(1)], [], s4, first4, low, high, faces4)
    low, high = exchange(second4, second4)
    (rest4,) = call(rest_last, [shape(1)], [], s4, total4, second4, low, high, faces4)
    s5, first5 = call(begin_last, [shape(1), shape(1)], [], rest4, partner(rest4), faces5)
    low, high = exchange(first5, first5, 2 * RING)
    back = transposed(back)
    sums = call(finish, [(strip, columns)] * RING, [],
                place, s5, first5, low, high, faces5, second2, second3, second4)
    (coarse_return,) = call(collect, [(RING, strip, columns)], [], place, sums[0], *[ring_permuted(sums[k], k) for k in ORDER], settled=(back,))

    fine_iterate = jnp.transpose(back[:, :planes], (1, 0, 2, 3)).reshape(planes, rows, columns)
    plane_iterate = back[:, planes].reshape(1, rows, columns)
    return fine_iterate, plane_iterate, coarse_return.reshape(1, rows, columns)


def solution(mesh):
    spec = P("gz", "xy", None)
    return jax.shard_map(
        on_device,
        mesh=mesh,
        in_specs=(spec, spec, spec),
        out_specs=(spec, spec, spec),
        check_vma=False,
    )
```

```python
from functools import partial

import jax
import jax.numpy as jnp
from jax import lax
from jax.experimental import pallas as pl
from jax.experimental.pallas import tpu as pltpu
from jax.sharding import PartitionSpec as P

RING = 8
HALO = 8
NEAR, FAR = 3, 6
THIN = 4
damping = 0.8
pore_value = 1.0
grain_value = 0.1
clay_value = 0.3
TINY = 1e-6


def ring_groups(count):
    return [[r * RING + k for k in range(RING)] for r in range(count // RING)]


def shifted(value, by):
    size = lax.axis_size("gz")
    pairs = [(i, i + by) for i in range(size) if 0 <= i + by < size]
    return lax.ppermute(value, "gz", pairs)


def row_shifted(value, by):
    pairs = []
    for ring in range(lax.axis_size("gz") // RING):
        for t in range(2 * RING):
            u = t + by
            if 0 <= u < 2 * RING:
                pairs.append(((ring * RING + t % RING) * 2 + t // RING, (ring * RING + u % RING) * 2 + u // RING))
    return lax.ppermute(value, ("gz", "xy"), pairs)


def partner(value):
    size = lax.axis_size("gz")
    return lax.ppermute(value, "gz", [(i, i + RING if (i // RING) % 2 == 0 else i - RING) for i in range(size)])


def transposed(value):
    return lax.all_to_all(value, "gz", 0, 0, axis_index_groups=ring_groups(lax.axis_size("gz")), tiled=True)


def conductivity(labels, fraction):
    return jnp.where(labels == 0, pore_value, jnp.where(labels == 1, grain_value, clay_value)) * fraction


def harmonic(one_side, other_side):
    return (2.0 * one_side * other_side) / jnp.maximum(one_side + other_side, TINY)


def next_row(v):
    return pltpu.roll(v, v.shape[0] - 1, 0)


def previous_row(v):
    return pltpu.roll(v, 1, 0)


def next_column(v):
    return pltpu.roll(v, v.shape[1] - 1, 1)


def previous_column(v):
    return pltpu.roll(v, 1, 1)


def neighbours(v, below, above, east, north, down, up):
    return (
        east * next_row(v)
        + previous_row(east * v)
        + north * next_column(v)
        + previous_column(north * v)
        + down * below
        + up * above
    )


def weight(c, east, north, down, up):
    diagonal = east + previous_row(east) + north + previous_column(north) + down + up
    return jnp.where(c > 0, damping / jnp.where(c > 0, diagonal, 1.0), 0.0)


def loop(count, body):
    def step(k, carry):
        body(k)
        return carry

    lax.fori_loop(0, count, step, 0)


def call(kernel, outs, scratch, *args, limit=8, work=0.0, settled=(), hbm_in=(), hbm_out=(), copies=0):
    shapes = [(pltpu.HBM if i in hbm_out else jax.ShapeDtypeStruct)(s, jnp.float32) for i, s in enumerate(outs)]
    vmem = pl.BlockSpec(memory_space=pltpu.VMEM)
    smem = pl.BlockSpec(memory_space=pltpu.SMEM)
    hbm = pl.BlockSpec(memory_space=pltpu.HBM)
    kinds = [hbm if i in hbm_in else smem if a.dtype == jnp.int32 and a.ndim == 1 else vmem for i, a in enumerate(args)]
    cost = pl.CostEstimate(flops=int(work * 1.0e9), bytes_accessed=int(work * 3.0e6), transcendentals=0) if work else None

    def body(*refs):
        kernel(*refs[len(settled):])

    args = [pltpu.with_memory_space_constraint(a, pltpu.HBM) if i in hbm_in else a for i, a in enumerate(args)]

    return pl.pallas_call(
        body,
        out_shape=shapes,
        in_specs=[pl.BlockSpec(memory_space=pl.ANY)] * len(settled) + kinds,
        out_specs=[hbm if i in hbm_out else vmem for i in range(len(shapes))],
        scratch_shapes=[pltpu.VMEM(s, jnp.float32) for s in scratch] + ([pltpu.SemaphoreType.DMA((copies,))] if copies else []),
        compiler_params=pltpu.CompilerParams(vmem_limit_bytes=limit * 1024 * 1024),
        cost_estimate=cost,
    )(*settled, *args)


ORDER = (3, 5, 4, 2, 6, 1, 7)


def ring_permuted(value, by):
    size = lax.axis_size("gz")
    return lax.ppermute(value, "gz", [(i, i // RING * RING + (i + by) % RING) for i in range(size)])


def after(value, *settled):
    def nothing(*refs):
        pass

    there = pl.BlockSpec(memory_space=pl.ANY)
    return pl.pallas_call(
        nothing,
        out_shape=jax.ShapeDtypeStruct(value.shape, value.dtype),
        in_specs=[there] * (1 + len(settled)),
        out_specs=there,
        compiler_params=pltpu.CompilerParams(vmem_limit_bytes=1024 * 1024),
        input_output_aliases={0: 0},
    )(value, *settled)


class Copies:
    def __init__(self, semaphores):
        self.semaphores, self.started = semaphores, []

    def start(self, source, target):
        copy = pltpu.make_async_copy(source, target, self.semaphores.at[len(self.started)])
        copy.start()
        self.started.append(copy)
        return copy


def cut_conduct(place, labels, fraction, top, bottom, *rest):
    outs, full = rest[:-1], rest[-1]
    planes, rows, _ = labels.shape
    strip = rows // RING
    for p in range(planes):
        full[p, :HALO] = top[p]
        full[p, HALO + rows:] = bottom[p]
        for k in range(RING):
            at = k * strip
            full[p, HALO + at:HALO + at + strip] = conductivity(labels[p, at:at + strip], fraction[p, at:at + strip])
        for k in range(RING):
            start = pl.multiple_of(((place[0] + k) % RING) * strip, strip)
            outs[k][p] = full[p, pl.ds(start, strip + 2 * HALO)]


def cut_source(source, top, bottom, out):
    planes, rows, _ = source.shape
    strip = rows // RING
    for p in range(planes):
        for k in range(RING):
            start = k * strip
            out[k, p, :THIN] = top[p, HALO - THIN:] if k == 0 else source[p, start - THIN:start]
            out[k, p, THIN:THIN + strip] = source[p, start:start + strip]
            out[k, p, THIN + strip:] = bottom[p, :THIN] if k == RING - 1 else source[p, start + strip:start + strip + THIN]


def join(place, *refs):
    c, near_low, near_high, far_low, far_high, ready, out, semaphores = refs[RING:]
    ready[...] = refs[0][0, :HALO]
    for k, ref in zip((0,) + ORDER, refs):
        start = ((place[0] + RING - k) % RING) * 2
        out[start] = ref[0]
        out[start + 1] = ref[1]
    copies = Copies(semaphores)
    for ref, first in ((near_low, 0), (near_high, 16 - NEAR), (far_low, NEAR), (far_high, 16 - NEAR - FAR), (c, 0)):
        copies.start(out.at[first:first + ref.shape[0]], ref)
    for copy in copies.started:
        copy.wait()


def plane_faces(c):
    last = lax.broadcasted_iota(jnp.int32, c.shape, 1) == c.shape[1] - 1
    return harmonic(c, next_row(c)), jnp.where(last, 0.0, harmonic(c, next_column(c)))


def parts(faces, count):
    east, north = faces.at[0:count], faces.at[count:2 * count]
    z, w = faces.at[2 * count:3 * count + 1], faces.at[3 * count + 1:4 * count + 1]
    return east, north, z, w, faces.at[4 * count + 1:] if faces.shape[0] > 4 * count + 1 else None


def planes_of(count):
    return 4 * count + 1 + (0 if count == 1 else 10 if count == 16 else 8)


def own_planes_of(count):
    return planes_of(count) if count > 4 else 4 * count + 1


def make_faces(place, c, low, high, out0, out1, out2, out3, out4, pack, edge, faces0, faces1, faces2, faces3, faces4, semaphores):
    east0, north0, z0, w0, halo0 = parts(faces0, 16)

    def z_face(p):
        z0[p] = harmonic(c[p - 1], c[p])

    loop(15, lambda k: z_face(k + 1))
    z0[0] = jnp.where(low[NEAR - 1] > 0, harmonic(low[NEAR - 1], c[0]), 2.0 * c[0])
    z0[16] = jnp.where(high[0] > 0, harmonic(c[15], high[0]), 2.0 * c[15])

    def weigh(p):
        east, north = plane_faces(c[p])
        east0[p] = east
        north0[p] = north
        w0[p] = weight(c[p], east, north, z0[p], z0[p + 1])

    copies = Copies(semaphores)
    loop(16, weigh)
    copies.start(faces0.at[0:65], out0.at[0:65])
    finer, count = faces0, 16
    for coarser in (faces1, faces2, faces3, faces4):
        east_f, north_f, z_f, _, _ = parts(finer, count)
        count //= 2
        east, north, z, w, _ = parts(coarser, count)

        def faces_and_weight(q):
            east_q = east_f[2 * q] + east_f[2 * q + 1]
            north_q = north_f[2 * q] + north_f[2 * q + 1]
            east[q] = east_q
            north[q] = north_q
            z[q] = z_f[2 * q]
            w[q] = weight(c[0], east_q, north_q, z_f[2 * q], z_f[2 * q + 2])

        loop(count, faces_and_weight)
        z[count] = z_f[2 * count]
        finer = coarser
    copies.start(faces1.at[0:33], out1.at[0:33])
    copies.start(faces2.at[0:17], out2.at[0:17])
    copies.start(faces3.at[0:9], out3.at[0:9])
    copies.start(faces4, out4)

    for side, ref, at, face in ((0, low, (2, 1, 0), 0), (1, high, (0, 1, 2), 16)):
        shared = z0[face]
        near, after_near, third = (ref[k] for k in at)
        middle = harmonic(near, after_near)
        outer = harmonic(after_near, third)
        east_near, north_near = plane_faces(near)
        east_next, north_next = plane_faces(after_near)
        east_sum, north_sum = east_near + east_next, north_near + north_next
        halo0[side] = east_near
        halo0[2 + side] = north_near
        halo0[4 + side] = middle
        halo0[6 + side] = weight(near, east_near, north_near, shared, middle)
        halo0[8 + side] = weight(after_near, east_next, north_next, middle, outer)
        halo1 = parts(faces1, 8)[4]
        halo1[side] = east_sum
        halo1[2 + side] = north_sum
        halo1[4 + side] = outer
        halo1[6 + side] = weight(near, east_sum, north_sum, shared, outer)
        edge[side] = east_sum
        edge[2 + side] = north_sum
        edge[4 + side] = shared
    copies.start(faces0.at[65:75], out0.at[65:75])
    copies.start(faces1.at[33:41], out1.at[33:41])
    pack[0] = faces4[0]
    pack[1] = faces4[1]
    pack[2] = jnp.where(place[1] == 0, faces4[2], faces4[3])
    for copy in copies.started:
        copy.wait()


def make_far_halos(edge, low, high, far_low, far_high, out2, out3, ready, halo2, halo3, semaphores):
    for side in range(2):
        def at(k):
            if side == 0:
                return low[NEAR - 1 - k] if k < NEAR else far_low[NEAR + FAR - 1 - k]
            return high[k] if k < NEAR else far_high[k - NEAR]

        near, east_sum, north_sum, shared = at(0), edge[side], edge[2 + side], edge[4 + side]
        for halo, thick in ((halo2, 4), (halo3, 8)):
            for k in range(thick // 2, thick):
                east, north = plane_faces(at(k))
                east_sum = east_sum + east
                north_sum = north_sum + north
            outer = harmonic(at(thick - 1), at(thick))
            halo[side] = east_sum
            halo[2 + side] = north_sum
            halo[4 + side] = outer
            halo[6 + side] = weight(near, east_sum, north_sum, shared, outer)
    copies = Copies(semaphores)
    copies.start(halo2, out2)
    copies.start(halo3, out3)
    ready[...] = edge[0, :HALO]
    for copy in copies.started:
        copy.wait()


def make_last_faces(place, faces4, other, faces5):
    east4, north4, z4, w4, _ = parts(faces4, 1)
    lower = place[1] == 0
    east = east4[0] + other[0]
    north = north4[0] + other[1]
    down = jnp.where(lower, z4[0], other[2])
    up = jnp.where(lower, other[2], z4[1])
    for k, value in enumerate((east, north, down, up, weight(w4[0], east, north, down, up))):
        faces5[k] = value


def begin_last(rest4, other, faces5, s, first):
    s[0] = rest4[0] + other[0]
    first[0] = faces5[4] * s[0]
def sweep_and_rest(s, first, total, second, faces, count):
    east, north, z, w, halo = parts(faces, count)

    def sweep(q):
        t = 1.2 * s[q + 1] + neighbours(first[q + 2], first[q + 1], first[q + 3], east[q], north[q], z[q], z[q + 1])
        total[q] = t
        second[q + 1] = w[q] * t

    loop(count, sweep)
    for side, q, down, up in ((0, -1, halo[4], z[0]), (1, count, z[count], halo[5])):
        second[q + 1] = halo[6 + side] * (1.2 * s[q + 1] + neighbours(
            first[q + 2], first[q + 1], first[q + 3], halo[side], halo[2 + side], down, up))

    def rest(q):
        return s[q + 1] - damping * total[q] + neighbours(
            second[q + 1], second[q], second[q + 2], east[q], north[q], z[q], z[q + 1])

    return rest


def put(ref, k, value):
    rows = value.shape[0]
    cut = (ref.shape[1] - rows) // 2
    if cut:
        blank = jnp.zeros((cut, value.shape[1]), jnp.float32)
        ref[k, :cut] = blank
        ref[k, cut + rows:] = blank
    ref[k, cut:cut + rows] = value


def fine_inside(s_own, there, there_next, s, first, total, second, s_next, faces, w_next, semaphores):
    east, north, z, w, _ = parts(faces, 16)
    copies = Copies(semaphores)
    weights = copies.start(there.at[49:75], faces.at[49:75])
    groups = []
    for k in range(4):
        spans = ((4 * k, 4), (16 + 4 * k, 4), (32, 5) if k == 0 else (33 + 4 * k, 4))
        groups.append([copies.start(there.at[a:a + n], faces.at[a:a + n]) for a, n in spans])
    later = copies.start(there_next.at[25:33], w_next)
    loop(16, lambda q: put(s, q, s_own[q]))
    weights.wait()

    def start(q):
        first[q] = w[q] * s[q]

    loop(16, start)

    def sweep(q):
        t = 1.2 * s[q] + neighbours(first[q], first[q - 1], first[q + 1], east[q], north[q], z[q], z[q + 1])
        total[q] = t
        second[q] = w[q] * t

    for k, group in enumerate(groups):
        for copy in group:
            copy.wait()
        low, high = max(4 * k, 1), min(4 * k + 4, 15)
        loop(high - low, lambda q: sweep(q + low))

    def rest(q):
        return s[q] - damping * total[q] + neighbours(second[q], second[q - 1], second[q + 1], east[q], north[q], z[q], z[q + 1])

    def pair(q):
        s_next[q + 1] = rest(2 * q + 2) + rest(2 * q + 3)

    loop(6, pair)
    later.wait()


def fine_ends(s_low, s_high, s, first, total, second, s_inside, faces, w_next, fine, s_next, edge_down, edge_up, frames):
    east, north, z, w, halo = parts(faces, 16)
    strip = fine.shape[2]
    own = slice(HALO, HALO + strip)
    inner = slice(HALO - THIN, HALO + strip + THIN)
    for k, value in enumerate((s_low[0], s_low[1], s_high[0], s_high[1])):
        put(frames, k, value)

    def copy(q):
        s_next[q + 1] = s_inside[q + 1]

    loop(6, copy)

    def keep(q):
        fine[q, 1] = second[2 * q + 1, own]
        fine[q + 1, 0] = second[2 * q + 2, own]

    loop(7, keep)

    def residual(q, t, v, below, above):
        return s[q] - damping * t + neighbours(v, below, above, east[q], north[q], z[q], z[q + 1])

    near = halo[6] * frames[1]
    t = 1.2 * frames[1] + neighbours(near, halo[8] * frames[0], first[0], halo[0], halo[2], halo[4], z[0])
    outside = halo[6] * t
    t = 1.2 * s[0] + neighbours(first[0], near, first[1], east[0], north[0], z[0], z[1])
    inside = w[0] * t
    fine[0, 0] = inside[own]
    s_next[0] = residual(0, t, inside, outside, second[1]) + residual(1, total[1], second[1], inside, second[2])
    near = halo[7] * frames[2]
    t = 1.2 * frames[2] + neighbours(near, first[15], halo[9] * frames[3], halo[1], halo[3], z[16], halo[5])
    outside = halo[7] * t
    t = 1.2 * s[15] + neighbours(first[15], first[14], near, east[15], north[15], z[15], z[16])
    inside = w[15] * t
    fine[7, 1] = inside[own]
    s_next[7] = residual(14, total[14], second[14], second[13], inside) + residual(15, t, inside, second[14], outside)

    edge_down[0] = s_next[0, inner]
    edge_down[1] = w_next[1, inner] * s_next[1, inner]
    edge_up[0] = w_next[6, inner] * s_next[6, inner]
    edge_up[1] = s_next[7, inner]


def open_level(s_own, faces, low, high, s, first):
    count = s_own.shape[0]
    _, _, _, w, halo = parts(faces, count)
    put(s, 0, low[1])
    put(s, count + 1, high[0])
    put(first, 0, low[0])
    first[1] = halo[6] * s[0]
    first[count + 2] = halo[7] * s[count + 1]
    put(first, count + 3, high[1])

    def start(q):
        s[q + 1] = s_own[q]
        first[q + 2] = w[q] * s_own[q]

    loop(count, start)


def first_coarse_level(s_own, low, high, faces, out, s_next, top, bottom, s, first, total, second):
    strip = out.shape[1]
    open_level(s_own, faces, low, high, s, first)
    rest = sweep_and_rest(s, first, total, second, faces, s_own.shape[0])

    def pair(q):
        value = rest(2 * q) + rest(2 * q + 1)
        s_next[q] = value[HALO:HALO + strip]
        top[q] = value[HALO:2 * HALO]
        bottom[q] = value[strip:HALO + strip]
        out[2 * q] = second[2 * q + 1, HALO:HALO + strip]
        out[2 * q + 1] = second[2 * q + 2, HALO:HALO + strip]

    loop(4, pair)


def middle_level(s_own, low, high, there, there_halo, there_next, out, s_next, faces_next, *rest_refs):
    edges, (s, first, total, second, faces, halo_next, semaphores) = rest_refs[:-7], rest_refs[-7:]
    count = s_own.shape[0]
    strip = out.shape[1]
    copies = Copies(semaphores)
    at = 3 * count + 1
    if count == 4:
        weights = [copies.start(there.at[at:at + count], faces.at[at:at + count]),
                   copies.start(there_halo, faces.at[at + count:at + count + 8])]
        others = copies.start(there.at[0:at], faces.at[0:at])
        later = [copies.start(there_next.at[0:9], faces_next.at[0:9]), copies.start(halo_next, faces_next.at[9:17])]
        for copy in weights:
            copy.wait()
    else:
        faces = there
        later = [copies.start(there_next, faces_next)]
    open_level(s_own, faces, low, high, s, first)
    if count == 4:
        others.wait()
    rest = sweep_and_rest(s, first, total, second, faces, count)
    for q in range(count // 2):
        s_next[q] = rest(2 * q) + rest(2 * q + 1)
    for copy in later:
        copy.wait()
    w_next = parts(faces_next, count // 2)[3]
    for q in range(count):
        out[q] = second[q + 1, HALO:HALO + strip]
    if len(edges) == 2:
        edge_down, edge_up = edges
        inner = slice(HALO - THIN, HALO + strip + THIN)
        edge_down[0] = s_next[0, inner]
        edge_down[1] = w_next[1, inner] * s_next[1, inner]
        edge_up[0] = w_next[count // 2 - 2, inner] * s_next[count // 2 - 2, inner]
        edge_up[1] = s_next[count // 2 - 1, inner]
    else:
        edges[0][0] = w_next[0] * s_next[0]


def second_level(s_own, low, high, there, there_halo, there_next, halo_next, out, s_next, faces_next, edge_down, edge_up,
                 s, first, total, second, faces, semaphores):
    middle_level(s_own, low, high, there, there_halo, there_next, out, s_next, faces_next, edge_down, edge_up,
                 s, first, total, second, faces, halo_next, semaphores)


def third_level(s_own, low, high, faces, there_next, out, s_next, faces_next, first_next, s, first, total, second, semaphores):
    middle_level(s_own, low, high, faces, None, there_next, out, s_next, faces_next, first_next,
                 s, first, total, second, None, None, semaphores)


def widen(source2, above, below, faces2, fine, plane_out, s, edge_down, edge_up, back, semaphores):
    copies = Copies(semaphores)
    copies.start(fine, back.at[:, 0:2])
    copies.start(plane_out, back.at[:, 2])
    count, strip, _ = source2.shape
    w2 = faces2.at[3 * count + 1:4 * count + 1]
    for q in range(count):
        s[q, :HALO] = above[q]
        s[q, HALO:HALO + strip] = source2[q]
        s[q, HALO + strip:] = below[q]
    edge_down[0] = s[0]
    edge_down[1] = w2[1] * s[1]
    edge_up[0] = w2[count - 2] * s[count - 2]
    edge_up[1] = s[count - 1]

    for copy in copies.started:
        copy.wait()


def sweep_last(s, first, low, high, faces, total, second):
    east, north, z, w, _ = parts(faces, 1)
    t = 1.2 * s[0] + neighbours(first[0], low[0], high[0], east[0], north[0], z[0], z[1])
    total[0] = t
    second[0] = w[0] * t


def rest_last(s, total, second, low, high, faces, out):
    east, north, z, _, _ = parts(faces, 1)
    out[0] = s[0] - damping * total[0] + neighbours(second[0], low[0], high[0], east[0], north[0], z[0], z[1])


def finish(place, s, first, low, high, faces5, second2, second3, second4, *outs):
    own = slice(HALO, HALO + outs[0].shape[0])
    east, north, down, up, w = (faces5[k] for k in range(5))
    second5 = (w * (1.2 * s[0] + neighbours(first[0], low[0], high[0], east, north, down, up)))[own]
    for k in range(RING):
        at = (place[0] + k) % RING
        outs[k][...] = ((second2[at // 2] + second3[at // 4]) + second4[0, own]) + second5


def collect(place, *refs):
    out = refs[RING]
    for k, ref in zip((0,) + ORDER, refs):
        out[(place[0] + RING - k) % RING] = ref[...]


def exchange(edge_low, edge_high, distance=RING):
    return shifted(edge_high, distance), shifted(edge_low, -distance)


def on_device(right_side, labels, fraction):
    planes, rows, columns = right_side.shape
    strip = rows // RING
    frame = strip + 2 * HALO
    at_core = lax.axis_index("xy")

    def edges_of(first_rows, last_rows):
        got = lax.ppermute(jnp.where(at_core == 0, last_rows, first_rows), "xy", [(0, 1), (1, 0)])
        return jnp.where(at_core == 1, got, 0.0), jnp.where(at_core == 0, got, 0.0)

    def shape(n):
        return (n, frame, columns)

    at_ring = lax.axis_index("gz")
    place = jnp.stack([at_ring % RING, at_ring // RING % 2]).astype(jnp.int32)
    c_top, c_bottom = edges_of(conductivity(labels[:, :HALO], fraction[:, :HALO]),
                               conductivity(labels[:, rows - HALO:], fraction[:, rows - HALO:]))
    cuts = call(cut_conduct, [(planes, frame, columns)] * RING, [(planes, rows + 2 * HALO, columns)],
                place, labels, fraction, c_top, c_bottom, limit=10)
    s_top, s_bottom = edges_of(right_side[:, :HALO], right_side[:, rows - HALO:])
    thin = strip + 2 * THIN
    (s_cut,) = call(cut_source, [(RING, planes, thin, columns)], [], right_side, s_top, s_bottom, limit=10)
    c_parts = [cuts[0]] + [ring_permuted(cuts[k], k) for k in ORDER]
    c, near_down, near_up, far_down, far_up, ready = call(
        join, [shape(n) for n in (16, NEAR, NEAR, FAR, FAR)] + [(HALO, columns)], [shape(16)], place, *c_parts, limit=10,
        settled=(s_cut,), hbm_out=range(5), copies=5)
    s_own = transposed(after(s_cut, ready))
    c_low, c_high = exchange(near_down, near_up)
    far_low, far_high = exchange(far_down, far_up)
    sizes = [shape(own_planes_of(n)) for n in (16, 8, 4, 2, 1)]
    faces0, faces1, faces2, faces3, faces4, pack, edge = call(
        make_faces, sizes + [shape(3), shape(6)], sizes, place, c, c_low, c_high,
        limit=30, work=10.0, hbm_out=range(5), copies=7)
    halo2, halo3, ready = call(
        make_far_halos, [shape(8), shape(8), (HALO, columns)], [shape(8), shape(8)], edge, c_low, c_high, far_low, far_high,
        limit=10, work=3.0, hbm_out=range(2), copies=2)
    (faces5,) = call(make_last_faces, [shape(5)], [], place, faces4, partner(pack))

    s_own = after(s_own, ready).reshape(RING * planes, thin, columns)
    s_low, s_high = exchange(s_own[:2], s_own[-2:])
    inside = call(
        fine_inside, [shape(n) for n in (16, 16, 16, 16, 8, 75, 8)], [],
        s_own, faces0, faces1, limit=28, work=8.0, hbm_in=(1, 2), copies=14)
    fine, s1, edge_down, edge_up = call(
        fine_ends, [(RING, planes, strip, columns), shape(8), (2, thin, columns), (2, thin, columns)], [shape(4)],
        s_low, s_high, *inside, limit=28)

    low, high = exchange(edge_down, edge_up)
    plane_out, s2, top, bottom = call(
        first_coarse_level,
        [(8, strip, columns), (4, strip, columns), (4, HALO, columns), (4, HALO, columns)],
        [shape(10), shape(12), shape(8), shape(10)], s1, low, high, faces1, limit=15, work=4.0)

    above = row_shifted(bottom, 1)
    below = row_shifted(top, -1)
    s2, edge_down, edge_up, back = call(
        widen, [shape(4), shape(2), shape(2), (RING, planes + 1, strip, columns)], [], s2, above, below, faces2, fine, plane_out, limit=10,
        hbm_out=(3,), copies=2)
    low, high = exchange(edge_down, edge_up)
    second2, s3, faces3, edge_down, edge_up = call(
        second_level, [(4, strip, columns), shape(2), shape(17), (2, thin, columns), (2, thin, columns)],
        [shape(6), shape(8), shape(4), shape(6), shape(25)],
        s2, low, high, faces2, halo2, faces3, halo3, limit=14, hbm_in=(3, 4, 5, 6), copies=5)
    low, high = exchange(edge_down, edge_up)
    second3, s4, faces4, first4 = call(
        third_level, [(2, strip, columns), shape(1), shape(5), shape(1)],
        [shape(4), shape(6), shape(2), shape(4)],
        s3, low, high, faces3, faces4, limit=12, hbm_in=(4,), copies=1)
    low, high = exchange(first4, first4)
    total4, second4 = call(sweep_last, [shape(1), shape(1)], [], s4, first4, low, high, faces4)
    low, high = exchange(second4, second4)
    (rest4,) = call(rest_last, [shape(1)], [], s4, total4, second4, low, high, faces4)
    s5, first5 = call(begin_last, [shape(1), shape(1)], [], rest4, partner(rest4), faces5)
    low, high = exchange(first5, first5, 2 * RING)
    back = transposed(back)
    sums = call(finish, [(strip, columns)] * RING, [],
                place, s5, first5, low, high, faces5, second2, second3, second4)
    (coarse_return,) = call(collect, [(RING, strip, columns)], [], place, sums[0], *[ring_permuted(sums[k], k) for k in ORDER], settled=(back,))

    fine_iterate = jnp.transpose(back[:, :planes], (1, 0, 2, 3)).reshape(planes, rows, columns)
    plane_iterate = back[:, planes].reshape(1, rows, columns)
    return fine_iterate, plane_iterate, coarse_return.reshape(1, rows, columns)


def solution(mesh):
    spec = P("gz", "xy", None)
    return jax.shard_map(
        on_device,
        mesh=mesh,
        in_specs=(spec, spec, spec),
        out_specs=(spec, spec, spec),
        check_vma=False,
    )
```

```python
from functools import partial

import jax
import jax.numpy as jnp
from jax import lax
from jax.experimental import pallas as pl
from jax.experimental.pallas import tpu as pltpu
from jax.sharding import PartitionSpec as P

RING = 8
HALO = 8
NEAR, FAR = 3, 6
THIN = 4
damping = 0.8
pore_value = 1.0
grain_value = 0.1
clay_value = 0.3
TINY = 1e-6


def ring_groups(count):
    return [[r * RING + k for k in range(RING)] for r in range(count // RING)]


def shifted(value, by):
    size = lax.axis_size("gz")
    pairs = [(i, i + by) for i in range(size) if 0 <= i + by < size]
    return lax.ppermute(value, "gz", pairs)


def row_shifted(value, by):
    pairs = []
    for ring in range(lax.axis_size("gz") // RING):
        for t in range(2 * RING):
            u = t + by
            if 0 <= u < 2 * RING:
                pairs.append(((ring * RING + t % RING) * 2 + t // RING, (ring * RING + u % RING) * 2 + u // RING))
    return lax.ppermute(value, ("gz", "xy"), pairs)


def partner(value):
    size = lax.axis_size("gz")
    return lax.ppermute(value, "gz", [(i, i + RING if (i // RING) % 2 == 0 else i - RING) for i in range(size)])


def transposed(value):
    return lax.all_to_all(value, "gz", 0, 0, axis_index_groups=ring_groups(lax.axis_size("gz")), tiled=True)


def conductivity(labels, fraction):
    return jnp.where(labels == 0, pore_value, jnp.where(labels == 1, grain_value, clay_value)) * fraction


def harmonic(one_side, other_side):
    return (2.0 * one_side * other_side) / jnp.maximum(one_side + other_side, TINY)


def next_row(v):
    return pltpu.roll(v, v.shape[0] - 1, 0)


def previous_row(v):
    return pltpu.roll(v, 1, 0)


def next_column(v):
    return pltpu.roll(v, v.shape[1] - 1, 1)


def previous_column(v):
    return pltpu.roll(v, 1, 1)


def neighbours(v, below, above, east, north, down, up):
    return (
        east * next_row(v)
        + previous_row(east * v)
        + north * next_column(v)
        + previous_column(north * v)
        + down * below
        + up * above
    )


def weight(c, east, north, down, up):
    diagonal = east + previous_row(east) + north + previous_column(north) + down + up
    return jnp.where(c > 0, damping / jnp.where(c > 0, diagonal, 1.0), 0.0)


def loop(count, body):
    def step(k, carry):
        body(k)
        return carry

    lax.fori_loop(0, count, step, 0)


def call(kernel, outs, scratch, *args, limit=8, work=0.0, settled=(), hbm_in=(), hbm_out=(), copies=0):
    shapes = [(pltpu.HBM if i in hbm_out else jax.ShapeDtypeStruct)(s, jnp.float32) for i, s in enumerate(outs)]
    vmem = pl.BlockSpec(memory_space=pltpu.VMEM)
    smem = pl.BlockSpec(memory_space=pltpu.SMEM)
    hbm = pl.BlockSpec(memory_space=pltpu.HBM)
    kinds = [hbm if i in hbm_in else smem if a.dtype == jnp.int32 and a.ndim == 1 else vmem for i, a in enumerate(args)]
    cost = pl.CostEstimate(flops=int(work * 1.0e9), bytes_accessed=int(work * 3.0e6), transcendentals=0) if work else None

    def body(*refs):
        kernel(*refs[len(settled):])

    args = [pltpu.with_memory_space_constraint(a, pltpu.HBM) if i in hbm_in else a for i, a in enumerate(args)]

    return pl.pallas_call(
        body,
        out_shape=shapes,
        in_specs=[pl.BlockSpec(memory_space=pl.ANY)] * len(settled) + kinds,
        out_specs=[hbm if i in hbm_out else vmem for i in range(len(shapes))],
        scratch_shapes=[pltpu.VMEM(s, jnp.float32) for s in scratch] + ([pltpu.SemaphoreType.DMA((copies,))] if copies else []),
        compiler_params=pltpu.CompilerParams(vmem_limit_bytes=limit * 1024 * 1024),
        cost_estimate=cost,
    )(*settled, *args)


ORDER = (3, 5, 4, 2, 6, 1, 7)


def ring_permuted(value, by):
    size = lax.axis_size("gz")
    return lax.ppermute(value, "gz", [(i, i // RING * RING + (i + by) % RING) for i in range(size)])


def after(value, *settled):
    def nothing(*refs):
        pass

    there = pl.BlockSpec(memory_space=pl.ANY)
    return pl.pallas_call(
        nothing,
        out_shape=jax.ShapeDtypeStruct(value.shape, value.dtype),
        in_specs=[there] * (1 + len(settled)),
        out_specs=there,
        compiler_params=pltpu.CompilerParams(vmem_limit_bytes=1024 * 1024),
        input_output_aliases={0: 0},
    )(value, *settled)


class Copies:
    def __init__(self, semaphores):
        self.semaphores, self.started = semaphores, []

    def start(self, source, target):
        copy = pltpu.make_async_copy(source, target, self.semaphores.at[len(self.started)])
        copy.start()
        self.started.append(copy)
        return copy


def cut_conduct(place, labels, fraction, top, bottom, *rest):
    outs, full = rest[:-1], rest[-1]
    planes, rows, _ = labels.shape
    strip = rows // RING
    for p in range(planes):
        full[p, :HALO] = top[p]
        full[p, HALO + rows:] = bottom[p]
        for k in range(RING):
            at = k * strip
            full[p, HALO + at:HALO + at + strip] = conductivity(labels[p, at:at + strip], fraction[p, at:at + strip])
        for k in range(RING):
            start = pl.multiple_of(((place[0] + k) % RING) * strip, strip)
            outs[k][p] = full[p, pl.ds(start, strip + 2 * HALO)]


def cut_source(source, top, bottom, out):
    planes, rows, _ = source.shape
    strip = rows // RING
    for p in range(planes):
        for k in range(RING):
            start = k * strip
            out[k, p, :THIN] = top[p, HALO - THIN:] if k == 0 else source[p, start - THIN:start]
            out[k, p, THIN:THIN + strip] = source[p, start:start + strip]
            out[k, p, THIN + strip:] = bottom[p, :THIN] if k == RING - 1 else source[p, start + strip:start + strip + THIN]


def join(place, *refs):
    c, near_low, near_high, far_low, far_high, ready, out, semaphores = refs[RING:]
    ready[...] = refs[0][0, :HALO]
    for k, ref in zip((0,) + ORDER, refs):
        start = ((place[0] + RING - k) % RING) * 2
        out[start] = ref[0]
        out[start + 1] = ref[1]
    copies = Copies(semaphores)
    for ref, first in ((near_low, 0), (near_high, 16 - NEAR), (far_low, NEAR), (far_high, 16 - NEAR - FAR), (c, 0)):
        copies.start(out.at[first:first + ref.shape[0]], ref)
    for copy in copies.started:
        copy.wait()


def plane_faces(c):
    last = lax.broadcasted_iota(jnp.int32, c.shape, 1) == c.shape[1] - 1
    return harmonic(c, next_row(c)), jnp.where(last, 0.0, harmonic(c, next_column(c)))


def parts(faces, count):
    east, north = faces.at[0:count], faces.at[count:2 * count]
    z, w = faces.at[2 * count:3 * count + 1], faces.at[3 * count + 1:4 * count + 1]
    return east, north, z, w, faces.at[4 * count + 1:] if faces.shape[0] > 4 * count + 1 else None


def planes_of(count):
    return 4 * count + 1 + (0 if count == 1 else 10 if count == 16 else 8)


def own_planes_of(count):
    return planes_of(count) if count > 4 else 4 * count + 1


def make_faces(place, c, low, high, out0, out1, out2, out3, out4, pack, edge, faces0, faces1, faces2, faces3, faces4, semaphores):
    east0, north0, z0, w0, halo0 = parts(faces0, 16)

    def z_face(p):
        z0[p] = harmonic(c[p - 1], c[p])

    loop(15, lambda k: z_face(k + 1))
    z0[0] = jnp.where(low[NEAR - 1] > 0, harmonic(low[NEAR - 1], c[0]), 2.0 * c[0])
    z0[16] = jnp.where(high[0] > 0, harmonic(c[15], high[0]), 2.0 * c[15])

    def weigh(p):
        east, north = plane_faces(c[p])
        east0[p] = east
        north0[p] = north
        w0[p] = weight(c[p], east, north, z0[p], z0[p + 1])

    copies = Copies(semaphores)
    loop(16, weigh)
    copies.start(faces0.at[0:65], out0.at[0:65])
    finer, count = faces0, 16
    for coarser in (faces1, faces2, faces3, faces4):
        east_f, north_f, z_f, _, _ = parts(finer, count)
        count //= 2
        east, north, z, w, _ = parts(coarser, count)

        def faces_and_weight(q):
            east_q = east_f[2 * q] + east_f[2 * q + 1]
            north_q = north_f[2 * q] + north_f[2 * q + 1]
            east[q] = east_q
            north[q] = north_q
            z[q] = z_f[2 * q]
            w[q] = weight(c[0], east_q, north_q, z_f[2 * q], z_f[2 * q + 2])

        loop(count, faces_and_weight)
        z[count] = z_f[2 * count]
        finer = coarser
    copies.start(faces1.at[0:33], out1.at[0:33])
    copies.start(faces2.at[0:17], out2.at[0:17])
    copies.start(faces3.at[0:9], out3.at[0:9])
    copies.start(faces4, out4)

    for side, ref, at, face in ((0, low, (2, 1, 0), 0), (1, high, (0, 1, 2), 16)):
        shared = z0[face]
        near, after_near, third = (ref[k] for k in at)
        middle = harmonic(near, after_near)
        outer = harmonic(after_near, third)
        east_near, north_near = plane_faces(near)
        east_next, north_next = plane_faces(after_near)
        east_sum, north_sum = east_near + east_next, north_near + north_next
        halo0[side] = east_near
        halo0[2 + side] = north_near
        halo0[4 + side] = middle
        halo0[6 + side] = weight(near, east_near, north_near, shared, middle)
        halo0[8 + side] = weight(after_near, east_next, north_next, middle, outer)
        halo1 = parts(faces1, 8)[4]
        halo1[side] = east_sum
        halo1[2 + side] = north_sum
        halo1[4 + side] = outer
        halo1[6 + side] = weight(near, east_sum, north_sum, shared, outer)
        edge[side] = east_sum
        edge[2 + side] = north_sum
        edge[4 + side] = shared
    copies.start(faces0.at[65:75], out0.at[65:75])
    copies.start(faces1.at[33:41], out1.at[33:41])
    pack[0] = faces4[0]
    pack[1] = faces4[1]
    pack[2] = jnp.where(place[1] == 0, faces4[2], faces4[3])
    for copy in copies.started:
        copy.wait()


def make_far_halos(edge, low, high, far_low, far_high, out2, out3, ready, halo2, halo3, semaphores):
    for side in range(2):
        def at(k):
            if side == 0:
                return low[NEAR - 1 - k] if k < NEAR else far_low[NEAR + FAR - 1 - k]
            return high[k] if k < NEAR else far_high[k - NEAR]

        near, east_sum, north_sum, shared = at(0), edge[side], edge[2 + side], edge[4 + side]
        for halo, thick in ((halo2, 4), (halo3, 8)):
            for k in range(thick // 2, thick):
                east, north = plane_faces(at(k))
                east_sum = east_sum + east
                north_sum = north_sum + north
            outer = harmonic(at(thick - 1), at(thick))
            halo[side] = east_sum
            halo[2 + side] = north_sum
            halo[4 + side] = outer
            halo[6 + side] = weight(near, east_sum, north_sum, shared, outer)
    copies = Copies(semaphores)
    copies.start(halo2, out2)
    copies.start(halo3, out3)
    ready[...] = edge[0, :HALO]
    for copy in copies.started:
        copy.wait()


def make_last_faces(place, faces4, other, faces5):
    east4, north4, z4, w4, _ = parts(faces4, 1)
    lower = place[1] == 0
    east = east4[0] + other[0]
    north = north4[0] + other[1]
    down = jnp.where(lower, z4[0], other[2])
    up = jnp.where(lower, other[2], z4[1])
    for k, value in enumerate((east, north, down, up, weight(w4[0], east, north, down, up))):
        faces5[k] = value


def begin_last(rest4, other, faces5, s, first, edge):
    put(s, 0, rest4[0] + other[0])
    first[0] = faces5[4] * s[0]
    edge[0] = first[0, HALO:HALO + edge.shape[1]]
def sweep_and_rest(s, first, total, second, faces, count):
    east, north, z, w, halo = parts(faces, count)

    def sweep(q):
        t = 1.2 * s[q + 1] + neighbours(first[q + 2], first[q + 1], first[q + 3], east[q], north[q], z[q], z[q + 1])
        total[q] = t
        second[q + 1] = w[q] * t

    loop(count, sweep)
    for side, q, down, up in ((0, -1, halo[4], z[0]), (1, count, z[count], halo[5])):
        second[q + 1] = halo[6 + side] * (1.2 * s[q + 1] + neighbours(
            first[q + 2], first[q + 1], first[q + 3], halo[side], halo[2 + side], down, up))

    def rest(q):
        return s[q + 1] - damping * total[q] + neighbours(
            second[q + 1], second[q], second[q + 2], east[q], north[q], z[q], z[q + 1])

    return rest


def put(ref, k, value):
    rows = value.shape[0]
    cut = (ref.shape[1] - rows) // 2
    if cut:
        blank = jnp.zeros((cut, value.shape[1]), jnp.float32)
        ref[k, :cut] = blank
        ref[k, cut + rows:] = blank
    ref[k, cut:cut + rows] = value


def fine_inside(s_own, there, there_next, s, first, total, second, s_next, faces, w_next, semaphores):
    east, north, z, w, _ = parts(faces, 16)
    copies = Copies(semaphores)
    weights = copies.start(there.at[49:75], faces.at[49:75])
    groups = []
    for k in range(4):
        spans = ((4 * k, 4), (16 + 4 * k, 4), (32, 5) if k == 0 else (33 + 4 * k, 4))
        groups.append([copies.start(there.at[a:a + n], faces.at[a:a + n]) for a, n in spans])
    later = copies.start(there_next.at[25:33], w_next)
    loop(16, lambda q: put(s, q, s_own[q]))
    weights.wait()

    def start(q):
        first[q] = w[q] * s[q]

    loop(16, start)

    def sweep(q):
        t = 1.2 * s[q] + neighbours(first[q], first[q - 1], first[q + 1], east[q], north[q], z[q], z[q + 1])
        total[q] = t
        second[q] = w[q] * t

    for k, group in enumerate(groups):
        for copy in group:
            copy.wait()
        low, high = max(4 * k, 1), min(4 * k + 4, 15)
        loop(high - low, lambda q: sweep(q + low))

    def rest(q):
        return s[q] - damping * total[q] + neighbours(second[q], second[q - 1], second[q + 1], east[q], north[q], z[q], z[q + 1])

    def pair(q):
        s_next[q + 1] = rest(2 * q + 2) + rest(2 * q + 3)

    loop(6, pair)
    later.wait()


def fine_ends(s_low, s_high, s, first, total, second, s_inside, faces, w_next, fine, s_next, edge_down, edge_up, frames):
    east, north, z, w, halo = parts(faces, 16)
    strip = fine.shape[2]
    own = slice(HALO, HALO + strip)
    inner = slice(HALO - THIN, HALO + strip + THIN)
    for k, value in enumerate((s_low[0], s_low[1], s_high[0], s_high[1])):
        put(frames, k, value)

    def copy(q):
        s_next[q + 1] = s_inside[q + 1]

    loop(6, copy)

    def keep(q):
        fine[q, 1] = second[2 * q + 1, own]
        fine[q + 1, 0] = second[2 * q + 2, own]

    loop(7, keep)

    def residual(q, t, v, below, above):
        return s[q] - damping * t + neighbours(v, below, above, east[q], north[q], z[q], z[q + 1])

    near = halo[6] * frames[1]
    t = 1.2 * frames[1] + neighbours(near, halo[8] * frames[0], first[0], halo[0], halo[2], halo[4], z[0])
    outside = halo[6] * t
    t = 1.2 * s[0] + neighbours(first[0], near, first[1], east[0], north[0], z[0], z[1])
    inside = w[0] * t
    fine[0, 0] = inside[own]
    s_next[0] = residual(0, t, inside, outside, second[1]) + residual(1, total[1], second[1], inside, second[2])
    near = halo[7] * frames[2]
    t = 1.2 * frames[2] + neighbours(near, first[15], halo[9] * frames[3], halo[1], halo[3], z[16], halo[5])
    outside = halo[7] * t
    t = 1.2 * s[15] + neighbours(first[15], first[14], near, east[15], north[15], z[15], z[16])
    inside = w[15] * t
    fine[7, 1] = inside[own]
    s_next[7] = residual(14, total[14], second[14], second[13], inside) + residual(15, t, inside, second[14], outside)

    edge_down[0] = s_next[0, inner]
    edge_down[1] = w_next[1, inner] * s_next[1, inner]
    edge_up[0] = w_next[6, inner] * s_next[6, inner]
    edge_up[1] = s_next[7, inner]


def open_level(s_own, faces, low, high, s, first):
    count = s_own.shape[0]
    _, _, _, w, halo = parts(faces, count)
    put(s, 0, low[1])
    put(s, count + 1, high[0])
    put(first, 0, low[0])
    first[1] = halo[6] * s[0]
    first[count + 2] = halo[7] * s[count + 1]
    put(first, count + 3, high[1])

    def start(q):
        s[q + 1] = s_own[q]
        first[q + 2] = w[q] * s_own[q]

    loop(count, start)


def first_coarse_level(s_own, low, high, faces, out, s_next, top, bottom, s, first, total, second):
    strip = out.shape[1]
    open_level(s_own, faces, low, high, s, first)
    rest = sweep_and_rest(s, first, total, second, faces, s_own.shape[0])

    def pair(q):
        value = rest(2 * q) + rest(2 * q + 1)
        s_next[q] = value[HALO:HALO + strip]
        top[q] = value[HALO:2 * HALO]
        bottom[q] = value[strip:HALO + strip]
        out[2 * q] = second[2 * q + 1, HALO:HALO + strip]
        out[2 * q + 1] = second[2 * q + 2, HALO:HALO + strip]

    loop(4, pair)


def fetch(*refs):
    faces2, halo2, faces3, halo3, faces4, out2, out3, out4, semaphores = refs
    copies = Copies(semaphores)
    copies.start(faces2, out2.at[0:17])
    copies.start(halo2, out2.at[17:25])
    copies.start(faces3, out3.at[0:9])
    copies.start(halo3, out3.at[9:17])
    copies.start(faces4, out4)
    for copy in copies.started:
        copy.wait()


def middle_level(s_own, low, high, faces, faces_next, out, s_next, *rest_refs):
    edges, (s, first, total, second) = rest_refs[:-4], rest_refs[-4:]
    count = s_own.shape[0]
    strip = out.shape[1]
    inner = slice(HALO - THIN, HALO + strip + THIN)
    w_next = parts(faces_next, count // 2)[3]
    open_level(s_own, faces, low, high, s, first)
    rest = sweep_and_rest(s, first, total, second, faces, count)
    for q in range(count // 2):
        s_next[q] = rest(2 * q) + rest(2 * q + 1)
    for q in range(count):
        out[q] = second[q + 1, HALO:HALO + strip]
    if count == 4:
        edge_down, edge_up = edges
        edge_down[0] = s_next[0, inner]
        edge_down[1] = w_next[1, inner] * s_next[1, inner]
        edge_up[0] = w_next[0, inner] * s_next[0, inner]
        edge_up[1] = s_next[1, inner]
    else:
        first_next, edge = edges
        first_next[0] = w_next[0] * s_next[0]
        edge[0] = first_next[0, inner]


def widen(source2, above, below, faces2, fine, plane_out, s, edge_down, edge_up, back, semaphores):
    copies = Copies(semaphores)
    copies.start(fine, back.at[:, 0:2])
    copies.start(plane_out, back.at[:, 2])
    count, strip, _ = source2.shape
    w2 = faces2.at[3 * count + 1:4 * count + 1]
    for q in range(count):
        s[q, :HALO] = above[q]
        s[q, HALO:HALO + strip] = source2[q]
        s[q, HALO + strip:] = below[q]
    edge_down[0] = s[0]
    edge_down[1] = w2[1] * s[1]
    edge_up[0] = w2[count - 2] * s[count - 2]
    edge_up[1] = s[count - 1]

    for copy in copies.started:
        copy.wait()


def sweep_last(s, first, low, high, faces, total, second, edge, frames):
    east, north, z, w, _ = parts(faces, 1)
    put(frames, 0, low[0])
    put(frames, 1, high[0])
    t = 1.2 * s[0] + neighbours(first[0], frames[0], frames[1], east[0], north[0], z[0], z[1])
    total[0] = t
    second[0] = w[0] * t
    cut = HALO - THIN
    edge[0] = second[0, cut:cut + edge.shape[1]]


def rest_last(s, total, second, low, high, faces, out, frames):
    east, north, z, _, _ = parts(faces, 1)
    put(frames, 0, low[0])
    put(frames, 1, high[0])
    frames[0] = s[0] - damping * total[0] + neighbours(second[0], frames[0], frames[1], east[0], north[0], z[0], z[1])
    cut = HALO - THIN
    out[0] = frames[0, cut:cut + out.shape[1]]


def finish(place, s, first, low, high, faces5, second2, second3, second4, *rest_refs):
    outs, frames = rest_refs[:-1], rest_refs[-1]
    own = slice(HALO, HALO + outs[0].shape[0])
    put(frames, 0, low[0])
    put(frames, 1, high[0])
    east, north, down, up, w = (faces5[k] for k in range(5))
    second5 = (w * (1.2 * s[0] + neighbours(first[0], frames[0], frames[1], east, north, down, up)))[own]
    for k in range(RING):
        at = (place[0] + k) % RING
        outs[k][...] = ((second2[at // 2] + second3[at // 4]) + second4[0, own]) + second5


def collect(place, *refs):
    out = refs[RING]
    for k, ref in zip((0,) + ORDER, refs):
        out[(place[0] + RING - k) % RING] = ref[...]


def exchange(edge_low, edge_high, distance=RING):
    return shifted(edge_high, distance), shifted(edge_low, -distance)


def on_device(right_side, labels, fraction):
    planes, rows, columns = right_side.shape
    strip = rows // RING
    frame = strip + 2 * HALO
    at_core = lax.axis_index("xy")

    def edges_of(first_rows, last_rows):
        got = lax.ppermute(jnp.where(at_core == 0, last_rows, first_rows), "xy", [(0, 1), (1, 0)])
        return jnp.where(at_core == 1, got, 0.0), jnp.where(at_core == 0, got, 0.0)

    def shape(n):
        return (n, frame, columns)

    at_ring = lax.axis_index("gz")
    place = jnp.stack([at_ring % RING, at_ring // RING % 2]).astype(jnp.int32)
    c_top, c_bottom = edges_of(conductivity(labels[:, :HALO], fraction[:, :HALO]),
                               conductivity(labels[:, rows - HALO:], fraction[:, rows - HALO:]))
    cuts = call(cut_conduct, [(planes, frame, columns)] * RING, [(planes, rows + 2 * HALO, columns)],
                place, labels, fraction, c_top, c_bottom, limit=10)
    s_top, s_bottom = edges_of(right_side[:, :HALO], right_side[:, rows - HALO:])
    thin = strip + 2 * THIN
    (s_cut,) = call(cut_source, [(RING, planes, thin, columns)], [], right_side, s_top, s_bottom, limit=10)
    c_parts = [cuts[0]] + [ring_permuted(cuts[k], k) for k in ORDER]
    c, near_down, near_up, far_down, far_up, ready = call(
        join, [shape(n) for n in (16, NEAR, NEAR, FAR, FAR)] + [(HALO, columns)], [shape(16)], place, *c_parts, limit=10,
        settled=(s_cut,), hbm_out=range(5), copies=5)
    s_own = transposed(after(s_cut, ready))
    c_low, c_high = exchange(near_down, near_up)
    far_low, far_high = exchange(far_down, far_up)
    sizes = [shape(own_planes_of(n)) for n in (16, 8, 4, 2, 1)]
    faces0, faces1, faces2, faces3, faces4, pack, edge = call(
        make_faces, sizes + [shape(3), shape(6)], sizes, place, c, c_low, c_high,
        limit=30, work=10.0, hbm_out=range(5), copies=7)
    halo2, halo3, ready = call(
        make_far_halos, [shape(8), shape(8), (HALO, columns)], [shape(8), shape(8)], edge, c_low, c_high, far_low, far_high,
        limit=10, work=3.0, hbm_out=range(2), copies=2)
    (faces5,) = call(make_last_faces, [shape(5)], [], place, faces4, partner(pack))

    s_own = after(s_own, ready).reshape(RING * planes, thin, columns)
    s_low, s_high = exchange(s_own[:2], s_own[-2:])
    inside = call(
        fine_inside, [shape(n) for n in (16, 16, 16, 16, 8, 75, 8)], [],
        s_own, faces0, faces1, limit=28, work=8.0, hbm_in=(1, 2), copies=14)
    fine, s1, edge_down, edge_up = call(
        fine_ends, [(RING, planes, strip, columns), shape(8), (2, thin, columns), (2, thin, columns)], [shape(4)],
        s_low, s_high, *inside, limit=28)

    low, high = exchange(edge_down, edge_up)
    plane_out, s2, top, bottom = call(
        first_coarse_level,
        [(8, strip, columns), (4, strip, columns), (4, HALO, columns), (4, HALO, columns)],
        [shape(10), shape(12), shape(8), shape(10)], s1, low, high, faces1, limit=15, work=4.0)

    above = row_shifted(bottom, 1)
    below = row_shifted(top, -1)
    s2, edge_down, edge_up, back = call(
        widen, [shape(4), shape(2), shape(2), (RING, planes + 1, strip, columns)], [], s2, above, below, faces2, fine, plane_out, limit=10,
        hbm_out=(3,), copies=2)
    low, high = exchange(edge_down, edge_up)
    faces2, faces3, faces4 = call(
        fetch, [shape(25), shape(17), shape(5)], [], faces2, halo2, faces3, halo3, faces4,
        limit=10, work=4.0, settled=(s2,), hbm_in=range(5), copies=5)
    second2, s3, edge_down, edge_up = call(
        middle_level, [(4, strip, columns), shape(2), (2, thin, columns), (2, thin, columns)],
        [shape(6), shape(8), shape(4), shape(6)], s2, low, high, faces2, faces3, limit=12)
    low, high = exchange(edge_down, edge_up)
    second3, s4, first4, edge = call(
        middle_level, [(2, strip, columns), shape(1), shape(1), (1, thin, columns)],
        [shape(4), shape(6), shape(2), shape(4)], s3, low, high, faces3, faces4, limit=10)
    low, high = exchange(edge, edge)
    total4, second4, edge = call(sweep_last, [shape(1), shape(1), (1, thin, columns)], [shape(2)], s4, first4, low, high, faces4)
    low, high = exchange(edge, edge)
    (rest4,) = call(rest_last, [(1, thin, columns)], [shape(2)], s4, total4, second4, low, high, faces4)
    s5, first5, edge = call(begin_last, [shape(1), shape(1), (1, strip, columns)], [], rest4, partner(rest4), faces5)
    low, high = exchange(edge, edge, 2 * RING)
    back = transposed(back)
    sums = call(finish, [(strip, columns)] * RING, [shape(2)],
                place, s5, first5, low, high, faces5, second2, second3, second4)
    (coarse_return,) = call(collect, [(RING, strip, columns)], [], place, sums[0], *[ring_permuted(sums[k], k) for k in ORDER], settled=(back,))

    fine_iterate = jnp.transpose(back[:, :planes], (1, 0, 2, 3)).reshape(planes, rows, columns)
    plane_iterate = back[:, planes].reshape(1, rows, columns)
    return fine_iterate, plane_iterate, coarse_return.reshape(1, rows, columns)


def solution(mesh):
    spec = P("gz", "xy", None)
    return jax.shard_map(
        on_device,
        mesh=mesh,
        in_specs=(spec, spec, spec),
        out_specs=(spec, spec, spec),
        check_vma=False,
    )
```

```python
from functools import partial

import jax
import jax.numpy as jnp
from jax import lax
from jax.experimental import pallas as pl
from jax.experimental.pallas import tpu as pltpu
from jax.sharding import PartitionSpec as P

RING = 8
HALO = 8
NEAR, FAR = 3, 6
THIN = 4
damping = 0.8
pore_value = 1.0
grain_value = 0.1
clay_value = 0.3
TINY = 1e-6


def ring_groups(count):
    return [[r * RING + k for k in range(RING)] for r in range(count // RING)]


def shifted(value, by):
    size = lax.axis_size("gz")
    pairs = [(i, i + by) for i in range(size) if 0 <= i + by < size]
    return lax.ppermute(value, "gz", pairs)


def row_shifted(value, by):
    pairs = []
    for ring in range(lax.axis_size("gz") // RING):
        for t in range(2 * RING):
            u = t + by
            if 0 <= u < 2 * RING:
                pairs.append(((ring * RING + t % RING) * 2 + t // RING, (ring * RING + u % RING) * 2 + u // RING))
    return lax.ppermute(value, ("gz", "xy"), pairs)


def partner(value):
    size = lax.axis_size("gz")
    return lax.ppermute(value, "gz", [(i, i + RING if (i // RING) % 2 == 0 else i - RING) for i in range(size)])


def transposed(value):
    return lax.all_to_all(value, "gz", 0, 0, axis_index_groups=ring_groups(lax.axis_size("gz")), tiled=True)


def conductivity(labels, fraction):
    return jnp.where(labels == 0, pore_value, jnp.where(labels == 1, grain_value, clay_value)) * fraction


def harmonic(one_side, other_side):
    return (2.0 * one_side * other_side) / jnp.maximum(one_side + other_side, TINY)


def next_row(v):
    return pltpu.roll(v, v.shape[0] - 1, 0)


def previous_row(v):
    return pltpu.roll(v, 1, 0)


def next_column(v):
    return pltpu.roll(v, v.shape[1] - 1, 1)


def previous_column(v):
    return pltpu.roll(v, 1, 1)


def neighbours(v, below, above, east, north, down, up):
    return (
        east * next_row(v)
        + previous_row(east * v)
        + north * next_column(v)
        + previous_column(north * v)
        + down * below
        + up * above
    )


def weight(c, east, north, down, up):
    diagonal = east + previous_row(east) + north + previous_column(north) + down + up
    return jnp.where(c > 0, damping / jnp.where(c > 0, diagonal, 1.0), 0.0)


def loop(count, body):
    def step(k, carry):
        body(k)
        return carry

    lax.fori_loop(0, count, step, 0)


def call(kernel, outs, scratch, *args, limit=8, work=0.0, settled=(), hbm_in=(), hbm_out=(), copies=0):
    shapes = [(pltpu.HBM if i in hbm_out else jax.ShapeDtypeStruct)(s, jnp.float32) for i, s in enumerate(outs)]
    vmem = pl.BlockSpec(memory_space=pltpu.VMEM)
    smem = pl.BlockSpec(memory_space=pltpu.SMEM)
    hbm = pl.BlockSpec(memory_space=pltpu.HBM)
    kinds = [hbm if i in hbm_in else smem if a.dtype == jnp.int32 and a.ndim == 1 else vmem for i, a in enumerate(args)]
    cost = pl.CostEstimate(flops=int(work * 1.0e9), bytes_accessed=int(work * 3.0e6), transcendentals=0) if work else None

    def body(*refs):
        kernel(*refs[len(settled):])

    args = [pltpu.with_memory_space_constraint(a, pltpu.HBM) if i in hbm_in else a for i, a in enumerate(args)]

    return pl.pallas_call(
        body,
        out_shape=shapes,
        in_specs=[pl.BlockSpec(memory_space=pl.ANY)] * len(settled) + kinds,
        out_specs=[hbm if i in hbm_out else vmem for i in range(len(shapes))],
        scratch_shapes=[pltpu.VMEM(s, jnp.float32) if isinstance(s, tuple) else s for s in scratch] + ([pltpu.SemaphoreType.DMA((copies,))] if copies else []),
        compiler_params=pltpu.CompilerParams(vmem_limit_bytes=limit * 1024 * 1024),
        cost_estimate=cost,
    )(*settled, *args)


ORDER = (3, 5, 4, 2, 6, 1, 7)


def ring_permuted(value, by):
    size = lax.axis_size("gz")
    return lax.ppermute(value, "gz", [(i, i // RING * RING + (i + by) % RING) for i in range(size)])


def after(value, *settled):
    def nothing(*refs):
        pass

    there = pl.BlockSpec(memory_space=pl.ANY)
    return pl.pallas_call(
        nothing,
        out_shape=jax.ShapeDtypeStruct(value.shape, value.dtype),
        in_specs=[there] * (1 + len(settled)),
        out_specs=there,
        compiler_params=pltpu.CompilerParams(vmem_limit_bytes=1024 * 1024),
        input_output_aliases={0: 0},
    )(value, *settled)


class Copies:
    def __init__(self, semaphores):
        self.semaphores, self.started = semaphores, []

    def start(self, source, target):
        copy = pltpu.make_async_copy(source, target, self.semaphores.at[len(self.started)])
        copy.start()
        self.started.append(copy)
        return copy


def cut_conduct(place, labels_there, fraction_there, top, bottom, *rest):
    outs, (full, labels, fraction, semaphores) = rest[:RING], rest[RING:]
    planes, rows, _ = labels.shape
    strip = rows // RING
    copies = Copies(semaphores)
    for p in range(planes):
        copies.start(labels_there.at[p], labels.at[p])
        copies.start(fraction_there.at[p], fraction.at[p])
    for p in range(planes):
        full[p, :HALO] = top[p]
        full[p, HALO + rows:] = bottom[p]
        copies.started[2 * p].wait()
        copies.started[2 * p + 1].wait()
        for k in range(RING):
            at = k * strip
            full[p, HALO + at:HALO + at + strip] = conductivity(labels[p, at:at + strip], fraction[p, at:at + strip])
        for k in range(RING):
            start = pl.multiple_of(((place[0] + k) % RING) * strip, strip)
            outs[k][p] = full[p, pl.ds(start, strip + 2 * HALO)]


def cut_source(source, top, bottom, out):
    planes, rows, _ = source.shape
    strip = rows // RING
    for p in range(planes):
        for k in range(RING):
            start = k * strip
            out[k, p, :THIN] = top[p, HALO - THIN:] if k == 0 else source[p, start - THIN:start]
            out[k, p, THIN:THIN + strip] = source[p, start:start + strip]
            out[k, p, THIN + strip:] = bottom[p, :THIN] if k == RING - 1 else source[p, start + strip:start + strip + THIN]


def join(place, *refs):
    c, near_low, near_high, far_low, far_high, ready, out, semaphores = refs[RING:]
    ready[...] = refs[0][0, :HALO]
    for k, ref in zip((0,) + ORDER, refs):
        start = ((place[0] + RING - k) % RING) * 2
        out[start] = ref[0]
        out[start + 1] = ref[1]
    copies = Copies(semaphores)
    for ref, first in ((near_low, 0), (near_high, 16 - NEAR), (far_low, NEAR), (far_high, 16 - NEAR - FAR), (c, 0)):
        copies.start(out.at[first:first + ref.shape[0]], ref)
    for copy in copies.started:
        copy.wait()


def plane_faces(c):
    last = lax.broadcasted_iota(jnp.int32, c.shape, 1) == c.shape[1] - 1
    return harmonic(c, next_row(c)), jnp.where(last, 0.0, harmonic(c, next_column(c)))


def parts(faces, count):
    east, north = faces.at[0:count], faces.at[count:2 * count]
    z, w = faces.at[2 * count:3 * count + 1], faces.at[3 * count + 1:4 * count + 1]
    return east, north, z, w, faces.at[4 * count + 1:] if faces.shape[0] > 4 * count + 1 else None


def planes_of(count):
    return 4 * count + 1 + (0 if count == 1 else 10 if count == 16 else 8)


def own_planes_of(count):
    return planes_of(count) if count > 4 else 4 * count + 1


def make_faces(place, c, low, high, out0, out1, out2, out3, out4, pack, edge, faces0, faces1, faces2, faces3, faces4, semaphores):
    east0, north0, z0, w0, halo0 = parts(faces0, 16)

    def z_face(p):
        z0[p] = harmonic(c[p - 1], c[p])

    loop(15, lambda k: z_face(k + 1))
    z0[0] = jnp.where(low[NEAR - 1] > 0, harmonic(low[NEAR - 1], c[0]), 2.0 * c[0])
    z0[16] = jnp.where(high[0] > 0, harmonic(c[15], high[0]), 2.0 * c[15])

    def weigh(p):
        east, north = plane_faces(c[p])
        east0[p] = east
        north0[p] = north
        w0[p] = weight(c[p], east, north, z0[p], z0[p + 1])

    copies = Copies(semaphores)
    loop(16, weigh)
    copies.start(faces0.at[0:65], out0.at[0:65])
    finer, count = faces0, 16
    for coarser in (faces1, faces2, faces3, faces4):
        east_f, north_f, z_f, _, _ = parts(finer, count)
        count //= 2
        east, north, z, w, _ = parts(coarser, count)

        def faces_and_weight(q):
            east_q = east_f[2 * q] + east_f[2 * q + 1]
            north_q = north_f[2 * q] + north_f[2 * q + 1]
            east[q] = east_q
            north[q] = north_q
            z[q] = z_f[2 * q]
            w[q] = weight(c[0], east_q, north_q, z_f[2 * q], z_f[2 * q + 2])

        loop(count, faces_and_weight)
        z[count] = z_f[2 * count]
        finer = coarser
    copies.start(faces1.at[0:33], out1.at[0:33])
    copies.start(faces2.at[0:17], out2.at[0:17])
    copies.start(faces3.at[0:9], out3.at[0:9])
    copies.start(faces4, out4)

    for side, ref, at, face in ((0, low, (2, 1, 0), 0), (1, high, (0, 1, 2), 16)):
        shared = z0[face]
        near, after_near, third = (ref[k] for k in at)
        middle = harmonic(near, after_near)
        outer = harmonic(after_near, third)
        east_near, north_near = plane_faces(near)
        east_next, north_next = plane_faces(after_near)
        east_sum, north_sum = east_near + east_next, north_near + north_next
        halo0[side] = east_near
        halo0[2 + side] = north_near
        halo0[4 + side] = middle
        halo0[6 + side] = weight(near, east_near, north_near, shared, middle)
        halo0[8 + side] = weight(after_near, east_next, north_next, middle, outer)
        halo1 = parts(faces1, 8)[4]
        halo1[side] = east_sum
        halo1[2 + side] = north_sum
        halo1[4 + side] = outer
        halo1[6 + side] = weight(near, east_sum, north_sum, shared, outer)
        edge[side] = east_sum
        edge[2 + side] = north_sum
        edge[4 + side] = shared
    copies.start(faces0.at[65:75], out0.at[65:75])
    copies.start(faces1.at[33:41], out1.at[33:41])
    pack[0] = faces4[0]
    pack[1] = faces4[1]
    pack[2] = jnp.where(place[1] == 0, faces4[2], faces4[3])
    for copy in copies.started:
        copy.wait()


def make_far_halos(edge, low, high, far_low, far_high, out2, out3, ready, halo2, halo3, semaphores):
    for side in range(2):
        def at(k):
            if side == 0:
                return low[NEAR - 1 - k] if k < NEAR else far_low[NEAR + FAR - 1 - k]
            return high[k] if k < NEAR else far_high[k - NEAR]

        near, east_sum, north_sum, shared = at(0), edge[side], edge[2 + side], edge[4 + side]
        for halo, thick in ((halo2, 4), (halo3, 8)):
            for k in range(thick // 2, thick):
                east, north = plane_faces(at(k))
                east_sum = east_sum + east
                north_sum = north_sum + north
            outer = harmonic(at(thick - 1), at(thick))
            halo[side] = east_sum
            halo[2 + side] = north_sum
            halo[4 + side] = outer
            halo[6 + side] = weight(near, east_sum, north_sum, shared, outer)
    copies = Copies(semaphores)
    copies.start(halo2, out2)
    copies.start(halo3, out3)
    ready[...] = edge[0, :HALO]
    for copy in copies.started:
        copy.wait()


def make_last_faces(place, faces4, other, faces5):
    east4, north4, z4, w4, _ = parts(faces4, 1)
    lower = place[1] == 0
    east = east4[0] + other[0]
    north = north4[0] + other[1]
    down = jnp.where(lower, z4[0], other[2])
    up = jnp.where(lower, other[2], z4[1])
    for k, value in enumerate((east, north, down, up, weight(w4[0], east, north, down, up))):
        faces5[k] = value


def begin_last(rest4, other, faces5, s, first, edge):
    put(s, 0, rest4[0] + other[0])
    first[0] = faces5[4] * s[0]
    edge[0] = first[0, HALO:HALO + edge.shape[1]]
def sweep_and_rest(s, first, total, second, faces, count):
    east, north, z, w, halo = parts(faces, count)

    def sweep(q):
        t = 1.2 * s[q + 1] + neighbours(first[q + 2], first[q + 1], first[q + 3], east[q], north[q], z[q], z[q + 1])
        total[q] = t
        second[q + 1] = w[q] * t

    loop(count, sweep)
    for side, q, down, up in ((0, -1, halo[4], z[0]), (1, count, z[count], halo[5])):
        second[q + 1] = halo[6 + side] * (1.2 * s[q + 1] + neighbours(
            first[q + 2], first[q + 1], first[q + 3], halo[side], halo[2 + side], down, up))

    def rest(q):
        return s[q + 1] - damping * total[q] + neighbours(
            second[q + 1], second[q], second[q + 2], east[q], north[q], z[q], z[q + 1])

    return rest


def put(ref, k, value):
    rows = value.shape[0]
    cut = (ref.shape[1] - rows) // 2
    if cut:
        blank = jnp.zeros((cut, value.shape[1]), jnp.float32)
        ref[k, :cut] = blank
        ref[k, cut + rows:] = blank
    ref[k, cut:cut + rows] = value


def fine_inside(s_own, there, there_next, s, first, total, second, s_next, faces, w_next, semaphores):
    east, north, z, w, _ = parts(faces, 16)
    copies = Copies(semaphores)
    weights = copies.start(there.at[49:75], faces.at[49:75])
    groups = []
    for k in range(4):
        spans = ((4 * k, 4), (16 + 4 * k, 4), (32, 5) if k == 0 else (33 + 4 * k, 4))
        groups.append([copies.start(there.at[a:a + n], faces.at[a:a + n]) for a, n in spans])
    later = copies.start(there_next.at[25:33], w_next)
    loop(16, lambda q: put(s, q, s_own[q]))
    weights.wait()

    def start(q):
        first[q] = w[q] * s[q]

    loop(16, start)

    def sweep(q):
        t = 1.2 * s[q] + neighbours(first[q], first[q - 1], first[q + 1], east[q], north[q], z[q], z[q + 1])
        total[q] = t
        second[q] = w[q] * t

    for k, group in enumerate(groups):
        for copy in group:
            copy.wait()
        low, high = max(4 * k, 1), min(4 * k + 4, 15)
        loop(high - low, lambda q: sweep(q + low))

    def rest(q):
        return s[q] - damping * total[q] + neighbours(second[q], second[q - 1], second[q + 1], east[q], north[q], z[q], z[q + 1])

    def pair(q):
        s_next[q + 1] = rest(2 * q + 2) + rest(2 * q + 3)

    loop(6, pair)
    later.wait()


def fine_ends(s_low, s_high, s, first, total, second, s_inside, faces, w_next, fine, s_next, edge_down, edge_up, frames):
    east, north, z, w, halo = parts(faces, 16)
    strip = fine.shape[2]
    own = slice(HALO, HALO + strip)
    inner = slice(HALO - THIN, HALO + strip + THIN)
    for k, value in enumerate((s_low[0], s_low[1], s_high[0], s_high[1])):
        put(frames, k, value)

    def copy(q):
        s_next[q + 1] = s_inside[q + 1]

    loop(6, copy)

    def keep(q):
        fine[q, 1] = second[2 * q + 1, own]
        fine[q + 1, 0] = second[2 * q + 2, own]

    loop(7, keep)

    def residual(q, t, v, below, above):
        return s[q] - damping * t + neighbours(v, below, above, east[q], north[q], z[q], z[q + 1])

    near = halo[6] * frames[1]
    t = 1.2 * frames[1] + neighbours(near, halo[8] * frames[0], first[0], halo[0], halo[2], halo[4], z[0])
    outside = halo[6] * t
    t = 1.2 * s[0] + neighbours(first[0], near, first[1], east[0], north[0], z[0], z[1])
    inside = w[0] * t
    fine[0, 0] = inside[own]
    s_next[0] = residual(0, t, inside, outside, second[1]) + residual(1, total[1], second[1], inside, second[2])
    near = halo[7] * frames[2]
    t = 1.2 * frames[2] + neighbours(near, first[15], halo[9] * frames[3], halo[1], halo[3], z[16], halo[5])
    outside = halo[7] * t
    t = 1.2 * s[15] + neighbours(first[15], first[14], near, east[15], north[15], z[15], z[16])
    inside = w[15] * t
    fine[7, 1] = inside[own]
    s_next[7] = residual(14, total[14], second[14], second[13], inside) + residual(15, t, inside, second[14], outside)

    edge_down[0] = s_next[0, inner]
    edge_down[1] = w_next[1, inner] * s_next[1, inner]
    edge_up[0] = w_next[6, inner] * s_next[6, inner]
    edge_up[1] = s_next[7, inner]


def open_level(s_own, faces, low, high, s, first):
    count = s_own.shape[0]
    _, _, _, w, halo = parts(faces, count)
    put(s, 0, low[1])
    put(s, count + 1, high[0])
    put(first, 0, low[0])
    first[1] = halo[6] * s[0]
    first[count + 2] = halo[7] * s[count + 1]
    put(first, count + 3, high[1])

    def start(q):
        s[q + 1] = s_own[q]
        first[q + 2] = w[q] * s_own[q]

    loop(count, start)


def first_coarse_level(s_own, low, high, faces, out, s_next, top, bottom, s, first, total, second):
    strip = out.shape[1]
    open_level(s_own, faces, low, high, s, first)
    rest = sweep_and_rest(s, first, total, second, faces, s_own.shape[0])

    def pair(q):
        value = rest(2 * q) + rest(2 * q + 1)
        s_next[q] = value[HALO:HALO + strip]
        top[q] = value[HALO:2 * HALO]
        bottom[q] = value[strip:HALO + strip]
        out[2 * q] = second[2 * q + 1, HALO:HALO + strip]
        out[2 * q + 1] = second[2 * q + 2, HALO:HALO + strip]

    loop(4, pair)


def fetch(*refs):
    faces2, halo2, faces3, halo3, faces4, out2, out3, out4, semaphores = refs
    copies = Copies(semaphores)
    copies.start(faces2, out2.at[0:17])
    copies.start(halo2, out2.at[17:25])
    copies.start(faces3, out3.at[0:9])
    copies.start(halo3, out3.at[9:17])
    copies.start(faces4, out4)
    for copy in copies.started:
        copy.wait()


def middle_level(s_own, low, high, faces, faces_next, out, s_next, *rest_refs):
    edges, (s, first, total, second) = rest_refs[:-4], rest_refs[-4:]
    count = s_own.shape[0]
    strip = out.shape[1]
    inner = slice(HALO - THIN, HALO + strip + THIN)
    w_next = parts(faces_next, count // 2)[3]
    open_level(s_own, faces, low, high, s, first)
    rest = sweep_and_rest(s, first, total, second, faces, count)
    for q in range(count // 2):
        s_next[q] = rest(2 * q) + rest(2 * q + 1)
    for q in range(count):
        out[q] = second[q + 1, HALO:HALO + strip]
    if count == 4:
        edge_down, edge_up = edges
        edge_down[0] = s_next[0, inner]
        edge_down[1] = w_next[1, inner] * s_next[1, inner]
        edge_up[0] = w_next[0, inner] * s_next[0, inner]
        edge_up[1] = s_next[1, inner]
    else:
        first_next, edge = edges
        first_next[0] = w_next[0] * s_next[0]
        edge[0] = first_next[0, inner]


def widen(source2, above, below, faces2, fine, plane_out, s, edge_down, edge_up, back, semaphores):
    copies = Copies(semaphores)
    copies.start(fine, back.at[:, 0:2])
    copies.start(plane_out, back.at[:, 2])
    count, strip, _ = source2.shape
    w2 = faces2.at[3 * count + 1:4 * count + 1]
    for q in range(count):
        s[q, :HALO] = above[q]
        s[q, HALO:HALO + strip] = source2[q]
        s[q, HALO + strip:] = below[q]
    edge_down[0] = s[0]
    edge_down[1] = w2[1] * s[1]
    edge_up[0] = w2[count - 2] * s[count - 2]
    edge_up[1] = s[count - 1]

    for copy in copies.started:
        copy.wait()


def sweep_last(s, first, low, high, faces, total, second, edge, frames):
    east, north, z, w, _ = parts(faces, 1)
    put(frames, 0, low[0])
    put(frames, 1, high[0])
    t = 1.2 * s[0] + neighbours(first[0], frames[0], frames[1], east[0], north[0], z[0], z[1])
    total[0] = t
    second[0] = w[0] * t
    cut = HALO - THIN
    edge[0] = second[0, cut:cut + edge.shape[1]]


def rest_last(s, total, second, low, high, faces, out, frames):
    east, north, z, _, _ = parts(faces, 1)
    put(frames, 0, low[0])
    put(frames, 1, high[0])
    frames[0] = s[0] - damping * total[0] + neighbours(second[0], frames[0], frames[1], east[0], north[0], z[0], z[1])
    cut = HALO - THIN
    out[0] = frames[0, cut:cut + out.shape[1]]


def finish(place, s, first, low, high, faces5, second2, second3, second4, *rest_refs):
    outs, frames = rest_refs[:-1], rest_refs[-1]
    own = slice(HALO, HALO + outs[0].shape[0])
    put(frames, 0, low[0])
    put(frames, 1, high[0])
    east, north, down, up, w = (faces5[k] for k in range(5))
    second5 = (w * (1.2 * s[0] + neighbours(first[0], frames[0], frames[1], east, north, down, up)))[own]
    for k in range(RING):
        at = (place[0] + k) % RING
        outs[k][...] = ((second2[at // 2] + second3[at // 4]) + second4[0, own]) + second5


def collect(place, *refs):
    out = refs[RING]
    for k, ref in zip((0,) + ORDER, refs):
        out[(place[0] + RING - k) % RING] = ref[...]


def exchange(edge_low, edge_high, distance=RING):
    return shifted(edge_high, distance), shifted(edge_low, -distance)


def on_device(right_side, labels, fraction):
    planes, rows, columns = right_side.shape
    strip = rows // RING
    frame = strip + 2 * HALO
    at_core = lax.axis_index("xy")

    def edges_of(first_rows, last_rows):
        got = lax.ppermute(jnp.where(at_core == 0, last_rows, first_rows), "xy", [(0, 1), (1, 0)])
        return jnp.where(at_core == 1, got, 0.0), jnp.where(at_core == 0, got, 0.0)

    def shape(n):
        return (n, frame, columns)

    at_ring = lax.axis_index("gz")
    place = jnp.stack([at_ring % RING, at_ring // RING % 2]).astype(jnp.int32)
    c_top, c_bottom = edges_of(conductivity(labels[:, :HALO], fraction[:, :HALO]),
                               conductivity(labels[:, rows - HALO:], fraction[:, rows - HALO:]))
    cuts = call(cut_conduct, [(planes, frame, columns)] * RING,
                [(planes, rows + 2 * HALO, columns), pltpu.VMEM((planes, rows, columns), jnp.int32), (planes, rows, columns)],
                place, labels, fraction, c_top, c_bottom, limit=14, hbm_in=(1, 2), copies=4)
    s_top, s_bottom = edges_of(right_side[:, :HALO], right_side[:, rows - HALO:])
    thin = strip + 2 * THIN
    (s_cut,) = call(cut_source, [(RING, planes, thin, columns)], [], right_side, s_top, s_bottom, limit=10)
    c_parts = [cuts[0]] + [ring_permuted(cuts[k], k) for k in ORDER]
    c, near_down, near_up, far_down, far_up, ready = call(
        join, [shape(n) for n in (16, NEAR, NEAR, FAR, FAR)] + [(HALO, columns)], [shape(16)], place, *c_parts, limit=10,
        settled=(s_cut,), hbm_out=range(5), copies=5)
    s_own = transposed(after(s_cut, ready))
    c_low, c_high = exchange(near_down, near_up)
    far_low, far_high = exchange(far_down, far_up)
    sizes = [shape(own_planes_of(n)) for n in (16, 8, 4, 2, 1)]
    faces0, faces1, faces2, faces3, faces4, pack, edge = call(
        make_faces, sizes + [shape(3), shape(6)], sizes, place, c, c_low, c_high,
        limit=30, work=10.0, hbm_out=range(5), copies=7)
    halo2, halo3, ready = call(
        make_far_halos, [shape(8), shape(8), (HALO, columns)], [shape(8), shape(8)], edge, c_low, c_high, far_low, far_high,
        limit=10, work=3.0, hbm_out=range(2), copies=2)
    (faces5,) = call(make_last_faces, [shape(5)], [], place, faces4, partner(pack))

    s_own = after(s_own, ready).reshape(RING * planes, thin, columns)
    s_low, s_high = exchange(s_own[:2], s_own[-2:])
    inside = call(
        fine_inside, [shape(n) for n in (16, 16, 16, 16, 8, 75, 8)], [],
        s_own, faces0, faces1, limit=28, work=8.0, hbm_in=(1, 2), copies=14)
    fine, s1, edge_down, edge_up = call(
        fine_ends, [(RING, planes, strip, columns), shape(8), (2, thin, columns), (2, thin, columns)], [shape(4)],
        s_low, s_high, *inside, limit=28)

    low, high = exchange(edge_down, edge_up)
    plane_out, s2, top, bottom = call(
        first_coarse_level,
        [(8, strip, columns), (4, strip, columns), (4, HALO, columns), (4, HALO, columns)],
        [shape(10), shape(12), shape(8), shape(10)], s1, low, high, faces1, limit=15, work=4.0)

    above = row_shifted(bottom, 1)
    below = row_shifted(top, -1)
    s2, edge_down, edge_up, back = call(
        widen, [shape(4), shape(2), shape(2), (RING, planes + 1, strip, columns)], [], s2, above, below, faces2, fine, plane_out, limit=10,
        hbm_out=(3,), copies=2)
    low, high = exchange(edge_down, edge_up)
    faces2, faces3, faces4 = call(
        fetch, [shape(25), shape(17), shape(5)], [], faces2, halo2, faces3, halo3, faces4,
        limit=10, work=4.0, settled=(s2,), hbm_in=range(5), copies=5)
    second2, s3, edge_down, edge_up = call(
        middle_level, [(4, strip, columns), shape(2), (2, thin, columns), (2, thin, columns)],
        [shape(6), shape(8), shape(4), shape(6)], s2, low, high, faces2, faces3, limit=12)
    low, high = exchange(edge_down, edge_up)
    second3, s4, first4, edge = call(
        middle_level, [(2, strip, columns), shape(1), shape(1), (1, thin, columns)],
        [shape(4), shape(6), shape(2), shape(4)], s3, low, high, faces3, faces4, limit=10)
    low, high = exchange(edge, edge)
    total4, second4, edge = call(sweep_last, [shape(1), shape(1), (1, thin, columns)], [shape(2)], s4, first4, low, high, faces4)
    low, high = exchange(edge, edge)
    (rest4,) = call(rest_last, [(1, thin, columns)], [shape(2)], s4, total4, second4, low, high, faces4)
    s5, first5, edge = call(begin_last, [shape(1), shape(1), (1, strip, columns)], [], rest4, partner(rest4), faces5)
    low, high = exchange(edge, edge, 2 * RING)
    back = transposed(back)
    sums = call(finish, [(strip, columns)] * RING, [shape(2)],
                place, s5, first5, low, high, faces5, second2, second3, second4)
    (coarse_return,) = call(collect, [(RING, strip, columns)], [], place, sums[0], *[ring_permuted(sums[k], k) for k in ORDER], settled=(back,))

    fine_iterate = jnp.transpose(back[:, :planes], (1, 0, 2, 3)).reshape(planes, rows, columns)
    plane_iterate = back[:, planes].reshape(1, rows, columns)
    return fine_iterate, plane_iterate, coarse_return.reshape(1, rows, columns)


def solution(mesh):
    spec = P("gz", "xy", None)
    return jax.shard_map(
        on_device,
        mesh=mesh,
        in_specs=(spec, spec, spec),
        out_specs=(spec, spec, spec),
        check_vma=False,
    )
```
